32 devices in a mesh: section: 1, expert: 32 (over z, y, x, core).
Axes of the slice: x: 2, y: 2, z: 4, core: 2. Of those that a mesh axis runs over, the one named last changes fastest.
Arguments:
- states_orig: bfloat16 [1, 256, 2048], P(None, 'expert'), may hold values from -400 to 400
- states_pruned: bfloat16 [1, 256, 2048], P(None, 'expert'), may hold values from -400 to 400
- ids_orig: int32 [1, 1, 256, 8], P('section', None, 'expert'), may hold values from 0 to 15, all different within a row; in each aligned block of 8 rows (0 to 7, 8 to 15, ..., all dimensions but the last counted through in order) at most 8 rows name the same one
- ids_pruned: int32 [1, 1, 256, 8], P('section', None, 'expert'), may hold values from 0 to 15, all different within a row; in each aligned block of 8 rows (0 to 7, 8 to 15, ..., all dimensions but the last counted through in order) at most 8 rows name the same one
- gates_orig: float32 [1, 1, 256, 8], P('section', None, 'expert'), may hold values from 0.02 to 2.7
- gates_pruned: float32 [1, 1, 256, 8], P('section', None, 'expert'), may hold values from 0.02 to 2.7
- keep_mask: int32 [1, 16], P('section'), may hold values 0 or 1
- w_in: bfloat16 [1, 32, 2048, 768], P('section', 'expert'), may hold values from -0.125 to 0.125
- w_out: bfloat16 [1, 32, 384, 2048], P('section', 'expert'), may hold values from -0.21875 to 0.21875
Outputs:
- moe_orig: bfloat16 [1, 1, 256, 2048], P('section', None, 'expert')
- moe_pruned: bfloat16 [1, 1, 256, 2048], P('section', None, 'expert')
- expert_loss: float32 [1, 16], P('section')
The draws below stay inside these ranges and needn't reach their ends.
Inputs may be any that keep to these rules, and one draw needn't show every extreme that they name: `ids_orig`: for each layer, micro-batch and device along expert, no expert is picked by more than 8 of that device's 8 tokens, and some expert is picked by exactly 8. The 8 picks of a token are different experts. `ids_pruned`: for each layer, micro-batch and device along expert, no expert is picked by more than 8 of that device's 8 tokens, and some expert is picked by exactly 8. The 8 picks of a token are different experts. `keep_mask`: 1 keeps an expert in the pruned model, 0 removes it.
All inputs are finite; a program needn't handle non-finite values. No bound on the sum of `keep_mask` on one device may be relied on, other than what follows from the above.
Results may differ from the reference program's by a relative error of at most 0.012.
Values may be sent and summed in bfloat16 or wider, within the bound.
No kernel may reach another device: no remote copies, remote signals or barrier semaphores. Data moves between devices by JAX's collectives and lax.ppermute only.
A program may use at most 64 MiB of HBM per device.

```python
import math
import jax
import jax.numpy as jnp
import numpy as np
from jax import lax

D = 2048
FF = 768
SPLIT = 2
MICRO = 1
TOK_DEV = 8
LAYERS = 1
EXPERTS = 16
SLICES = 32
HID = 384
TOPK = 8
EXP_CAP = 8
TOKENS = 256
N_EXPERT = 32


def token_ramp(top_value):
    placement = jnp.arange(TOKENS, dtype=jnp.float32) / (TOKENS - 1)
    return jnp.power(top_value, placement)


def gate_values(key_base):
    shape_all = (LAYERS, MICRO, TOKENS, TOPK)
    base_values = jnp.exp(jax.random.uniform(key_base, shape_all, jnp.float32, math.log(0.03), math.log(0.3)))
    ramp_values = token_ramp(3.0)
    return (base_values * ramp_values[None, None, :, None]).astype(jnp.float32)


def state_values(key_base):
    shape_all = (MICRO, TOKENS, D)
    key_rows = jax.random.fold_in(key_base, 1)
    key_cols = jax.random.fold_in(key_base, 2)
    key_body = jax.random.fold_in(key_base, 3)
    row_scale = jnp.exp(jax.random.uniform(key_rows, (MICRO, TOKENS, 1), jnp.float32, 0.0, math.log(10.0)))
    col_scale = jnp.exp(jax.random.uniform(key_cols, (1, 1, D), jnp.float32, 0.0, math.log(10.0)))
    base_values = jnp.clip(jax.random.normal(key_body, shape_all, jnp.float32), -4.0, 4.0)
    return (base_values * row_scale * col_scale).astype(jnp.bfloat16)


def draw_states_orig(key, part):
    return state_values(jax.random.fold_in(key, 101))


def draw_states_pruned(key, part):
    return state_values(jax.random.fold_in(key, 202))


def draw_gates_orig(key, part):
    return gate_values(jax.random.fold_in(key, 303))


def draw_gates_pruned(key, part):
    return gate_values(jax.random.fold_in(key, 404))


def set_ends(result, stream_key, smallest, high):
    dims = result.shape
    place = [jax.random.randint(jax.random.fold_in(stream_key, axis), (), 0, dims[axis]) for axis in range(len(dims))]
    result = result.at[tuple(place)].set(smallest)
    longest = dims.index(max(dims))
    place[longest] = (place[longest] + 1) % dims[longest]
    return result.at[tuple(place)].set(high)


def level_of(stream_key, extent, shards, least, high):
    def one(axis_at, shards_of):
        heights = jax.random.uniform(jax.random.fold_in(jax.random.fold_in(stream_key, 6), axis_at), (shards_of,), jnp.float32, least / len(shards), high / len(shards))
        return jnp.repeat(jnp.exp(heights), extent[axis_at] // shards_of).reshape((-1,) + (1,) * (len(extent) - axis_at - 1))

    loudness = one(*shards[0])
    for cut in shards[1:]:
        loudness = loudness * one(*cut)
    return loudness


def shared_out(key, own, number, rows, count, top, bound, skew):
    sequence = jax.random.permutation(key, count)
    crowded, usual = load_shares(count, rows * top, bound, skew, True), load_shares(count, rows * top, bound, skew, False)
    places = jnp.arange(count)

    def named(sizes, turn):
        used = int((sizes > 0).sum())
        fixed = max(1, used // 4)
        shifted = fixed + (places - fixed + turn * (used - fixed)) % max(1, count - fixed)
        return jnp.zeros((count,), jnp.int32).at[sequence[jnp.where(places < fixed, places, shifted)]].set(jnp.asarray(sizes, jnp.int32))

    sizes = jnp.where(number % 4 == 0, named(crowded, number // 4), named(usual, number - number // 4 - 1))
    mixed = jax.random.permutation(jax.random.fold_in(own, 3), count)
    giver, sink = mixed[0:count // 2 * 2:2], mixed[1:count // 2 * 2:2]
    slack = jnp.minimum(sizes[giver] - 1, bound - sizes[sink]) // 2
    slack = jnp.where((giver == sequence[0]) | (sink == sequence[0]) | (sizes[sink] == 0), 0, jnp.maximum(slack, 0))
    shifted = jax.random.randint(jax.random.fold_in(own, 4), (count // 2,), 0, 1 << 20) % (slack + 1)
    sizes = sizes.at[giver].add(-shifted).at[sink].add(shifted)
    items = jnp.searchsorted(jnp.cumsum(sizes), jnp.arange(rows * top), side="right").astype(jnp.int32)
    grid = items.reshape(top, rows).T
    grid = grid[jax.random.permutation(jax.random.fold_in(own, 1), rows)]
    turn = jax.random.randint(jax.random.fold_in(own, 2), (rows, 1), 0, top)
    return jnp.take_along_axis(grid, (jnp.arange(top)[None, :] + turn) % top, axis=1)


def load_shares(count, total, most, skew, full):
    portions = [(1 << 20) // math.isqrt(rank ** skew) + 1 for rank in range(1, count + 1)]
    largest = most if full else min(most, max(-(-total // count), total * portions[0] // sum(portions)))
    least = 1 if total - largest >= count - 1 else 0
    counts, surplus = [largest] + [least] * (count - 1), total - largest - least * (count - 1)
    while surplus > 0:
        candidates = [i for i in range(1, count) if counts[i] < largest] or [i for i in range(1, count) if counts[i] < most]
        mass, remaining = sum([portions[i] for i in candidates]), surplus
        for i in candidates:
            addition = min(most - counts[i], max(1, remaining * portions[i] // mass), surplus)
            counts[i] = counts[i] + addition
            surplus = surplus - addition
    return np.array(counts)


def centred(own_key, extent, scale, bound, split=(), held_as=jnp.bfloat16):
    drawn = scale * jax.random.normal(own_key, extent, jnp.float32)
    if split:
        drawn = drawn * level_of(own_key, extent, split, -0.22, 0.18)
    return jnp.clip(drawn, -bound, bound).astype(held_as)


def setup_inputs(seed: int = 0) -> dict:
    streams_of = jax.random.split(jax.random.key(seed), 10)
    states_orig = draw_states_orig(jax.random.fold_in(streams_of[9], 71), 0)
    states_pruned = draw_states_pruned(jax.random.fold_in(streams_of[9], 71), 0)
    ids_orig_keys = jax.random.split(jax.random.fold_in(streams_of[2], 1), LAYERS * MICRO * TOKENS // TOK_DEV)
    ids_orig_turns = jax.random.permutation(jax.random.fold_in(streams_of[2], 3), LAYERS * MICRO * TOKENS // TOK_DEV)
    ids_orig = jax.vmap(lambda own, number: shared_out(jax.random.fold_in(streams_of[2], 2), own, number, TOK_DEV, EXPERTS, TOPK, EXP_CAP, 2))(ids_orig_keys, ids_orig_turns).reshape((LAYERS, MICRO, TOKENS, TOPK))
    ids_pruned_keys = jax.random.split(jax.random.fold_in(streams_of[3], 1), LAYERS * MICRO * TOKENS // TOK_DEV)
    ids_pruned_turns = jax.random.permutation(jax.random.fold_in(streams_of[3], 3), LAYERS * MICRO * TOKENS // TOK_DEV)
    ids_pruned = jax.vmap(lambda own, number: shared_out(jax.random.fold_in(streams_of[3], 2), own, number, TOK_DEV, EXPERTS, TOPK, EXP_CAP, 2))(ids_pruned_keys, ids_pruned_turns).reshape((LAYERS, MICRO, TOKENS, TOPK))
    gates_orig = draw_gates_orig(jax.random.fold_in(streams_of[9], 71), 0)
    gates_pruned = draw_gates_pruned(jax.random.fold_in(streams_of[9], 71), 0)
    keep_mask = set_ends((jax.random.randint(streams_of[6], (LAYERS, EXPERTS), 0, 4) < 3).astype(jnp.int32), jax.random.fold_in(streams_of[6], 1), 0, 1)
    w_in = centred(streams_of[7], (LAYERS, SLICES, D, 2 * HID), D ** -0.5, 0.125, ((1, 32),))
    w_out = centred(streams_of[8], (LAYERS, SLICES, HID, D), FF ** -0.5, 0.21875, ((1, 32),))
    return {"states_orig": states_orig, "states_pruned": states_pruned, "ids_orig": ids_orig, "ids_pruned": ids_pruned, "gates_orig": gates_orig, "gates_pruned": gates_pruned, "keep_mask": keep_mask, "w_in": w_in, "w_out": w_out}


def normalize_rows(state_rows):
    values = state_rows.astype(jnp.float32)
    factor = lax.rsqrt(lax.optimization_barrier(jnp.mean(values * values, axis=-1, keepdims=True)) + 1e-06)
    return (values * factor).astype(jnp.bfloat16)

def expert_matrices(slices_in, slices_out):
    joined = slices_in.reshape(EXPERTS, SPLIT, D, 2, HID)
    gate_full = jnp.transpose(joined[:, :, :, 0, :], (0, 2, 1, 3)).reshape(EXPERTS, D, FF)
    up_full = jnp.transpose(joined[:, :, :, 1, :], (0, 2, 1, 3)).reshape(EXPERTS, D, FF)
    down_full = slices_out.reshape(EXPERTS, FF, D)
    return (gate_full, up_full, down_full)

def slot_positions(picked):
    blocks = picked.reshape(N_EXPERT, TOK_DEV * TOPK)
    labels = jnp.arange(EXPERTS, dtype=jnp.int32)
    choose = (blocks[:, :, None] == labels[None, None, :]).astype(jnp.int32)
    before = jnp.cumsum(choose, axis=1) - choose
    pick_ranks = lax.optimization_barrier(jnp.sum(before * choose, axis=2))
    sources = jnp.arange(N_EXPERT, dtype=jnp.int32)[:, None]
    return (sources * EXP_CAP + pick_ranks).reshape(TOKENS, TOPK).astype(jnp.int32)

def expert_block(normed, picked, weights, gate_full, up_full, down_full):
    positions = slot_positions(picked)
    inputs = jnp.zeros((EXPERTS, N_EXPERT * EXP_CAP, D), jnp.bfloat16)
    spread = jnp.broadcast_to(normed[:, None, :], (TOKENS, TOPK, D)).reshape(TOKENS * TOPK, D)
    inputs = inputs.at[picked.reshape(-1), positions.reshape(-1)].set(spread)

    def one_expert(operands):
        rows_in, gate_one, up_one, down_one = operands
        gate_part = jnp.dot(rows_in, gate_one, preferred_element_type=jnp.float32)
        up_part = jnp.dot(rows_in, up_one, preferred_element_type=jnp.float32)
        hidden = (jax.nn.silu(gate_part) * up_part).astype(jnp.bfloat16)
        return jnp.dot(hidden, down_one, preferred_element_type=jnp.float32).astype(jnp.bfloat16)
    outputs = lax.map(one_expert, (inputs, gate_full, up_full, down_full))
    chosen = outputs[picked, positions].astype(jnp.float32)
    return lax.optimization_barrier(jnp.sum(weights[:, :, None] * chosen, axis=1))

def reference(states_orig, states_pruned, ids_orig, ids_pruned, gates_orig, gates_pruned, keep_mask, w_in, w_out):
    factor = EXPERTS / (TOPK * MICRO * TOKENS)
    labels = jnp.arange(EXPERTS, dtype=jnp.int32)
    current_orig = [states_orig[micro_index] for micro_index in range(MICRO)]
    current_pruned = [states_pruned[micro_index] for micro_index in range(MICRO)]
    orig_layers = []
    pruned_layers = []
    loss_layers = []
    for layer_index in range(LAYERS):
        gate_full, up_full, down_full = expert_matrices(w_in[layer_index], w_out[layer_index])
        kept_scale = keep_mask[layer_index].astype(jnp.float32)
        layer_loss = jnp.zeros((EXPERTS,), jnp.float32)
        orig_micro = []
        pruned_micro = []
        for micro_index in range(MICRO):
            picked_orig = ids_orig[layer_index, micro_index]
            picked_pruned = ids_pruned[layer_index, micro_index]
            weight_orig = gates_orig[layer_index, micro_index]
            weight_pruned = gates_pruned[layer_index, micro_index] * kept_scale[picked_pruned]
            orig_moe = expert_block(normalize_rows(current_orig[micro_index]), picked_orig, weight_orig, gate_full, up_full, down_full)
            pruned_moe = expert_block(normalize_rows(current_pruned[micro_index]), picked_pruned, weight_pruned, gate_full, up_full, down_full)
            differ = orig_moe - pruned_moe
            errors = lax.optimization_barrier(jnp.mean(differ * differ, axis=1))
            choose = (picked_orig[:, :, None] == labels[None, None, :]).astype(jnp.float32)
            weighted = weight_orig * errors[:, None]
            layer_loss = layer_loss + factor * lax.optimization_barrier(jnp.sum(choose * weighted[:, :, None], axis=(0, 1)))
            orig_micro.append(orig_moe.astype(jnp.bfloat16))
            pruned_micro.append(pruned_moe.astype(jnp.bfloat16))
            current_orig[micro_index] = (current_orig[micro_index].astype(jnp.float32) + orig_moe).astype(jnp.bfloat16)
            current_pruned[micro_index] = (current_pruned[micro_index].astype(jnp.float32) + pruned_moe).astype(jnp.bfloat16)
        orig_layers.append(jnp.stack(orig_micro))
        pruned_layers.append(jnp.stack(pruned_micro))
        loss_layers.append(layer_loss)
    return (jnp.stack(orig_layers), jnp.stack(pruned_layers), jnp.stack(loss_layers))
```

```python
import functools

import jax
import jax.numpy as jnp
from jax import lax
from jax.experimental import pallas as pl
from jax.experimental.pallas import tpu as pltpu
from jax.sharding import PartitionSpec as P

SPLIT = 2
LANES = 128


def whole(memory_space=pltpu.VMEM):
    return pl.BlockSpec(memory_space=memory_space)


def normalize_rows(values):
    factor = lax.rsqrt(jnp.mean(values * values, axis=-1, keepdims=True) + 1e-06)
    return values * factor


def dense_weights(picked, gates, experts, width):
    rows = picked.shape[0]
    label = lax.broadcasted_iota(jnp.int32, (rows, width), 1) % experts
    total = jnp.zeros((rows, width), jnp.float32)
    for k in range(picked.shape[1]):
        total = total + jnp.where(picked[:, k : k + 1] == label, gates[:, k : k + 1], 0.0)
    return total


def pack_kernel(experts, so_ref, sp_ref, io_ref, ip_ref, go_ref, gp_ref, keep_ref, out_ref):
    model_width = so_ref.shape[1]
    extra = out_ref.shape[1] - model_width
    states = jnp.concatenate(
        [so_ref[...].astype(jnp.float32), sp_ref[...].astype(jnp.float32)], axis=0
    )
    out_ref[:, :model_width] = normalize_rows(states).astype(jnp.bfloat16)
    dense_orig = dense_weights(io_ref[...], go_ref[...], experts, extra)
    dense_pruned = dense_weights(ip_ref[...], gp_ref[...], experts, extra)
    dense_pruned = dense_pruned * keep_ref[...]
    dense = jnp.concatenate([dense_orig, dense_pruned], axis=0)
    high = dense.astype(jnp.bfloat16).astype(jnp.float32)
    lane = lax.broadcasted_iota(jnp.int32, dense.shape, 1)
    out_ref[:, model_width:] = jnp.where(lane < experts, high, dense - high).astype(jnp.bfloat16)


def expert_kernel(experts, rows_ref, in_a_ref, in_b_ref, out_a_ref, out_b_ref, result_ref, hidden):
    half = out_a_ref.shape[0]
    model_width = out_a_ref.shape[1]
    expert = lax.axis_index("expert") // SPLIT
    extra = rows_ref[:, model_width:].astype(jnp.float32)
    lane = lax.broadcasted_iota(jnp.int32, extra.shape, 1)
    mine = jnp.logical_or(lane == expert, lane == expert + experts)
    weight = jnp.sum(jnp.where(mine, extra, 0.0), axis=1, keepdims=True)
    for place, in_ref in enumerate((in_a_ref, in_b_ref)):
        both = jnp.dot(
            rows_ref[:, :model_width], in_ref[...], preferred_element_type=jnp.float32
        )
        gate, up = both[:, :half], both[:, half:]
        hidden[:, place * half : (place + 1) * half] = (
            gate / (1.0 + jnp.exp(-gate)) * up
        ).astype(jnp.bfloat16)
    step = 512
    for start in range(0, model_width, step):
        value = jnp.dot(
            hidden[:, :half], out_a_ref[:, start : start + step], preferred_element_type=jnp.float32
        ) + jnp.dot(
            hidden[:, half:], out_b_ref[:, start : start + step], preferred_element_type=jnp.float32
        )
        result_ref[:, start : start + step] = (value * weight).astype(jnp.bfloat16)


def on_device(
    states_orig,
    states_pruned,
    ids_orig,
    ids_pruned,
    gates_orig,
    gates_pruned,
    keep_mask,
    w_in,
    w_out,
):
    devices = lax.axis_size("expert")
    section_count = lax.axis_size("section")
    section_index = lax.axis_index("section")
    micro_count, tok_rows, model_width = states_orig.shape
    experts = keep_mask.shape[1]
    top_count = ids_orig.shape[-1]
    loss_factor = experts / (top_count * micro_count * tok_rows * devices)
    extra = -(-2 * experts // LANES) * LANES
    rows = 2 * tok_rows
    own_in, own_out = w_in[0, 0], w_out[0, 0]
    pairs = [(source, source ^ 1) for source in range(devices)]
    other_in = lax.ppermute(own_in, "expert", pairs)
    other_out = lax.ppermute(own_out, "expert", pairs)
    groups = [list(range(core, devices, SPLIT)) for core in range(SPLIT)]
    kept = jnp.tile(keep_mask.astype(jnp.float32), (1, -(-extra // experts)))[:, :extra]

    step_count = micro_count + section_count - 1
    carry = jnp.zeros((2, tok_rows, model_width), jnp.bfloat16)
    moe_orig = jnp.zeros((micro_count, tok_rows, model_width), jnp.bfloat16)
    moe_pruned = moe_orig
    terms = jnp.zeros((experts,), jnp.float32)
    for tick in range(step_count):
        if section_count == 1:
            position, active = tick, True
            item = lambda buffer: buffer[position]
        else:
            position = jnp.clip(tick - section_index, 0, micro_count - 1)
            active = jnp.logical_and(
                tick - section_index >= 0, tick - section_index < micro_count
            )
            item = lambda buffer: lax.dynamic_index_in_dim(buffer, position, 0, keepdims=False)
        fresh = min(tick, micro_count - 1)
        state_orig, state_pruned = states_orig[fresh], states_pruned[fresh]
        if section_count > 1:
            state_orig = jnp.where(section_index == 0, state_orig, carry[0])
            state_pruned = jnp.where(section_index == 0, state_pruned, carry[1])
        picked_orig, weight_orig = item(ids_orig[0]), item(gates_orig[0])
        packed = pl.pallas_call(
            functools.partial(pack_kernel, experts),
            out_shape=jax.ShapeDtypeStruct((rows, model_width + extra), jnp.bfloat16),
            in_specs=[whole()] * 7,
            out_specs=whole(),
        )(
            state_orig,
            state_pruned,
            picked_orig,
            item(ids_pruned[0]),
            weight_orig,
            item(gates_pruned[0]),
            kept,
        )
        gathered = lax.all_gather(
            packed, "expert", axis_index_groups=groups, axis=0, tiled=True
        )
        partial = pl.pallas_call(
            functools.partial(expert_kernel, experts),
            out_shape=jax.ShapeDtypeStruct((gathered.shape[0], model_width), jnp.bfloat16),
            in_specs=[whole()] * 5,
            out_specs=whole(),
            scratch_shapes=[
                pltpu.VMEM((gathered.shape[0], SPLIT * own_out.shape[0]), jnp.bfloat16)
            ],
            compiler_params=pltpu.CompilerParams(vmem_limit_bytes=40 * 2**20),
        )(gathered, own_in, other_in, own_out, other_out)
        moe = lax.psum_scatter(
            partial, "expert", axis_index_groups=groups, scatter_dimension=0, tiled=True
        ).astype(jnp.float32)
        value_orig, value_pruned = moe[:tok_rows], moe[tok_rows:]
        differ = value_orig - value_pruned
        errors = jnp.mean(differ * differ, axis=1)
        chosen = picked_orig[:, :, None] == jnp.arange(experts, dtype=jnp.int32)
        tick_terms = loss_factor * jnp.sum(
            jnp.where(chosen, (weight_orig * errors[:, None])[:, :, None], 0.0), axis=(0, 1)
        )
        round_orig, round_pruned = moe[:tok_rows], moe[tok_rows:]
        round_orig = value_orig.astype(jnp.bfloat16)
        round_pruned = value_pruned.astype(jnp.bfloat16)
        if section_count > 1:
            tick_terms = jnp.where(active, tick_terms, 0.0)
            round_orig = jnp.where(active, round_orig, item(moe_orig))
            round_pruned = jnp.where(active, round_pruned, item(moe_pruned))
        terms = terms + tick_terms
        moe_orig = lax.dynamic_update_index_in_dim(moe_orig, round_orig, position, 0)
        moe_pruned = lax.dynamic_update_index_in_dim(moe_pruned, round_pruned, position, 0)
        if tick + 1 < step_count and section_count > 1:
            following = jnp.stack(
                [
                    (state_orig.astype(jnp.float32) + value_orig).astype(jnp.bfloat16),
                    (state_pruned.astype(jnp.float32) + value_pruned).astype(jnp.bfloat16),
                ]
            )
            onward = [(i, i + 1) for i in range(section_count - 1)]
            carry = lax.ppermute(following, "section", onward)
    spread = jnp.broadcast_to(terms[None], (devices, experts))
    shared = lax.all_to_all(spread, "expert", split_axis=0, concat_axis=0, tiled=True)
    loss = jnp.sum(shared, axis=0)
    return (moe_orig[None], moe_pruned[None], loss[None])


def solution(mesh):
    return jax.shard_map(
        on_device,
        mesh=mesh,
        in_specs=(
            P(None, "expert", None),
            P(None, "expert", None),
            P("section", None, "expert", None),
            P("section", None, "expert", None),
            P("section", None, "expert", None),
            P("section", None, "expert", None),
            P("section", None),
            P("section", "expert", None, None),
            P("section", "expert", None, None),
        ),
        out_specs=(
            P("section", None, "expert", None),
            P("section", None, "expert", None),
            P("section", None),
        ),
        check_vma=False,
    )
```

```python
import functools

import jax
import jax.numpy as jnp
from jax import lax
from jax.experimental import pallas as pl
from jax.experimental.pallas import tpu as pltpu
from jax.sharding import PartitionSpec as P

SPLIT = 2
LANES = 128


def whole(memory_space=pltpu.VMEM):
    return pl.BlockSpec(memory_space=memory_space)


def normalize_rows(values):
    factor = lax.rsqrt(jnp.mean(values * values, axis=-1, keepdims=True) + 1e-06)
    return values * factor


def dense_weights(picked, gates, experts, width):
    rows = picked.shape[0]
    label = lax.broadcasted_iota(jnp.int32, (rows, width), 1) % experts
    total = jnp.zeros((rows, width), jnp.float32)
    for k in range(picked.shape[1]):
        total = total + jnp.where(picked[:, k : k + 1] == label, gates[:, k : k + 1], 0.0)
    return total


def pack_kernel(experts, so_ref, sp_ref, io_ref, ip_ref, go_ref, gp_ref, keep_ref, out_ref):
    model_width = so_ref.shape[1]
    extra = out_ref.shape[1] - model_width
    states = jnp.concatenate(
        [so_ref[...].astype(jnp.float32), sp_ref[...].astype(jnp.float32)], axis=0
    )
    out_ref[:, :model_width] = normalize_rows(states).astype(jnp.bfloat16)
    dense_orig = dense_weights(io_ref[...], go_ref[...], experts, extra)
    dense_pruned = dense_weights(ip_ref[...], gp_ref[...], experts, extra)
    dense_pruned = dense_pruned * keep_ref[...]
    dense = jnp.concatenate([dense_orig, dense_pruned], axis=0)
    high = dense.astype(jnp.bfloat16).astype(jnp.float32)
    lane = lax.broadcasted_iota(jnp.int32, dense.shape, 1)
    out_ref[:, model_width:] = jnp.where(lane < experts, high, dense - high).astype(jnp.bfloat16)


def expert_kernel(
    experts, inner, outer, *refs
):
    count = inner * outer
    row_refs, refs = refs[:count], refs[count:]
    in_hbm, out_hbm, refs = refs[:SPLIT], refs[SPLIT : 2 * SPLIT], refs[2 * SPLIT :]
    result_refs, (rows, hidden, weight_in, weight_out, in_sems, out_sems) = (
        refs[:inner],
        refs[inner:],
    )
    in_copies = [
        pltpu.make_async_copy(in_hbm[k], weight_in.at[k], in_sems.at[k]) for k in range(SPLIT)
    ]
    out_copies = [
        pltpu.make_async_copy(out_hbm[k], weight_out.at[k], out_sems.at[k]) for k in range(SPLIT)
    ]
    for copy in in_copies + out_copies:
        copy.start()
    half, model_width = weight_out.shape[1:]
    size = row_refs[0].shape[0]
    expert = lax.axis_index("expert") // SPLIT
    weights = []
    for place, row_ref in enumerate(row_refs):
        rows[place * size : (place + 1) * size, :] = row_ref[:, :model_width]
        extra = row_ref[:, model_width:].astype(jnp.float32)
        lane = lax.broadcasted_iota(jnp.int32, extra.shape, 1)
        mine = jnp.logical_or(lane == expert, lane == expert + experts)
        weights.append(jnp.sum(jnp.where(mine, extra, 0.0), axis=1, keepdims=True))
    weight = jnp.concatenate(weights, axis=0)
    for place in range(SPLIT):
        in_copies[place].wait()
        both = jnp.dot(rows[...], weight_in[place], preferred_element_type=jnp.float32)
        gate, up = both[:, :half], both[:, half:]
        hidden[:, place * half : (place + 1) * half] = (
            gate / (1.0 + jnp.exp(-gate)) * up
        ).astype(jnp.bfloat16)
    for copy in out_copies:
        copy.wait()
    step = 512
    part = outer * size
    for start in range(0, model_width, step):
        value = sum(
            jnp.dot(
                hidden[:, k * half : (k + 1) * half],
                weight_out[k, :, start : start + step],
                preferred_element_type=jnp.float32,
            )
            for k in range(SPLIT)
        )
        value = (value * weight).astype(jnp.bfloat16)
        for i in range(inner):
            result_refs[i][:, start : start + step] = value[i * part : (i + 1) * part]


def plane_kernel(inner, outer, *refs):
    part_refs, (kept_ref, *send_refs) = refs[:inner], refs[inner:]
    size = kept_ref.shape[0]
    for j in range(outer):
        total = sum(
            ref[j * size : (j + 1) * size, :].astype(jnp.float32) for ref in part_refs
        )
        if j == 0:
            kept_ref[...] = total
        else:
            send_refs[j - 1][...] = total.astype(jnp.bfloat16)


def final_kernel(
    outer, factor, kept_ref, *refs
):
    part_refs, refs = refs[: outer - 1], refs[outer - 1 :]
    ids_ref, gates_ref, orig_ref, pruned_ref, value_ref, terms_ref = refs
    total = kept_ref[...]
    for ref in part_refs:
        total = total + ref[...].astype(jnp.float32)
    tok_rows = orig_ref.shape[0]
    value_ref[...] = total
    value_orig, value_pruned = total[:tok_rows], total[tok_rows:]
    orig_ref[...] = value_orig.astype(jnp.bfloat16)
    pruned_ref[...] = value_pruned.astype(jnp.bfloat16)
    differ = value_orig - value_pruned
    errors = jnp.mean(differ * differ, axis=1, keepdims=True)
    experts = terms_ref.shape[1]
    dense = dense_weights(ids_ref[...], gates_ref[...], experts, experts)
    terms_ref[...] = factor * jnp.sum(dense * errors, axis=0, keepdims=True)


def exclusive(value, axis, mask):
    pairs = [(source, source ^ mask) for source in range(lax.axis_size(axis))]
    return lax.ppermute(value, axis, pairs)


def gather_rows(packed, inner, outer):
    columns = [packed] + [exclusive(packed, "expert", SPLIT * inner * j) for j in range(1, outer)]
    placed = {(0, j): columns[j] for j in range(outer)}
    for j in range(outer):
        for i in range(1, inner):
            placed[i, j] = exclusive(columns[j], "expert", SPLIT * i)
    return [placed[i, j] for i in range(inner) for j in range(outer)]


def on_device(
    states_orig,
    states_pruned,
    ids_orig,
    ids_pruned,
    gates_orig,
    gates_pruned,
    keep_mask,
    w_in,
    w_out,
):
    devices = lax.axis_size("expert")
    section_count = lax.axis_size("section")
    section_index = lax.axis_index("section")
    micro_count, tok_rows, model_width = states_orig.shape
    experts = keep_mask.shape[1]
    top_count = ids_orig.shape[-1]
    loss_factor = experts / (top_count * micro_count * tok_rows * devices)
    extra = -(-2 * experts // LANES) * LANES
    rows = 2 * tok_rows
    own_in, own_out = w_in[0, 0], w_out[0, 0]
    pairs = [(source, source ^ 1) for source in range(devices)]
    other_in = lax.ppermute(own_in, "expert", pairs)
    other_out = lax.ppermute(own_out, "expert", pairs)
    chips = devices // SPLIT
    inner = min(4, chips)
    outer = chips // inner
    kept = jnp.tile(keep_mask.astype(jnp.float32), (1, -(-extra // experts)))[:, :extra]

    step_count = micro_count + section_count - 1
    carry = jnp.zeros((2, tok_rows, model_width), jnp.bfloat16)
    moe_orig = jnp.zeros((micro_count, tok_rows, model_width), jnp.bfloat16)
    moe_pruned = moe_orig
    terms = jnp.zeros((1, experts), jnp.float32)
    for tick in range(step_count):
        if section_count == 1:
            position, active = tick, True
            item = lambda buffer: buffer[position]
        else:
            position = jnp.clip(tick - section_index, 0, micro_count - 1)
            active = jnp.logical_and(
                tick - section_index >= 0, tick - section_index < micro_count
            )
            item = lambda buffer: lax.dynamic_index_in_dim(buffer, position, 0, keepdims=False)
        fresh = min(tick, micro_count - 1)
        state_orig, state_pruned = states_orig[fresh], states_pruned[fresh]
        if section_count > 1:
            state_orig = jnp.where(section_index == 0, state_orig, carry[0])
            state_pruned = jnp.where(section_index == 0, state_pruned, carry[1])
        picked_orig, weight_orig = item(ids_orig[0]), item(gates_orig[0])
        packed = pl.pallas_call(
            functools.partial(pack_kernel, experts),
            out_shape=jax.ShapeDtypeStruct((rows, model_width + extra), jnp.bfloat16),
            in_specs=[whole()] * 7,
            out_specs=whole(),
        )(
            state_orig,
            state_pruned,
            picked_orig,
            item(ids_pruned[0]),
            weight_orig,
            item(gates_pruned[0]),
            kept,
        )
        gathered = gather_rows(packed, inner, outer)
        partials = pl.pallas_call(
            functools.partial(expert_kernel, experts, inner, outer),
            out_shape=[jax.ShapeDtypeStruct((outer * rows, model_width), jnp.bfloat16)] * inner,
            in_specs=[whole()] * chips + [whole(pl.ANY)] * (2 * SPLIT),
            out_specs=[whole()] * inner,
            scratch_shapes=[
                pltpu.VMEM((chips * rows, model_width), jnp.bfloat16),
                pltpu.VMEM((chips * rows, SPLIT * own_out.shape[0]), jnp.bfloat16),
                pltpu.VMEM((SPLIT,) + own_in.shape, jnp.bfloat16),
                pltpu.VMEM((SPLIT,) + own_out.shape, jnp.bfloat16),
                pltpu.SemaphoreType.DMA((SPLIT,)),
                pltpu.SemaphoreType.DMA((SPLIT,)),
            ],
            compiler_params=pltpu.CompilerParams(vmem_limit_bytes=48 * 2**20),
        )(*gathered, own_in, other_in, own_out, other_out)
        partials = [partials[0]] + [
            exclusive(partials[i], "expert", SPLIT * i) for i in range(1, inner)
        ]
        kept_rows, *outgoing = pl.pallas_call(
            functools.partial(plane_kernel, inner, outer),
            out_shape=[jax.ShapeDtypeStruct((rows, model_width), jnp.float32)]
            + [jax.ShapeDtypeStruct((rows, model_width), jnp.bfloat16)] * (outer - 1),
            in_specs=[whole()] * inner,
            out_specs=[whole()] * outer,
            compiler_params=pltpu.CompilerParams(vmem_limit_bytes=48 * 2**20),
        )(*partials)
        incoming = [
            exclusive(outgoing[j - 1], "expert", SPLIT * inner * j) for j in range(1, outer)
        ]
        round_orig, round_pruned, moe, tick_terms = pl.pallas_call(
            functools.partial(final_kernel, outer, loss_factor),
            out_shape=[jax.ShapeDtypeStruct((tok_rows, model_width), jnp.bfloat16)] * 2
            + [
                jax.ShapeDtypeStruct((rows, model_width), jnp.float32),
                jax.ShapeDtypeStruct((1, experts), jnp.float32),
            ],
            in_specs=[whole()] * (outer + 2),
            out_specs=[whole()] * 4,
        )(kept_rows, *incoming, picked_orig, weight_orig)
        value_orig, value_pruned = moe[:tok_rows], moe[tok_rows:]
        if section_count > 1:
            tick_terms = jnp.where(active, tick_terms, 0.0)
            round_orig = jnp.where(active, round_orig, item(moe_orig))
            round_pruned = jnp.where(active, round_pruned, item(moe_pruned))
        terms = terms + tick_terms
        moe_orig = lax.dynamic_update_index_in_dim(moe_orig, round_orig, position, 0)
        moe_pruned = lax.dynamic_update_index_in_dim(moe_pruned, round_pruned, position, 0)
        if tick + 1 < step_count and section_count > 1:
            following = jnp.stack(
                [
                    (state_orig.astype(jnp.float32) + value_orig).astype(jnp.bfloat16),
                    (state_pruned.astype(jnp.float32) + value_pruned).astype(jnp.bfloat16),
                ]
            )
            onward = [(i, i + 1) for i in range(section_count - 1)]
            carry = lax.ppermute(following, "section", onward)
    spread = jnp.broadcast_to(terms[None], (devices, 1, experts))
    shared = lax.all_to_all(spread, "expert", split_axis=0, concat_axis=0, tiled=True)
    loss = jnp.sum(shared, axis=0)
    return (moe_orig[None], moe_pruned[None], loss)


def solution(mesh):
    return jax.shard_map(
        on_device,
        mesh=mesh,
        in_specs=(
            P(None, "expert", None),
            P(None, "expert", None),
            P("section", None, "expert", None),
            P("section", None, "expert", None),
            P("section", None, "expert", None),
            P("section", None, "expert", None),
            P("section", None),
            P("section", "expert", None, None),
            P("section", "expert", None, None),
        ),
        out_specs=(
            P("section", None, "expert", None),
            P("section", None, "expert", None),
            P("section", None),
        ),
        check_vma=False,
    )
```

```python
import functools

import jax
import jax.numpy as jnp
from jax import lax
from jax.experimental import pallas as pl
from jax.experimental.pallas import tpu as pltpu
from jax.sharding import PartitionSpec as P

SPLIT = 2
LANES = 128
MIB = 2**20


def run_kernel(body, outs, operands, scratch=(), limit=16):
    return pl.pallas_call(
        body,
        out_shape=outs,
        in_specs=[pl.BlockSpec(memory_space=pltpu.VMEM)] * len(operands),
        out_specs=jax.tree.map(lambda _: pl.BlockSpec(memory_space=pltpu.VMEM), outs),
        scratch_shapes=list(scratch),
        compiler_params=pltpu.CompilerParams(vmem_limit_bytes=limit * MIB),
    )(*operands)


def like(rows, columns, dtype=jnp.bfloat16):
    return jax.ShapeDtypeStruct((rows, columns), dtype)


def exclusive(value, mask):
    pairs = [(source, source ^ mask) for source in range(lax.axis_size("expert"))]
    return lax.ppermute(value, "expert", pairs)


def normalize_rows(values):
    factor = lax.rsqrt(jnp.mean(values * values, axis=-1, keepdims=True) + 1e-06)
    return values * factor


def dense_weights(picked, gates, experts):
    rows = picked.shape[0]
    label = lax.broadcasted_iota(jnp.int32, (rows, experts), 1)
    total = jnp.zeros((rows, experts), jnp.float32)
    for k in range(picked.shape[1]):
        total = total + jnp.where(picked[:, k : k + 1] == label, gates[:, k : k + 1], 0.0)
    return total


def pack_kernel(so_ref, sp_ref, io_ref, ip_ref, go_ref, gp_ref, keep_ref, out_ref):
    model_width = so_ref.shape[1]
    extra = out_ref.shape[1] - model_width
    experts = keep_ref.shape[1]
    states = jnp.concatenate(
        [so_ref[...].astype(jnp.float32), sp_ref[...].astype(jnp.float32)], axis=0
    )
    out_ref[:, :model_width] = normalize_rows(states).astype(jnp.bfloat16)
    dense_orig = dense_weights(io_ref[...], go_ref[...], experts)
    dense_pruned = dense_weights(ip_ref[...], gp_ref[...], experts)
    dense_pruned = dense_pruned * keep_ref[...].astype(jnp.float32)
    dense = jnp.concatenate([dense_orig, dense_pruned], axis=0)
    high = dense.astype(jnp.bfloat16)
    low = (dense - high.astype(jnp.float32)).astype(jnp.bfloat16)
    source = lax.broadcasted_iota(jnp.int32, (experts, extra), 0)
    lane = lax.broadcasted_iota(jnp.int32, (experts, extra), 1)
    out_ref[:, model_width:] = (
        jnp.dot(
            high,
            (lane == source).astype(jnp.float32).astype(jnp.bfloat16),
            preferred_element_type=jnp.float32,
        )
        + jnp.dot(
            low,
            (lane == source + experts).astype(jnp.float32).astype(jnp.bfloat16),
            preferred_element_type=jnp.float32,
        )
    ).astype(jnp.bfloat16)


def join_kernel(*refs):
    part_refs, out_ref = refs[:-1], refs[-1]
    size = part_refs[0].shape[0]
    for place, ref in enumerate(part_refs):
        out_ref[place * size : (place + 1) * size, :] = ref[...]


def expert_kernel(experts, row_count, sizes, *refs):
    row_refs, refs = refs[:row_count], refs[row_count:]
    in_refs, out_refs, refs = refs[:SPLIT], refs[SPLIT : 2 * SPLIT], refs[2 * SPLIT :]
    result_refs, (rows, hidden) = refs[: len(sizes)], refs[len(sizes) :]
    half, model_width = out_refs[0].shape
    expert = lax.axis_index("expert") // SPLIT
    weights = []
    filled = 0
    for row_ref in row_refs:
        size = row_ref.shape[0]
        rows[filled : filled + size, :] = row_ref[:, :model_width]
        filled += size
        extra = row_ref[:, model_width:].astype(jnp.float32)
        lane = lax.broadcasted_iota(jnp.int32, extra.shape, 1)
        mine = jnp.logical_or(lane == expert, lane == expert + experts)
        weights.append(jnp.sum(jnp.where(mine, extra, 0.0), axis=1, keepdims=True))
    weight = jnp.concatenate(weights, axis=0)
    for place, in_ref in enumerate(in_refs):
        both = jnp.dot(rows[...], in_ref[...], preferred_element_type=jnp.float32)
        gate, up = both[:, :half], both[:, half:]
        hidden[:, place * half : (place + 1) * half] = (
            gate / (1.0 + jnp.exp(-gate)) * up
        ).astype(jnp.bfloat16)
    step = min(512, model_width)
    for start in range(0, model_width, step):
        value = sum(
            jnp.dot(
                hidden[:, place * half : (place + 1) * half],
                out_ref[:, start : start + step],
                preferred_element_type=jnp.float32,
            )
            for place, out_ref in enumerate(out_refs)
        )
        value = (value * weight).astype(jnp.bfloat16)
        filled = 0
        for size, result_ref in zip(sizes, result_refs):
            result_ref[:, start : start + step] = value[filled : filled + size]
            filled += size


def run_expert(experts, row_arrays, weights, sizes):
    total = sum(array.shape[0] for array in row_arrays)
    half, model_width = weights[-1].shape
    return run_kernel(
        functools.partial(expert_kernel, experts, len(row_arrays), sizes),
        [like(size, model_width) for size in sizes],
        list(row_arrays) + list(weights),
        [
            pltpu.VMEM((total, model_width), jnp.bfloat16),
            pltpu.VMEM((total, SPLIT * half), jnp.bfloat16),
        ],
        limit=24,
    )


def plane_kernel(inner, outer, *refs):
    mine_ref, near_refs, far_refs = refs[0], refs[1:inner], refs[inner : 2 * inner - 1]
    kept_ref, *send_refs = refs[2 * inner - 1 :]
    size = kept_ref.shape[0]
    kept_ref[...] = mine_ref[:size, :].astype(jnp.float32) + sum(
        ref[...].astype(jnp.float32) for ref in near_refs
    )
    for j in range(1, outer):
        total = mine_ref[j * size : (j + 1) * size, :].astype(jnp.float32)
        for ref in far_refs:
            total = total + ref[(j - 1) * size : j * size, :].astype(jnp.float32)
        send_refs[j - 1][...] = total.astype(jnp.bfloat16)


def final_kernel(parts, factor, *refs):
    part_refs, refs = refs[:parts], refs[parts:]
    ids_ref, gates_ref, orig_ref, pruned_ref, terms_ref, *value_refs = refs
    total = sum(ref[...].astype(jnp.float32) for ref in part_refs)
    tok_rows = orig_ref.shape[0]
    for value_ref in value_refs:
        value_ref[...] = total
    value_orig, value_pruned = total[:tok_rows], total[tok_rows:]
    orig_ref[...] = value_orig.astype(jnp.bfloat16)
    pruned_ref[...] = value_pruned.astype(jnp.bfloat16)
    differ = value_orig - value_pruned
    errors = jnp.mean(differ * differ, axis=1, keepdims=True)
    dense = dense_weights(ids_ref[...], gates_ref[...], terms_ref.shape[1])
    terms_ref[...] = factor * jnp.sum(dense * errors, axis=0, keepdims=True)


def add_kernel(*refs):
    refs[-1][...] = sum(ref[...] for ref in refs[:-1])


def sum_over(value, masks):
    parts = [value] + [exclusive(value, mask) for mask in masks]
    return run_kernel(add_kernel, like(*value.shape, jnp.float32), parts)


def on_device(
    states_orig,
    states_pruned,
    ids_orig,
    ids_pruned,
    gates_orig,
    gates_pruned,
    keep_mask,
    w_in,
    w_out,
):
    devices = lax.axis_size("expert")
    section_count = lax.axis_size("section")
    section_index = lax.axis_index("section")
    micro_count, tok_rows, model_width = states_orig.shape
    experts = keep_mask.shape[1]
    top_count = ids_orig.shape[-1]
    loss_factor = experts / (top_count * micro_count * tok_rows * devices)
    extra = -(-2 * experts // LANES) * LANES
    rows = 2 * tok_rows
    chips = devices // SPLIT
    inner = min(4, chips)
    outer = chips // inner
    inner_masks = [SPLIT * i for i in range(1, inner)]
    outer_masks = [SPLIT * inner * j for j in range(1, outer)]
    own_in, own_out = w_in[0, 0], w_out[0, 0]
    other_in, other_out = exclusive(own_in, 1), exclusive(own_out, 1)
    weights = [own_in, other_in, own_out, other_out]

    step_count = micro_count + section_count - 1
    carry = jnp.zeros((2, tok_rows, model_width), jnp.bfloat16)
    moe_orig = jnp.zeros((micro_count, tok_rows, model_width), jnp.bfloat16)
    moe_pruned = moe_orig
    terms = jnp.zeros((1, experts), jnp.float32)
    for tick in range(step_count):
        if section_count == 1:
            position = tick
            item = lambda buffer: buffer[position]
        else:
            position = jnp.clip(tick - section_index, 0, micro_count - 1)
            active = jnp.logical_and(
                tick - section_index >= 0, tick - section_index < micro_count
            )
            item = lambda buffer: lax.dynamic_index_in_dim(buffer, position, 0, keepdims=False)
        fresh = min(tick, micro_count - 1)
        state_orig, state_pruned = states_orig[fresh], states_pruned[fresh]
        if section_count > 1:
            state_orig = jnp.where(section_index == 0, state_orig, carry[0])
            state_pruned = jnp.where(section_index == 0, state_pruned, carry[1])
        picked_orig, weight_orig = item(ids_orig[0]), item(gates_orig[0])
        packed = run_kernel(
            pack_kernel,
            like(rows, model_width + extra),
            [
                state_orig,
                state_pruned,
                picked_orig,
                item(ids_pruned[0]),
                weight_orig,
                item(gates_pruned[0]),
                keep_mask,
            ],
        )
        column = [exclusive(packed, mask) for mask in outer_masks]
        near = [exclusive(packed, mask) for mask in inner_masks]
        joined = run_kernel(join_kernel, like((outer - 1) * rows, model_width + extra), column)
        far = [exclusive(joined, mask) for mask in inner_masks]
        mine, *near_out = run_expert(
            experts,
            [packed, joined] + near,
            weights,
            [outer * rows] + [rows] * (inner - 1),
        )
        far_out = run_expert(experts, far, weights, [(outer - 1) * rows] * (inner - 1))
        near_back = [exclusive(part, mask) for part, mask in zip(near_out, inner_masks)]
        far_back = [exclusive(part, mask) for part, mask in zip(far_out, inner_masks)]
        kept_rows, *outgoing = run_kernel(
            functools.partial(plane_kernel, inner, outer),
            [like(rows, model_width, jnp.float32)] + [like(rows, model_width)] * (outer - 1),
            [mine] + near_back + far_back,
        )
        incoming = [exclusive(part, mask) for part, mask in zip(outgoing, outer_masks)]
        round_orig, round_pruned, tick_terms, *moe = run_kernel(
            functools.partial(final_kernel, outer, loss_factor),
            [like(tok_rows, model_width)] * 2
            + [like(1, experts, jnp.float32)]
            + [like(rows, model_width, jnp.float32)] * (section_count > 1),
            [kept_rows] + incoming + [picked_orig, weight_orig],
        )
        if section_count > 1:
            tick_terms = jnp.where(active, tick_terms, 0.0)
            round_orig = jnp.where(active, round_orig, item(moe_orig))
            round_pruned = jnp.where(active, round_pruned, item(moe_pruned))
        terms = tick_terms if tick == 0 else terms + tick_terms
        moe_orig = lax.dynamic_update_index_in_dim(moe_orig, round_orig, position, 0)
        moe_pruned = lax.dynamic_update_index_in_dim(moe_pruned, round_pruned, position, 0)
        if tick + 1 < step_count and section_count > 1:
            state = jnp.stack([state_orig, state_pruned]).astype(jnp.float32)
            following = (state + moe[0].reshape(state.shape)).astype(jnp.bfloat16)
            onward = [(i, i + 1) for i in range(section_count - 1)]
            carry = lax.ppermute(following, "section", onward)
    for masks in ([1], inner_masks, outer_masks):
        terms = sum_over(terms, masks)
    return (moe_orig[None], moe_pruned[None], terms)


def solution(mesh):
    return jax.shard_map(
        on_device,
        mesh=mesh,
        in_specs=(
            P(None, "expert", None),
            P(None, "expert", None),
            P("section", None, "expert", None),
            P("section", None, "expert", None),
            P("section", None, "expert", None),
            P("section", None, "expert", None),
            P("section", None),
            P("section", "expert", None, None),
            P("section", "expert", None, None),
        ),
        out_specs=(
            P("section", None, "expert", None),
            P("section", None, "expert", None),
            P("section", None),
        ),
        check_vma=False,
    )
```

```python
import functools

import jax
import jax.numpy as jnp
from jax import lax
from jax.experimental import pallas as pl
from jax.experimental.pallas import tpu as pltpu
from jax.sharding import PartitionSpec as P

SPLIT = 2
LANES = 128
MIB = 2**20


def run_kernel(body, outs, operands, scratch=(), limit=16, space=pltpu.VMEM):
    return pl.pallas_call(
        body,
        out_shape=outs,
        in_specs=[pl.BlockSpec(memory_space=space)] * len(operands),
        out_specs=jax.tree.map(lambda _: pl.BlockSpec(memory_space=pltpu.VMEM), outs),
        scratch_shapes=list(scratch),
        compiler_params=pltpu.CompilerParams(vmem_limit_bytes=limit * MIB),
    )(*operands)


def in_hbm(value):
    return pltpu.with_memory_space_constraint(value, pltpu.HBM)


def like(rows, columns, dtype=jnp.bfloat16):
    return jax.ShapeDtypeStruct((rows, columns), dtype)


def exclusive(value, mask):
    pairs = [(source, source ^ mask) for source in range(lax.axis_size("expert"))]
    return lax.ppermute(value, "expert", pairs)


def normalize_rows(values):
    factor = lax.rsqrt(jnp.mean(values * values, axis=-1, keepdims=True) + 1e-06)
    return values * factor


def dense_weights(picked, gates, experts):
    rows = picked.shape[0]
    label = lax.broadcasted_iota(jnp.int32, (rows, experts), 1)
    total = jnp.zeros((rows, experts), jnp.float32)
    for k in range(picked.shape[1]):
        total = total + jnp.where(picked[:, k : k + 1] == label, gates[:, k : k + 1], 0.0)
    return total


def pack_kernel(count, *refs):
    sources, (out_ref, spread_ref), scratch = refs[:count], refs[count : count + 2], refs[count + 2 :]
    held, sems = scratch[:count], scratch[count]
    copies = [
        pltpu.make_async_copy(source, target, sems.at[place])
        for place, (source, target) in enumerate(zip(sources, held))
    ]
    for copy in copies:
        copy.start()
    for copy in copies:
        copy.wait()
    so_ref, sp_ref, io_ref, ip_ref, go_ref, gp_ref, keep_ref = held
    model_width = so_ref.shape[1]
    extra = out_ref.shape[1] - model_width
    experts = keep_ref.shape[1]
    states = jnp.concatenate(
        [so_ref[...].astype(jnp.float32), sp_ref[...].astype(jnp.float32)], axis=0
    )
    out_ref[:, :model_width] = normalize_rows(states).astype(jnp.bfloat16)
    dense_orig = dense_weights(io_ref[...], go_ref[...], experts)
    dense_pruned = dense_weights(ip_ref[...], gp_ref[...], experts)
    dense_pruned = dense_pruned * keep_ref[...].astype(jnp.float32)
    dense = jnp.concatenate([dense_orig, dense_pruned], axis=0)
    high = dense.astype(jnp.bfloat16)
    low = (dense - high.astype(jnp.float32)).astype(jnp.bfloat16)
    source = lax.broadcasted_iota(jnp.int32, (experts, extra), 0)
    lane = lax.broadcasted_iota(jnp.int32, (experts, extra), 1)
    out_ref[:, model_width:] = (
        jnp.dot(
            high,
            (lane == source).astype(jnp.float32).astype(jnp.bfloat16),
            preferred_element_type=jnp.float32,
        )
        + jnp.dot(
            low,
            (lane == source + experts).astype(jnp.float32).astype(jnp.bfloat16),
            preferred_element_type=jnp.float32,
        )
    ).astype(jnp.bfloat16)


    rows = out_ref.shape[0]
    for place in range(spread_ref.shape[0] // rows):
        spread_ref[place * rows : (place + 1) * rows, :] = out_ref[...]


def at_distance(j, inner, rows):
    layer = lax.axis_index("expert") // (SPLIT * inner)
    return pl.ds(pl.multiple_of((layer ^ j) * rows, rows), rows)


def stage_kernel(count, *refs):
    sources, targets, sems = refs[:count], refs[count : 2 * count], refs[2 * count]
    copies = [
        pltpu.make_async_copy(source, target, sems.at[place])
        for place, (source, target) in enumerate(zip(sources, targets))
    ]
    for copy in copies:
        copy.start()
    for copy in copies:
        copy.wait()


def join_kernel(inner, column_ref, packed_ref, *refs):
    near_refs, (far_ref, early_ref) = refs[:-2], refs[-2:]
    rows = packed_ref.shape[0]
    early_ref[:rows, :] = packed_ref[...]
    for j in range(1, column_ref.shape[0] // rows):
        block = column_ref[at_distance(j, inner, rows), :]
        far_ref[(j - 1) * rows : j * rows, :] = block
        early_ref[j * rows : (j + 1) * rows, :] = block
    for place, near_ref in enumerate(near_refs):
        start = column_ref.shape[0] + place * rows
        early_ref[start : start + rows, :] = near_ref[...]


def expert_kernel(experts, row_count, sizes, *refs):
    row_refs, refs = refs[:row_count], refs[row_count:]
    in_refs, out_refs, refs = refs[:SPLIT], refs[SPLIT : 2 * SPLIT], refs[2 * SPLIT :]
    result_refs, (rows, hidden) = refs[: len(sizes)], refs[len(sizes) :]
    half, model_width = out_refs[0].shape
    expert = lax.axis_index("expert") // SPLIT
    weights = []
    filled = 0
    for row_ref in row_refs:
        size = row_ref.shape[0]
        rows[filled : filled + size, :] = row_ref[:, :model_width]
        filled += size
        extra = row_ref[:, model_width:].astype(jnp.float32)
        lane = lax.broadcasted_iota(jnp.int32, extra.shape, 1)
        mine = jnp.logical_or(lane == expert, lane == expert + experts)
        weights.append(jnp.sum(jnp.where(mine, extra, 0.0), axis=1, keepdims=True))
    weight = jnp.concatenate(weights, axis=0)
    for place, in_ref in enumerate(in_refs):
        both = jnp.dot(rows[...], in_ref[...], preferred_element_type=jnp.float32)
        gate, up = both[:, :half], both[:, half:]
        hidden[:, place * half : (place + 1) * half] = (
            gate / (1.0 + jnp.exp(-gate)) * up
        ).astype(jnp.bfloat16)
    step = min(512, model_width)
    for start in range(0, model_width, step):
        value = sum(
            jnp.dot(
                hidden[:, place * half : (place + 1) * half],
                out_ref[:, start : start + step],
                preferred_element_type=jnp.float32,
            )
            for place, out_ref in enumerate(out_refs)
        )
        value = (value * weight).astype(jnp.bfloat16)
        filled = 0
        for size, result_ref in zip(sizes, result_refs):
            result_ref[:, start : start + step] = value[filled : filled + size]
            filled += size


def run_expert(experts, row_arrays, weights, sizes):
    total = sum(array.shape[0] for array in row_arrays)
    half, model_width = weights[-1].shape
    return run_kernel(
        functools.partial(expert_kernel, experts, len(row_arrays), sizes),
        [like(size, model_width) for size in sizes],
        list(row_arrays) + list(weights),
        [
            pltpu.VMEM((total, model_width), jnp.bfloat16),
            pltpu.VMEM((total, SPLIT * half), jnp.bfloat16),
        ],
        limit=24,
    )


def plane_kernel(inner, mine_ref, *refs):
    part_refs, out_ref = refs[:-1], refs[-1]
    rows = mine_ref.shape[0] - part_refs[0].shape[0]
    for j in range(out_ref.shape[0] // rows):
        if j == 0:
            total = jnp.zeros((rows, out_ref.shape[1]), jnp.float32)
        else:
            total = mine_ref[j * rows : (j + 1) * rows, :].astype(jnp.float32)
            for ref in part_refs:
                total = total + ref[(j - 1) * rows : j * rows, :].astype(jnp.float32)
        out_ref[at_distance(j, inner, rows), :] = total.astype(jnp.bfloat16)


def final_kernel(parts, factor, *refs):
    column_ref, mine_ref, near_refs, refs = refs[0], refs[1], refs[2:parts], refs[parts:]
    ids_ref, gates_ref, orig_ref, pruned_ref, terms_ref, *value_refs = refs
    tok_rows = orig_ref.shape[0]
    rows = 2 * tok_rows
    total = mine_ref[:rows, :].astype(jnp.float32)
    for ref in near_refs:
        total = total + ref[...].astype(jnp.float32)
    for place in range(column_ref.shape[0] // rows):
        total = total + column_ref[place * rows : (place + 1) * rows, :].astype(jnp.float32)
    for value_ref in value_refs:
        value_ref[...] = total
    value_orig, value_pruned = total[:tok_rows], total[tok_rows:]
    orig_ref[...] = value_orig.astype(jnp.bfloat16)
    pruned_ref[...] = value_pruned.astype(jnp.bfloat16)
    differ = value_orig - value_pruned
    errors = jnp.mean(differ * differ, axis=1, keepdims=True)
    experts = terms_ref.shape[1]
    dense = dense_weights(ids_ref[...], gates_ref[...], experts)
    terms = factor * jnp.sum(dense * errors, axis=0, keepdims=True)
    terms_ref[...] = jnp.broadcast_to(terms, terms_ref.shape)


def add_kernel(parts_ref, out_ref):
    out_ref[...] = jnp.sum(parts_ref[...], axis=0, keepdims=True)


def on_device(
    states_orig,
    states_pruned,
    ids_orig,
    ids_pruned,
    gates_orig,
    gates_pruned,
    keep_mask,
    w_in,
    w_out,
):
    devices = lax.axis_size("expert")
    section_count = lax.axis_size("section")
    section_index = lax.axis_index("section")
    micro_count, tok_rows, model_width = states_orig.shape
    experts = keep_mask.shape[1]
    top_count = ids_orig.shape[-1]
    loss_factor = experts / (top_count * micro_count * tok_rows * devices)
    extra = -(-2 * experts // LANES) * LANES
    rows = 2 * tok_rows
    chips = devices // SPLIT
    inner = min(4, chips)
    outer = chips // inner
    inner_masks = [SPLIT * i for i in range(1, inner)]
    columns = [
        [place + SPLIT * inner * j for j in range(outer)] for place in range(SPLIT * inner)
    ]
    along_column = functools.partial(
        lax.all_to_all,
        axis_name="expert",
        split_axis=0,
        concat_axis=0,
        axis_index_groups=columns,
        tiled=True,
    )
    own_in, own_out = w_in[0, 0], w_out[0, 0]
    other_in, other_out = exclusive(own_in, 1), exclusive(own_out, 1)
    weights = [own_in, other_in, own_out, other_out]
    weights = run_kernel(
        functools.partial(stage_kernel, len(weights)),
        [pltpu.VMEM(value.shape, value.dtype) for value in weights],
        [in_hbm(own_in), other_in, in_hbm(own_out), other_out],
        [pltpu.SemaphoreType.DMA((len(weights),))],
        space=pl.ANY,
    )

    step_count = micro_count + section_count - 1
    carry = jnp.zeros((2, tok_rows, model_width), jnp.bfloat16)
    moe_orig = jnp.zeros((micro_count, tok_rows, model_width), jnp.bfloat16)
    moe_pruned = moe_orig
    terms = jnp.zeros((devices, experts), jnp.float32)
    for tick in range(step_count):
        if section_count == 1:
            position = tick
            item = lambda buffer: buffer[position]
        else:
            position = jnp.clip(tick - section_index, 0, micro_count - 1)
            active = jnp.logical_and(
                tick - section_index >= 0, tick - section_index < micro_count
            )
            item = lambda buffer: lax.dynamic_index_in_dim(buffer, position, 0, keepdims=False)
        fresh = min(tick, micro_count - 1)
        state_orig, state_pruned = states_orig[fresh], states_pruned[fresh]
        if section_count > 1:
            state_orig = jnp.where(section_index == 0, state_orig, carry[0])
            state_pruned = jnp.where(section_index == 0, state_pruned, carry[1])
        picked_orig, weight_orig = item(ids_orig[0]), item(gates_orig[0])
        operands = [
            state_orig,
            state_pruned,
            picked_orig,
            item(ids_pruned[0]),
            weight_orig,
            item(gates_pruned[0]),
            keep_mask,
        ]
        packed, spread = run_kernel(
            functools.partial(pack_kernel, len(operands)),
            [like(rows, model_width + extra), like(outer * rows, model_width + extra)],
            [in_hbm(value) for value in operands],
            [pltpu.VMEM(value.shape, value.dtype) for value in operands]
            + [pltpu.SemaphoreType.DMA((len(operands),))],
            space=pl.ANY,
        )
        column = along_column(spread)
        near = [exclusive(packed, mask) for mask in inner_masks]
        joined, early = run_kernel(
            functools.partial(join_kernel, inner),
            [
                like((outer - 1) * rows, model_width + extra),
                like((outer + inner - 1) * rows, model_width + extra),
            ],
            [column, packed] + near,
        )
        far = [exclusive(joined, mask) for mask in inner_masks]
        far_out = run_expert(experts, far, weights, [(outer - 1) * rows] * (inner - 1))
        far_back = [exclusive(part, mask) for part, mask in zip(far_out, inner_masks)]
        mine, *near_out = run_expert(
            experts,
            [early],
            weights,
            [outer * rows] + [rows] * (inner - 1),
        )
        near_back = [exclusive(part, mask) for part, mask in zip(near_out, inner_masks)]
        outgoing = run_kernel(
            functools.partial(plane_kernel, inner),
            like(outer * rows, model_width),
            [mine] + far_back,
        )
        incoming = along_column(outgoing)
        round_orig, round_pruned, tick_terms, *moe = run_kernel(
            functools.partial(final_kernel, inner + 1, loss_factor),
            [like(tok_rows, model_width)] * 2
            + [like(devices, experts, jnp.float32)]
            + [like(rows, model_width, jnp.float32)] * (section_count > 1),
            [incoming, mine] + near_back + [picked_orig, weight_orig],
        )
        if section_count > 1:
            tick_terms = jnp.where(active, tick_terms, 0.0)
            round_orig = jnp.where(active, round_orig, item(moe_orig))
            round_pruned = jnp.where(active, round_pruned, item(moe_pruned))
        terms = tick_terms if tick == 0 else terms + tick_terms
        moe_orig = lax.dynamic_update_index_in_dim(moe_orig, round_orig, position, 0)
        moe_pruned = lax.dynamic_update_index_in_dim(moe_pruned, round_pruned, position, 0)
        if tick + 1 < step_count and section_count > 1:
            state = jnp.stack([state_orig, state_pruned]).astype(jnp.float32)
            following = (state + moe[0].reshape(state.shape)).astype(jnp.bfloat16)
            onward = [(i, i + 1) for i in range(section_count - 1)]
            carry = lax.ppermute(following, "section", onward)
    shared = lax.all_to_all(terms, "expert", split_axis=0, concat_axis=0, tiled=True)
    loss = run_kernel(add_kernel, like(1, experts, jnp.float32), [shared])
    return (moe_orig[None], moe_pruned[None], loss)


def solution(mesh):
    return jax.shard_map(
        on_device,
        mesh=mesh,
        in_specs=(
            P(None, "expert", None),
            P(None, "expert", None),
            P("section", None, "expert", None),
            P("section", None, "expert", None),
            P("section", None, "expert", None),
            P("section", None, "expert", None),
            P("section", None),
            P("section", "expert", None, None),
            P("section", "expert", None, None),
        ),
        out_specs=(
            P("section", None, "expert", None),
            P("section", None, "expert", None),
            P("section", None),
        ),
        check_vma=False,
    )
```

```python
import functools

import jax
import jax.numpy as jnp
from jax import lax
from jax.experimental import pallas as pl
from jax.experimental.pallas import tpu as pltpu
from jax.sharding import PartitionSpec as P

SPLIT = 2
LANES = 128
MIB = 2**20


def run_kernel(body, outs, operands, scratch=(), limit=16, space=pltpu.VMEM):
    return pl.pallas_call(
        body,
        out_shape=outs,
        in_specs=[pl.BlockSpec(memory_space=space)] * len(operands),
        out_specs=jax.tree.map(lambda _: pl.BlockSpec(memory_space=pltpu.VMEM), outs),
        scratch_shapes=list(scratch),
        compiler_params=pltpu.CompilerParams(vmem_limit_bytes=limit * MIB),
    )(*operands)


def in_hbm(value):
    return pltpu.with_memory_space_constraint(value, pltpu.HBM)


def like(rows, columns, dtype=jnp.bfloat16):
    return jax.ShapeDtypeStruct((rows, columns), dtype)


def exclusive(value, mask):
    pairs = [(source, source ^ mask) for source in range(lax.axis_size("expert"))]
    return lax.ppermute(value, "expert", pairs)


def normalize_rows(values):
    factor = lax.rsqrt(jnp.mean(values * values, axis=-1, keepdims=True) + 1e-06)
    return values * factor


def dense_weights(picked, gates, experts):
    rows = picked.shape[0]
    label = lax.broadcasted_iota(jnp.int32, (rows, experts), 1)
    total = jnp.zeros((rows, experts), jnp.float32)
    for k in range(picked.shape[1]):
        total = total + jnp.where(picked[:, k : k + 1] == label, gates[:, k : k + 1], 0.0)
    return total


def pack_kernel(count, *refs):
    sources, out_ref, scratch = refs[:count], refs[count], refs[count + 1 :]
    held, sems = scratch[:count], scratch[count]
    copies = [
        pltpu.make_async_copy(source, target, sems.at[place])
        for place, (source, target) in enumerate(zip(sources, held))
    ]
    for copy in copies:
        copy.start()
    for copy in copies:
        copy.wait()
    so_ref, sp_ref, io_ref, ip_ref, go_ref, gp_ref, keep_ref = held
    model_width = so_ref.shape[1]
    extra = out_ref.shape[1] - model_width
    experts = keep_ref.shape[1]
    states = jnp.concatenate(
        [so_ref[...].astype(jnp.float32), sp_ref[...].astype(jnp.float32)], axis=0
    )
    out_ref[:, :model_width] = normalize_rows(states).astype(jnp.bfloat16)
    dense_orig = dense_weights(io_ref[...], go_ref[...], experts)
    dense_pruned = dense_weights(ip_ref[...], gp_ref[...], experts)
    dense_pruned = dense_pruned * keep_ref[...].astype(jnp.float32)
    dense = jnp.concatenate([dense_orig, dense_pruned], axis=0)
    high = dense.astype(jnp.bfloat16)
    low = (dense - high.astype(jnp.float32)).astype(jnp.bfloat16)
    source = lax.broadcasted_iota(jnp.int32, (experts, extra), 0)
    lane = lax.broadcasted_iota(jnp.int32, (experts, extra), 1)
    out_ref[:, model_width:] = (
        jnp.dot(
            high,
            (lane == source).astype(jnp.float32).astype(jnp.bfloat16),
            preferred_element_type=jnp.float32,
        )
        + jnp.dot(
            low,
            (lane == source + experts).astype(jnp.float32).astype(jnp.bfloat16),
            preferred_element_type=jnp.float32,
        )
    ).astype(jnp.bfloat16)


def stage_kernel(count, *refs):
    sources, targets, sems = refs[:count], refs[count : 2 * count], refs[2 * count]
    copies = [
        pltpu.make_async_copy(source, target, sems.at[place])
        for place, (source, target) in enumerate(zip(sources, targets))
    ]
    for copy in copies:
        copy.start()
    for copy in copies:
        copy.wait()


def stage_weights(own_in, own_out, awaited):
    sent_out, _ = lax.optimization_barrier((own_out, awaited))
    other_in, other_out = exclusive(own_in, 1), exclusive(sent_out, 1)
    weights = [in_hbm(own_in), other_in, in_hbm(own_out), other_out]
    return run_kernel(
        functools.partial(stage_kernel, len(weights)),
        [pltpu.VMEM(value.shape, value.dtype) for value in weights],
        weights,
        [pltpu.SemaphoreType.DMA((len(weights),))],
        space=pl.ANY,
    )


def join_kernel(outer, packed_ref, *refs):
    part_refs, (far_ref, early_ref) = refs[:-2], refs[-2:]
    rows = packed_ref.shape[0]
    early_ref[:rows, :] = packed_ref[...]
    for place, part_ref in enumerate(part_refs):
        early_ref[(place + 1) * rows : (place + 2) * rows, :] = part_ref[...]
        if place < outer - 1:
            far_ref[place * rows : (place + 1) * rows, :] = part_ref[...]


def expert_kernel(experts, row_count, sizes, *refs):
    row_refs, refs = refs[:row_count], refs[row_count:]
    in_refs, out_refs, refs = refs[:SPLIT], refs[SPLIT : 2 * SPLIT], refs[2 * SPLIT :]
    result_refs, (rows, hidden) = refs[: len(sizes)], refs[len(sizes) :]
    half, model_width = out_refs[0].shape
    expert = lax.axis_index("expert") // SPLIT
    weights = []
    filled = 0
    for row_ref in row_refs:
        size = row_ref.shape[0]
        rows[filled : filled + size, :] = row_ref[:, :model_width]
        filled += size
        extra = row_ref[:, model_width:].astype(jnp.float32)
        lane = lax.broadcasted_iota(jnp.int32, extra.shape, 1)
        mine = jnp.logical_or(lane == expert, lane == expert + experts)
        weights.append(jnp.sum(jnp.where(mine, extra, 0.0), axis=1, keepdims=True))
    weight = jnp.concatenate(weights, axis=0)
    for place, in_ref in enumerate(in_refs):
        both = jnp.dot(rows[...], in_ref[...], preferred_element_type=jnp.float32)
        gate, up = both[:, :half], both[:, half:]
        hidden[:, place * half : (place + 1) * half] = (
            gate / (1.0 + jnp.exp(-gate)) * up
        ).astype(jnp.bfloat16)
    step = min(512, model_width)
    for start in range(0, model_width, step):
        value = sum(
            jnp.dot(
                hidden[:, place * half : (place + 1) * half],
                out_ref[:, start : start + step],
                preferred_element_type=jnp.float32,
            )
            for place, out_ref in enumerate(out_refs)
        )
        value = (value * weight).astype(jnp.bfloat16)
        filled = 0
        for size, result_ref in zip(sizes, result_refs):
            result_ref[:, start : start + step] = value[filled : filled + size]
            filled += size


def run_expert(experts, row_arrays, weights, sizes):
    total = sum(array.shape[0] for array in row_arrays)
    half, model_width = weights[-1].shape
    return run_kernel(
        functools.partial(expert_kernel, experts, len(row_arrays), sizes),
        [like(size, model_width) for size in sizes],
        list(row_arrays) + list(weights),
        [
            pltpu.VMEM((total, model_width), jnp.bfloat16),
            pltpu.VMEM((total, SPLIT * half), jnp.bfloat16),
        ],
        limit=24,
    )


def plane_kernel(inner, outer, mine_ref, *refs):
    far_refs, near_refs, refs = refs[: inner - 1], refs[inner - 1 : 2 * inner - 2], refs[2 * inner - 2 :]
    sum_refs, sent_refs = refs[: outer - 1], refs[outer - 1 :]
    rows = near_refs[0].shape[0]
    for place, sum_ref in enumerate(sum_refs):
        total = mine_ref[(place + 1) * rows : (place + 2) * rows, :].astype(jnp.float32)
        for ref in far_refs:
            total = total + ref[place * rows : (place + 1) * rows, :].astype(jnp.float32)
        sum_ref[...] = total.astype(jnp.bfloat16)
    for near_ref, sent_ref in zip(near_refs, sent_refs):
        sent_ref[...] = near_ref[...]


def final_kernel(parts, factor, *refs):
    mine_ref, part_refs, refs = refs[0], refs[1:parts], refs[parts:]
    ids_ref, gates_ref, orig_ref, pruned_ref, terms_ref, *value_refs = refs
    tok_rows = orig_ref.shape[0]
    rows = 2 * tok_rows
    total = mine_ref[:rows, :].astype(jnp.float32)
    for ref in part_refs:
        total = total + ref[...].astype(jnp.float32)
    for value_ref in value_refs:
        value_ref[...] = total
    value_orig, value_pruned = total[:tok_rows], total[tok_rows:]
    orig_ref[...] = value_orig.astype(jnp.bfloat16)
    pruned_ref[...] = value_pruned.astype(jnp.bfloat16)
    differ = value_orig - value_pruned
    errors = jnp.mean(differ * differ, axis=1, keepdims=True)
    experts = terms_ref.shape[1]
    dense = dense_weights(ids_ref[...], gates_ref[...], experts)
    terms = factor * jnp.sum(dense * errors, axis=0, keepdims=True)
    terms_ref[...] = jnp.broadcast_to(terms, terms_ref.shape)


def add_kernel(parts_ref, out_ref):
    out_ref[...] = jnp.sum(parts_ref[...], axis=0, keepdims=True)


def on_device(
    states_orig,
    states_pruned,
    ids_orig,
    ids_pruned,
    gates_orig,
    gates_pruned,
    keep_mask,
    w_in,
    w_out,
):
    devices = lax.axis_size("expert")
    section_count = lax.axis_size("section")
    section_index = lax.axis_index("section")
    micro_count, tok_rows, model_width = states_orig.shape
    experts = keep_mask.shape[1]
    top_count = ids_orig.shape[-1]
    loss_factor = experts / (top_count * micro_count * tok_rows * devices)
    extra = -(-2 * experts // LANES) * LANES
    rows = 2 * tok_rows
    chips = devices // SPLIT
    inner = min(4, chips)
    outer = chips // inner
    inner_masks = [SPLIT * i for i in range(1, inner)]
    outer_masks = [SPLIT * inner * j for j in reversed(range(1, outer))]
    own_in, own_out = w_in[0, 0], w_out[0, 0]
    step_count = micro_count + section_count - 1
    carry = jnp.zeros((2, tok_rows, model_width), jnp.bfloat16)
    moe_orig = jnp.zeros((micro_count, tok_rows, model_width), jnp.bfloat16)
    moe_pruned = moe_orig
    terms = jnp.zeros((devices, experts), jnp.float32)
    for tick in range(step_count):
        if section_count == 1:
            position = tick
            item = lambda buffer: buffer[position]
        else:
            position = jnp.clip(tick - section_index, 0, micro_count - 1)
            active = jnp.logical_and(
                tick - section_index >= 0, tick - section_index < micro_count
            )
            item = lambda buffer: lax.dynamic_index_in_dim(buffer, position, 0, keepdims=False)
        fresh = min(tick, micro_count - 1)
        state_orig, state_pruned = states_orig[fresh], states_pruned[fresh]
        if section_count > 1:
            state_orig = jnp.where(section_index == 0, state_orig, carry[0])
            state_pruned = jnp.where(section_index == 0, state_pruned, carry[1])
        picked_orig, weight_orig = item(ids_orig[0]), item(gates_orig[0])
        operands = [
            state_orig,
            state_pruned,
            picked_orig,
            item(ids_pruned[0]),
            weight_orig,
            item(gates_pruned[0]),
            keep_mask,
        ]
        packed = run_kernel(
            functools.partial(pack_kernel, len(operands)),
            like(rows, model_width + extra),
            [in_hbm(value) for value in operands],
            [pltpu.VMEM(value.shape, value.dtype) for value in operands]
            + [pltpu.SemaphoreType.DMA((len(operands),))],
            space=pl.ANY,
        )
        column = [exclusive(packed, mask) for mask in outer_masks]
        near = [exclusive(packed, mask) for mask in inner_masks]
        joined, early = run_kernel(
            functools.partial(join_kernel, outer),
            [
                like((outer - 1) * rows, model_width + extra),
                like((outer + inner - 1) * rows, model_width + extra),
            ],
            [packed] + column + near,
        )
        if tick == 0:
            weights = stage_weights(own_in, own_out, joined)
        far = [exclusive(joined, mask) for mask in inner_masks]
        far_out = run_expert(experts, far, weights, [(outer - 1) * rows] * (inner - 1))
        far_back = [exclusive(part, mask) for part, mask in zip(far_out, inner_masks)]
        mine, *near_out = run_expert(
            experts,
            [early],
            weights,
            [outer * rows] + [rows] * (inner - 1),
        )
        outgoing = run_kernel(
            functools.partial(plane_kernel, inner, outer),
            [like(rows, model_width)] * (outer + inner - 2),
            [mine] + far_back + near_out,
        )
        incoming = [
            exclusive(part, mask) for part, mask in zip(outgoing, outer_masks + inner_masks)
        ]
        round_orig, round_pruned, tick_terms, *moe = run_kernel(
            functools.partial(final_kernel, outer + inner - 1, loss_factor),
            [like(tok_rows, model_width)] * 2
            + [like(devices, experts, jnp.float32)]
            + [like(rows, model_width, jnp.float32)] * (section_count > 1),
            [mine] + incoming + [picked_orig, weight_orig],
        )
        if section_count > 1:
            tick_terms = jnp.where(active, tick_terms, 0.0)
            round_orig = jnp.where(active, round_orig, item(moe_orig))
            round_pruned = jnp.where(active, round_pruned, item(moe_pruned))
        terms = tick_terms if tick == 0 else terms + tick_terms
        moe_orig = lax.dynamic_update_index_in_dim(moe_orig, round_orig, position, 0)
        moe_pruned = lax.dynamic_update_index_in_dim(moe_pruned, round_pruned, position, 0)
        if tick + 1 < step_count and section_count > 1:
            state = jnp.stack([state_orig, state_pruned]).astype(jnp.float32)
            following = (state + moe[0].reshape(state.shape)).astype(jnp.bfloat16)
            onward = [(i, i + 1) for i in range(section_count - 1)]
            carry = lax.ppermute(following, "section", onward)
    shared = lax.all_to_all(terms, "expert", split_axis=0, concat_axis=0, tiled=True)
    loss = run_kernel(add_kernel, like(1, experts, jnp.float32), [shared])
    return (moe_orig[None], moe_pruned[None], loss)


def solution(mesh):
    return jax.shard_map(
        on_device,
        mesh=mesh,
        in_specs=(
            P(None, "expert", None),
            P(None, "expert", None),
            P("section", None, "expert", None),
            P("section", None, "expert", None),
            P("section", None, "expert", None),
            P("section", None, "expert", None),
            P("section", None),
            P("section", "expert", None, None),
            P("section", "expert", None, None),
        ),
        out_specs=(
            P("section", None, "expert", None),
            P("section", None, "expert", None),
            P("section", None),
        ),
        check_vma=False,
    )
```

```python
import functools

import jax
import jax.numpy as jnp
from jax import lax
from jax.experimental import pallas as pl
from jax.experimental.pallas import tpu as pltpu
from jax.sharding import PartitionSpec as P

SPLIT = 2
LANES = 128
MIB = 2**20


def run_kernel(body, outs, operands, scratch=(), limit=16, space=pltpu.VMEM):
    return pl.pallas_call(
        body,
        out_shape=outs,
        in_specs=[pl.BlockSpec(memory_space=space)] * len(operands),
        out_specs=jax.tree.map(lambda _: pl.BlockSpec(memory_space=pltpu.VMEM), outs),
        scratch_shapes=list(scratch),
        compiler_params=pltpu.CompilerParams(vmem_limit_bytes=limit * MIB),
    )(*operands)


def in_hbm(value):
    return pltpu.with_memory_space_constraint(value, pltpu.HBM)


def like(rows, columns, dtype=jnp.bfloat16):
    return jax.ShapeDtypeStruct((rows, columns), dtype)


def exclusive(value, mask):
    pairs = [(source, source ^ mask) for source in range(lax.axis_size("expert"))]
    return lax.ppermute(value, "expert", pairs)


def normalize_rows(values):
    factor = lax.rsqrt(jnp.mean(values * values, axis=-1, keepdims=True) + 1e-06)
    return values * factor


def dense_weights(picked, gates, experts):
    rows = picked.shape[0]
    label = lax.broadcasted_iota(jnp.int32, (rows, experts), 1)
    total = jnp.zeros((rows, experts), jnp.float32)
    for k in range(picked.shape[1]):
        total = total + jnp.where(picked[:, k : k + 1] == label, gates[:, k : k + 1], 0.0)
    return total


def pack_kernel(count, *refs):
    sources, out_ref, scratch = refs[:count], refs[count], refs[count + 1 :]
    held, sems = scratch[:count], scratch[count]
    copies = [
        pltpu.make_async_copy(source, target, sems.at[place])
        for place, (source, target) in enumerate(zip(sources, held))
    ]
    for copy in copies:
        copy.start()
    for copy in copies:
        copy.wait()
    so_ref, sp_ref, io_ref, ip_ref, go_ref, gp_ref, keep_ref = held
    model_width = so_ref.shape[1]
    extra = out_ref.shape[1] - model_width
    experts = keep_ref.shape[1]
    states = jnp.concatenate(
        [so_ref[...].astype(jnp.float32), sp_ref[...].astype(jnp.float32)], axis=0
    )
    out_ref[:, :model_width] = normalize_rows(states).astype(jnp.bfloat16)
    dense_orig = dense_weights(io_ref[...], go_ref[...], experts)
    dense_pruned = dense_weights(ip_ref[...], gp_ref[...], experts)
    dense_pruned = dense_pruned * keep_ref[...].astype(jnp.float32)
    dense = jnp.concatenate([dense_orig, dense_pruned], axis=0)
    high = dense.astype(jnp.bfloat16)
    low = (dense - high.astype(jnp.float32)).astype(jnp.bfloat16)
    source = lax.broadcasted_iota(jnp.int32, (experts, extra), 0)
    lane = lax.broadcasted_iota(jnp.int32, (experts, extra), 1)
    out_ref[:, model_width:] = (
        jnp.dot(
            high,
            (lane == source).astype(jnp.float32).astype(jnp.bfloat16),
            preferred_element_type=jnp.float32,
        )
        + jnp.dot(
            low,
            (lane == source + experts).astype(jnp.float32).astype(jnp.bfloat16),
            preferred_element_type=jnp.float32,
        )
    ).astype(jnp.bfloat16)


def stage_kernel(count, *refs):
    sources, targets, sems = refs[:count], refs[count : 2 * count], refs[2 * count]
    copies = [
        pltpu.make_async_copy(source, target, sems.at[place])
        for place, (source, target) in enumerate(zip(sources, targets))
    ]
    for copy in copies:
        copy.start()
    for copy in copies:
        copy.wait()


def stage_weights(own_in, own_out, other_in, other_out):
    weights = [in_hbm(own_in), other_in, in_hbm(own_out), other_out]
    return run_kernel(
        functools.partial(stage_kernel, len(weights)),
        [pltpu.VMEM(value.shape, value.dtype) for value in weights],
        weights,
        [pltpu.SemaphoreType.DMA((len(weights),))],
        space=pl.ANY,
    )


def after(value, *awaited):
    return lax.optimization_barrier((value, awaited))[0]


def join_kernel(*refs):
    part_refs, out_ref = refs[:-1], refs[-1]
    rows = part_refs[0].shape[0]
    for place, part_ref in enumerate(part_refs):
        out_ref[place * rows : (place + 1) * rows, :] = part_ref[...]


def join_rows(parts):
    rows, columns = parts[0].shape
    return run_kernel(join_kernel, like(len(parts) * rows, columns), parts)


def expert_kernel(experts, row_count, sizes, *refs):
    row_refs, refs = refs[:row_count], refs[row_count:]
    in_refs, out_refs, refs = refs[:SPLIT], refs[SPLIT : 2 * SPLIT], refs[2 * SPLIT :]
    result_refs, (rows, hidden) = refs[: len(sizes)], refs[len(sizes) :]
    half, model_width = out_refs[0].shape
    expert = lax.axis_index("expert") // SPLIT
    weights = []
    filled = 0
    for row_ref in row_refs:
        size = row_ref.shape[0]
        rows[filled : filled + size, :] = row_ref[:, :model_width]
        filled += size
        extra = row_ref[:, model_width:].astype(jnp.float32)
        lane = lax.broadcasted_iota(jnp.int32, extra.shape, 1)
        mine = jnp.logical_or(lane == expert, lane == expert + experts)
        weights.append(jnp.sum(jnp.where(mine, extra, 0.0), axis=1, keepdims=True))
    weight = jnp.concatenate(weights, axis=0)
    for place, in_ref in enumerate(in_refs):
        both = jnp.dot(rows[...], in_ref[...], preferred_element_type=jnp.float32)
        gate, up = both[:, :half], both[:, half:]
        hidden[:, place * half : (place + 1) * half] = (
            gate / (1.0 + jnp.exp(-gate)) * up
        ).astype(jnp.bfloat16)
    step = min(512, model_width)
    for start in range(0, model_width, step):
        value = sum(
            jnp.dot(
                hidden[:, place * half : (place + 1) * half],
                out_ref[:, start : start + step],
                preferred_element_type=jnp.float32,
            )
            for place, out_ref in enumerate(out_refs)
        )
        value = (value * weight).astype(jnp.bfloat16)
        filled = 0
        for size, result_ref in zip(sizes, result_refs):
            result_ref[:, start : start + step] = value[filled : filled + size]
            filled += size


def run_expert(experts, row_arrays, weights, sizes):
    total = sum(array.shape[0] for array in row_arrays)
    half, model_width = weights[-1].shape
    return run_kernel(
        functools.partial(expert_kernel, experts, len(row_arrays), sizes),
        [like(size, model_width) for size in sizes],
        list(row_arrays) + list(weights),
        [
            pltpu.VMEM((total, model_width), jnp.bfloat16),
            pltpu.VMEM((total, SPLIT * half), jnp.bfloat16),
        ],
        limit=24,
    )


def plane_kernel(count, *refs):
    part_refs, out_refs = refs[:count], refs[count:]
    rows = out_refs[0].shape[0]
    for place, out_ref in enumerate(out_refs):
        out_ref[...] = sum(
            ref[place * rows : (place + 1) * rows, :].astype(jnp.float32) for ref in part_refs
        ).astype(out_ref.dtype)


def final_kernel(parts, factor, *refs):
    part_refs, refs = refs[:parts], refs[parts:]
    ids_ref, gates_ref, orig_ref, pruned_ref, terms_ref, *value_refs = refs
    tok_rows = orig_ref.shape[0]
    total = sum(ref[...].astype(jnp.float32) for ref in part_refs)
    for value_ref in value_refs:
        value_ref[...] = total
    value_orig, value_pruned = total[:tok_rows], total[tok_rows:]
    orig_ref[...] = value_orig.astype(jnp.bfloat16)
    pruned_ref[...] = value_pruned.astype(jnp.bfloat16)
    differ = value_orig - value_pruned
    errors = jnp.mean(differ * differ, axis=1, keepdims=True)
    experts = terms_ref.shape[1]
    dense = dense_weights(ids_ref[...], gates_ref[...], experts)
    terms = factor * jnp.sum(dense * errors, axis=0, keepdims=True)
    terms_ref[...] = jnp.broadcast_to(terms, terms_ref.shape)


def add_kernel(parts_ref, out_ref):
    out_ref[...] = jnp.sum(parts_ref[...], axis=0, keepdims=True)


def on_device(
    states_orig,
    states_pruned,
    ids_orig,
    ids_pruned,
    gates_orig,
    gates_pruned,
    keep_mask,
    w_in,
    w_out,
):
    devices = lax.axis_size("expert")
    section_count = lax.axis_size("section")
    section_index = lax.axis_index("section")
    micro_count, tok_rows, model_width = states_orig.shape
    experts = keep_mask.shape[1]
    top_count = ids_orig.shape[-1]
    loss_factor = experts / (top_count * micro_count * tok_rows * devices)
    extra = -(-2 * experts // LANES) * LANES
    rows = 2 * tok_rows
    chips = devices // SPLIT
    inner = min(4, chips)
    outer = chips // inner
    inner_masks = [SPLIT * i for i in range(1, inner)]
    layer_mask = lambda j: SPLIT * inner * j
    nearer = list(range(1, outer // 2 + 1))
    streams = [[j for j in range(outer) if j not in nearer], nearer]
    own_in, own_out = w_in[0, 0], w_out[0, 0]
    other_out, other_in = exclusive(own_out, 1), exclusive(own_in, 1)
    weights = None

    step_count = micro_count + section_count - 1
    carry = jnp.zeros((2, tok_rows, model_width), jnp.bfloat16)
    moe_orig = jnp.zeros((micro_count, tok_rows, model_width), jnp.bfloat16)
    moe_pruned = moe_orig
    terms = jnp.zeros((devices, experts), jnp.float32)
    for tick in range(step_count):
        if section_count == 1:
            position = tick
            item = lambda buffer: buffer[position]
        else:
            position = jnp.clip(tick - section_index, 0, micro_count - 1)
            active = jnp.logical_and(
                tick - section_index >= 0, tick - section_index < micro_count
            )
            item = lambda buffer: lax.dynamic_index_in_dim(buffer, position, 0, keepdims=False)
        fresh = min(tick, micro_count - 1)
        state_orig, state_pruned = states_orig[fresh], states_pruned[fresh]
        if section_count > 1:
            state_orig = jnp.where(section_index == 0, state_orig, carry[0])
            state_pruned = jnp.where(section_index == 0, state_pruned, carry[1])
        picked_orig, weight_orig = item(ids_orig[0]), item(gates_orig[0])
        operands = [
            state_orig,
            state_pruned,
            picked_orig,
            item(ids_pruned[0]),
            weight_orig,
            item(gates_pruned[0]),
            keep_mask,
        ]
        packed = run_kernel(
            functools.partial(pack_kernel, len(operands)),
            like(rows, model_width + extra),
            [in_hbm(value) for value in operands],
            [pltpu.VMEM(value.shape, value.dtype) for value in operands]
            + [pltpu.SemaphoreType.DMA((len(operands),))],
            space=pl.ANY,
        )
        column = {0: packed}
        for j in streams[1][::-1] + streams[0][1:]:
            column[j] = exclusive(packed, layer_mask(j))
        blocks = []
        for stream, layers in enumerate(streams):
            joined = join_rows([column[j] for j in layers])
            block = [joined]
            for mask in inner_masks:
                block.append(exclusive(joined, mask))
                if stream == 0 and tick == 0:
                    joined = after(joined, other_out if len(block) == 2 else other_in)
            blocks.append(block)
        if weights is None:
            weights = stage_weights(own_in, own_out, other_in, other_out)
        summed = []
        for stream, layers in enumerate(streams):
            partial = run_expert(
                experts, blocks[stream], weights, [len(layers) * rows] * inner
            )
            returned = [partial[0]] + [
                exclusive(part, mask) for part, mask in zip(partial[1:], inner_masks)
            ]
            outs = [like(rows, model_width)] * len(layers)
            if stream == 0:
                outs[0] = like(rows, model_width, jnp.float32)
            sums = run_kernel(functools.partial(plane_kernel, inner), outs, returned)
            for j, value in list(zip(layers, sums))[::-1]:
                summed.append(exclusive(value, layer_mask(j)) if j else value)
        round_orig, round_pruned, tick_terms, *moe = run_kernel(
            functools.partial(final_kernel, outer, loss_factor),
            [like(tok_rows, model_width)] * 2
            + [like(devices, experts, jnp.float32)]
            + [like(rows, model_width, jnp.float32)] * (section_count > 1),
            summed + [picked_orig, weight_orig],
        )
        if section_count > 1:
            tick_terms = jnp.where(active, tick_terms, 0.0)
            round_orig = jnp.where(active, round_orig, item(moe_orig))
            round_pruned = jnp.where(active, round_pruned, item(moe_pruned))
        terms = tick_terms if tick == 0 else terms + tick_terms
        moe_orig = lax.dynamic_update_index_in_dim(moe_orig, round_orig, position, 0)
        moe_pruned = lax.dynamic_update_index_in_dim(moe_pruned, round_pruned, position, 0)
        if tick + 1 < step_count and section_count > 1:
            state = jnp.stack([state_orig, state_pruned]).astype(jnp.float32)
            following = (state + moe[0].reshape(state.shape)).astype(jnp.bfloat16)
            onward = [(i, i + 1) for i in range(section_count - 1)]
            carry = lax.ppermute(following, "section", onward)
    shared = lax.all_to_all(terms, "expert", split_axis=0, concat_axis=0, tiled=True)
    loss = run_kernel(add_kernel, like(1, experts, jnp.float32), [shared])
    return (moe_orig[None], moe_pruned[None], loss)


def solution(mesh):
    return jax.shard_map(
        on_device,
        mesh=mesh,
        in_specs=(
            P(None, "expert", None),
            P(None, "expert", None),
            P("section", None, "expert", None),
            P("section", None, "expert", None),
            P("section", None, "expert", None),
            P("section", None, "expert", None),
            P("section", None),
            P("section", "expert", None, None),
            P("section", "expert", None, None),
        ),
        out_specs=(
            P("section", None, "expert", None),
            P("section", None, "expert", None),
            P("section", None),
        ),
        check_vma=False,
    )
```

```python
import functools

import jax
import jax.numpy as jnp
from jax import lax
from jax.experimental import pallas as pl
from jax.experimental.pallas import tpu as pltpu
from jax.sharding import PartitionSpec as P

SPLIT = 2
LANES = 128
MIB = 2**20


def run_kernel(body, outs, operands, scratch=(), limit=16, space=pltpu.VMEM):
    return pl.pallas_call(
        body,
        out_shape=outs,
        in_specs=[pl.BlockSpec(memory_space=space)] * len(operands),
        out_specs=jax.tree.map(lambda _: pl.BlockSpec(memory_space=pltpu.VMEM), outs),
        scratch_shapes=list(scratch),
        compiler_params=pltpu.CompilerParams(vmem_limit_bytes=limit * MIB),
    )(*operands)


def in_hbm(value):
    return pltpu.with_memory_space_constraint(value, pltpu.HBM)


def like(rows, columns, dtype=jnp.bfloat16):
    return jax.ShapeDtypeStruct((rows, columns), dtype)


def exclusive(value, mask):
    pairs = [(source, source ^ mask) for source in range(lax.axis_size("expert"))]
    return lax.ppermute(value, "expert", pairs)


def normalize_rows(values):
    factor = lax.rsqrt(jnp.mean(values * values, axis=-1, keepdims=True) + 1e-06)
    return values * factor


def dense_weights(picked, gates, experts):
    rows = picked.shape[0]
    label = lax.broadcasted_iota(jnp.int32, (rows, experts), 1)
    total = jnp.zeros((rows, experts), jnp.float32)
    for k in range(picked.shape[1]):
        total = total + jnp.where(picked[:, k : k + 1] == label, gates[:, k : k + 1], 0.0)
    return total


def pack_kernel(count, *refs):
    sources, out_ref, scratch = refs[:count], refs[count], refs[count + 1 :]
    held, sems = scratch[:count], scratch[count]
    copies = [
        pltpu.make_async_copy(source, target, sems.at[place])
        for place, (source, target) in enumerate(zip(sources, held))
    ]
    for copy in copies:
        copy.start()
    for copy in copies:
        copy.wait()
    so_ref, sp_ref, io_ref, ip_ref, go_ref, gp_ref, keep_ref = held
    model_width = so_ref.shape[1]
    extra = out_ref.shape[1] - model_width
    experts = keep_ref.shape[1]
    states = jnp.concatenate(
        [so_ref[...].astype(jnp.float32), sp_ref[...].astype(jnp.float32)], axis=0
    )
    out_ref[:, :model_width] = normalize_rows(states).astype(jnp.bfloat16)
    dense_orig = dense_weights(io_ref[...], go_ref[...], experts)
    dense_pruned = dense_weights(ip_ref[...], gp_ref[...], experts)
    dense_pruned = dense_pruned * keep_ref[...].astype(jnp.float32)
    dense = jnp.concatenate([dense_orig, dense_pruned], axis=0)
    high = dense.astype(jnp.bfloat16)
    low = (dense - high.astype(jnp.float32)).astype(jnp.bfloat16)
    source = lax.broadcasted_iota(jnp.int32, (experts, extra), 0)
    lane = lax.broadcasted_iota(jnp.int32, (experts, extra), 1)
    out_ref[:, model_width:] = (
        jnp.dot(
            high,
            (lane == source).astype(jnp.float32).astype(jnp.bfloat16),
            preferred_element_type=jnp.float32,
        )
        + jnp.dot(
            low,
            (lane == source + experts).astype(jnp.float32).astype(jnp.bfloat16),
            preferred_element_type=jnp.float32,
        )
    ).astype(jnp.bfloat16)


def stage_kernel(count, *refs):
    sources, targets, sems = refs[:count], refs[count : 2 * count], refs[2 * count]
    copies = [
        pltpu.make_async_copy(source, target, sems.at[place])
        for place, (source, target) in enumerate(zip(sources, targets))
    ]
    for copy in copies:
        copy.start()
    for copy in copies:
        copy.wait()


def stage(arrays):
    return run_kernel(
        functools.partial(stage_kernel, len(arrays)),
        [pltpu.VMEM(value.shape, value.dtype) for value in arrays],
        arrays,
        [pltpu.SemaphoreType.DMA((len(arrays),))],
        space=pl.ANY,
    )


def after(value, *awaited):
    return lax.optimization_barrier((value, awaited))[0]


def join_kernel(*refs):
    part_refs, out_ref = refs[:-1], refs[-1]
    rows = part_refs[0].shape[0]
    for place, part_ref in enumerate(part_refs):
        out_ref[place * rows : (place + 1) * rows, :] = part_ref[...]


def join_rows(parts):
    rows, columns = parts[0].shape
    return run_kernel(join_kernel, like(len(parts) * rows, columns), parts)


def expert_kernel(experts, row_count, sizes, *refs):
    row_refs, refs = refs[:row_count], refs[row_count:]
    in_refs, out_refs, refs = refs[:SPLIT], refs[SPLIT : 2 * SPLIT], refs[2 * SPLIT :]
    result_refs, (rows, hidden) = refs[: len(sizes)], refs[len(sizes) :]
    half, model_width = out_refs[0].shape
    expert = lax.axis_index("expert") // SPLIT
    weights = []
    filled = 0
    for row_ref in row_refs:
        size = row_ref.shape[0]
        rows[filled : filled + size, :] = row_ref[:, :model_width]
        filled += size
        extra = row_ref[:, model_width:].astype(jnp.float32)
        lane = lax.broadcasted_iota(jnp.int32, extra.shape, 1)
        mine = jnp.logical_or(lane == expert, lane == expert + experts)
        weights.append(jnp.sum(jnp.where(mine, extra, 0.0), axis=1, keepdims=True))
    weight = jnp.concatenate(weights, axis=0)
    for place, in_ref in enumerate(in_refs):
        both = jnp.dot(rows[...], in_ref[...], preferred_element_type=jnp.float32)
        gate, up = both[:, :half], both[:, half:]
        hidden[:, place * half : (place + 1) * half] = (
            gate / (1.0 + jnp.exp(-gate)) * up
        ).astype(jnp.bfloat16)
    step = min(512, model_width)
    for start in range(0, model_width, step):
        value = sum(
            jnp.dot(
                hidden[:, place * half : (place + 1) * half],
                out_ref[:, start : start + step],
                preferred_element_type=jnp.float32,
            )
            for place, out_ref in enumerate(out_refs)
        )
        value = (value * weight).astype(jnp.bfloat16)
        filled = 0
        for size, result_ref in zip(sizes, result_refs):
            result_ref[:, start : start + step] = value[filled : filled + size]
            filled += size


def run_expert(experts, row_arrays, weights, sizes):
    total = sum(array.shape[0] for array in row_arrays)
    half, model_width = weights[-1].shape
    return run_kernel(
        functools.partial(expert_kernel, experts, len(row_arrays), sizes),
        [like(size, model_width) for size in sizes],
        list(row_arrays) + list(weights),
        [
            pltpu.VMEM((total, model_width), jnp.bfloat16),
            pltpu.VMEM((total, SPLIT * half), jnp.bfloat16),
        ],
        limit=24,
    )


def add_parts_kernel(kept_ref, came_ref, *out_refs):
    filled = 0
    for out_ref in out_refs:
        rows = slice(filled, filled + out_ref.shape[0])
        filled += out_ref.shape[0]
        total = kept_ref[rows, :].astype(jnp.float32) + came_ref[rows, :].astype(jnp.float32)
        out_ref[...] = total.astype(out_ref.dtype)


def final_kernel(parts, factor, *refs):
    part_refs, refs = refs[:parts], refs[parts:]
    ids_ref, gates_ref, orig_ref, pruned_ref, terms_ref, *value_refs = refs
    tok_rows = orig_ref.shape[0]
    total = sum(ref[...].astype(jnp.float32) for ref in part_refs)
    for value_ref in value_refs:
        value_ref[...] = total
    value_orig, value_pruned = total[:tok_rows], total[tok_rows:]
    orig_ref[...] = value_orig.astype(jnp.bfloat16)
    pruned_ref[...] = value_pruned.astype(jnp.bfloat16)
    differ = value_orig - value_pruned
    errors = jnp.mean(differ * differ, axis=1, keepdims=True)
    experts = terms_ref.shape[1]
    dense = dense_weights(ids_ref[...], gates_ref[...], experts)
    terms = factor * jnp.sum(dense * errors, axis=0, keepdims=True)
    terms_ref[...] = jnp.broadcast_to(terms, terms_ref.shape)


def add_kernel(parts_ref, out_ref):
    out_ref[...] = jnp.sum(parts_ref[...], axis=0, keepdims=True)


def on_device(
    states_orig,
    states_pruned,
    ids_orig,
    ids_pruned,
    gates_orig,
    gates_pruned,
    keep_mask,
    w_in,
    w_out,
):
    devices = lax.axis_size("expert")
    section_count = lax.axis_size("section")
    section_index = lax.axis_index("section")
    micro_count, tok_rows, model_width = states_orig.shape
    experts = keep_mask.shape[1]
    top_count = ids_orig.shape[-1]
    loss_factor = experts / (top_count * micro_count * tok_rows * devices)
    extra = -(-2 * experts // LANES) * LANES
    rows = 2 * tok_rows
    chips = devices // SPLIT
    inner = 4
    outer = chips // inner
    plane_masks = [SPLIT, 2 * SPLIT]
    layer_mask = lambda j: SPLIT * inner * j
    nearer = list(range(1, outer // 2 + 1))
    streams = [[j for j in range(outer) if j not in nearer], nearer]
    own_in, own_out = w_in[0, 0], w_out[0, 0]
    other_out, other_in = exclusive(own_out, 1), exclusive(own_in, 1)

    step_count = micro_count + section_count - 1
    carry = jnp.zeros((2, tok_rows, model_width), jnp.bfloat16)
    moe_orig = jnp.zeros((micro_count, tok_rows, model_width), jnp.bfloat16)
    moe_pruned = moe_orig
    terms = jnp.zeros((devices, experts), jnp.float32)
    for tick in range(step_count):
        if section_count == 1:
            position = tick
            item = lambda buffer: buffer[position]
        else:
            position = jnp.clip(tick - section_index, 0, micro_count - 1)
            active = jnp.logical_and(
                tick - section_index >= 0, tick - section_index < micro_count
            )
            item = lambda buffer: lax.dynamic_index_in_dim(buffer, position, 0, keepdims=False)
        fresh = min(tick, micro_count - 1)
        state_orig, state_pruned = states_orig[fresh], states_pruned[fresh]
        if section_count > 1:
            state_orig = jnp.where(section_index == 0, state_orig, carry[0])
            state_pruned = jnp.where(section_index == 0, state_pruned, carry[1])
        picked_orig, weight_orig = item(ids_orig[0]), item(gates_orig[0])
        operands = [
            state_orig,
            state_pruned,
            picked_orig,
            item(ids_pruned[0]),
            weight_orig,
            item(gates_pruned[0]),
            keep_mask,
        ]
        packed = run_kernel(
            functools.partial(pack_kernel, len(operands)),
            like(rows, model_width + extra),
            [in_hbm(value) for value in operands],
            [pltpu.VMEM(value.shape, value.dtype) for value in operands]
            + [pltpu.SemaphoreType.DMA((len(operands),))],
            space=pl.ANY,
        )
        column = {0: packed}
        for j in streams[1][::-1] + streams[0][1:]:
            column[j] = exclusive(packed, layer_mask(j))
        if tick == 0:
            own = stage([in_hbm(own_in), in_hbm(own_out)])
            other = stage([other_in, other_out])
            weights = [own[0], other[0], own[1], other[1]]
            column[nearer[0]] = after(column[nearer[0]], own)
        blocks = []
        for layers, masks in zip(streams, (plane_masks, plane_masks[::-1])):
            joined = join_rows([column[j] for j in layers])
            both = join_rows([joined, exclusive(joined, masks[0])])
            blocks.append([both, exclusive(both, masks[1])])
        summed = []
        for block, layers, masks in zip(blocks, streams, (plane_masks, plane_masks[::-1])):
            half = block[0].shape[0] // 2
            kept, sent = run_expert(experts, block, weights, [2 * half] * 2)
            kept, sent = run_kernel(
                add_parts_kernel,
                [like(half, model_width, jnp.float32), like(half, model_width)],
                [kept, exclusive(sent, masks[1])],
            )
            outs = [like(rows, model_width, jnp.bfloat16 if j else jnp.float32) for j in layers]
            sums = run_kernel(add_parts_kernel, outs, [kept, exclusive(sent, masks[0])])
            for j, value in list(zip(layers, sums))[::-1]:
                summed.append(exclusive(value, layer_mask(j)) if j else value)
        round_orig, round_pruned, tick_terms, *moe = run_kernel(
            functools.partial(final_kernel, outer, loss_factor),
            [like(tok_rows, model_width)] * 2
            + [like(devices, experts, jnp.float32)]
            + [like(rows, model_width, jnp.float32)] * (section_count > 1),
            summed + [picked_orig, weight_orig],
        )
        if section_count > 1:
            tick_terms = jnp.where(active, tick_terms, 0.0)
            round_orig = jnp.where(active, round_orig, item(moe_orig))
            round_pruned = jnp.where(active, round_pruned, item(moe_pruned))
        terms = tick_terms if tick == 0 else terms + tick_terms
        moe_orig = lax.dynamic_update_index_in_dim(moe_orig, round_orig, position, 0)
        moe_pruned = lax.dynamic_update_index_in_dim(moe_pruned, round_pruned, position, 0)
        if tick + 1 < step_count and section_count > 1:
            state = jnp.stack([state_orig, state_pruned]).astype(jnp.float32)
            following = (state + moe[0].reshape(state.shape)).astype(jnp.bfloat16)
            onward = [(i, i + 1) for i in range(section_count - 1)]
            carry = lax.ppermute(following, "section", onward)
    shared = lax.all_to_all(terms, "expert", split_axis=0, concat_axis=0, tiled=True)
    loss = run_kernel(add_kernel, like(1, experts, jnp.float32), [shared])
    return (moe_orig[None], moe_pruned[None], loss)


def solution(mesh):
    return jax.shard_map(
        on_device,
        mesh=mesh,
        in_specs=(
            P(None, "expert", None),
            P(None, "expert", None),
            P("section", None, "expert", None),
            P("section", None, "expert", None),
            P("section", None, "expert", None),
            P("section", None, "expert", None),
            P("section", None),
            P("section", "expert", None, None),
            P("section", "expert", None, None),
        ),
        out_specs=(
            P("section", None, "expert", None),
            P("section", None, "expert", None),
            P("section", None),
        ),
        check_vma=False,
    )
```

```python
import functools

import jax
import jax.numpy as jnp
from jax import lax
from jax.experimental import pallas as pl
from jax.experimental.pallas import tpu as pltpu
from jax.sharding import PartitionSpec as P

SPLIT = 2
LANES = 128
MIB = 2**20


def run_kernel(body, outs, operands, scratch=(), limit=16, space=pltpu.VMEM):
    return pl.pallas_call(
        body,
        out_shape=outs,
        in_specs=[pl.BlockSpec(memory_space=space)] * len(operands),
        out_specs=jax.tree.map(lambda _: pl.BlockSpec(memory_space=pltpu.VMEM), outs),
        scratch_shapes=list(scratch),
        compiler_params=pltpu.CompilerParams(vmem_limit_bytes=limit * MIB),
    )(*operands)


def in_hbm(value):
    return pltpu.with_memory_space_constraint(value, pltpu.HBM)


def like(rows, columns, dtype=jnp.bfloat16):
    return jax.ShapeDtypeStruct((rows, columns), dtype)


def exclusive(value, mask):
    pairs = [(source, source ^ mask) for source in range(lax.axis_size("expert"))]
    return lax.ppermute(value, "expert", pairs)


def normalize_rows(values):
    factor = lax.rsqrt(jnp.mean(values * values, axis=-1, keepdims=True) + 1e-06)
    return values * factor


def dense_weights(picked, gates, experts):
    rows = picked.shape[0]
    label = lax.broadcasted_iota(jnp.int32, (rows, experts), 1)
    total = jnp.zeros((rows, experts), jnp.float32)
    for k in range(picked.shape[1]):
        total = total + jnp.where(picked[:, k : k + 1] == label, gates[:, k : k + 1], 0.0)
    return total


def pack_kernel(count, *refs):
    sources, out_ref, scratch = refs[:count], refs[count], refs[count + 1 :]
    held, sems = scratch[:count], scratch[count]
    copies = [
        pltpu.make_async_copy(source, target, sems.at[place])
        for place, (source, target) in enumerate(zip(sources, held))
    ]
    for copy in copies:
        copy.start()
    for copy in copies:
        copy.wait()
    so_ref, sp_ref, io_ref, ip_ref, go_ref, gp_ref, keep_ref = held
    model_width = so_ref.shape[1]
    extra = out_ref.shape[1] - model_width
    experts = keep_ref.shape[1]
    states = jnp.concatenate(
        [so_ref[...].astype(jnp.float32), sp_ref[...].astype(jnp.float32)], axis=0
    )
    out_ref[:, :model_width] = normalize_rows(states).astype(jnp.bfloat16)
    dense_orig = dense_weights(io_ref[...], go_ref[...], experts)
    dense_pruned = dense_weights(ip_ref[...], gp_ref[...], experts)
    dense_pruned = dense_pruned * keep_ref[...].astype(jnp.float32)
    dense = jnp.concatenate([dense_orig, dense_pruned], axis=0)
    high = dense.astype(jnp.bfloat16)
    low = (dense - high.astype(jnp.float32)).astype(jnp.bfloat16)
    source = lax.broadcasted_iota(jnp.int32, (experts, extra), 0)
    lane = lax.broadcasted_iota(jnp.int32, (experts, extra), 1)
    out_ref[:, model_width:] = (
        jnp.dot(
            high,
            (lane == source).astype(jnp.float32).astype(jnp.bfloat16),
            preferred_element_type=jnp.float32,
        )
        + jnp.dot(
            low,
            (lane == source + experts).astype(jnp.float32).astype(jnp.bfloat16),
            preferred_element_type=jnp.float32,
        )
    ).astype(jnp.bfloat16)


def stage_kernel(count, *refs):
    sources, targets, sems = refs[:count], refs[count : 2 * count], refs[2 * count]
    copies = [
        pltpu.make_async_copy(source, target, sems.at[place])
        for place, (source, target) in enumerate(zip(sources, targets))
    ]
    for copy in copies:
        copy.start()
    for copy in copies:
        copy.wait()


def stage_weights(own_in, own_out, other_in, other_out):
    weights = [in_hbm(own_in), other_in, in_hbm(own_out), other_out]
    return run_kernel(
        functools.partial(stage_kernel, len(weights)),
        [pltpu.VMEM(value.shape, value.dtype) for value in weights],
        weights,
        [pltpu.SemaphoreType.DMA((len(weights),))],
        space=pl.ANY,
    )


def after(value, *awaited):
    return lax.optimization_barrier((value, awaited))[0]


def join_kernel(*refs):
    part_refs, out_ref = refs[:-1], refs[-1]
    rows = part_refs[0].shape[0]
    for place, part_ref in enumerate(part_refs):
        out_ref[place * rows : (place + 1) * rows, :] = part_ref[...]


def join_rows(parts):
    rows, columns = parts[0].shape
    return run_kernel(join_kernel, like(len(parts) * rows, columns), parts)


def expert_kernel(experts, row_count, sizes, *refs):
    row_refs, refs = refs[:row_count], refs[row_count:]
    in_refs, out_refs, refs = refs[:SPLIT], refs[SPLIT : 2 * SPLIT], refs[2 * SPLIT :]
    result_refs, (rows, hidden) = refs[: len(sizes)], refs[len(sizes) :]
    half, model_width = out_refs[0].shape
    expert = lax.axis_index("expert") // SPLIT
    weights = []
    filled = 0
    for row_ref in row_refs:
        size = row_ref.shape[0]
        rows[filled : filled + size, :] = row_ref[:, :model_width]
        filled += size
        extra = row_ref[:, model_width:].astype(jnp.float32)
        lane = lax.broadcasted_iota(jnp.int32, extra.shape, 1)
        mine = jnp.logical_or(lane == expert, lane == expert + experts)
        weights.append(jnp.sum(jnp.where(mine, extra, 0.0), axis=1, keepdims=True))
    weight = jnp.concatenate(weights, axis=0)
    for place, in_ref in enumerate(in_refs):
        both = jnp.dot(rows[...], in_ref[...], preferred_element_type=jnp.float32)
        gate, up = both[:, :half], both[:, half:]
        hidden[:, place * half : (place + 1) * half] = (
            gate / (1.0 + jnp.exp(-gate)) * up
        ).astype(jnp.bfloat16)
    step = min(512, model_width)
    for start in range(0, model_width, step):
        value = sum(
            jnp.dot(
                hidden[:, place * half : (place + 1) * half],
                out_ref[:, start : start + step],
                preferred_element_type=jnp.float32,
            )
            for place, out_ref in enumerate(out_refs)
        )
        value = (value * weight).astype(jnp.bfloat16)
        filled = 0
        for size, result_ref in zip(sizes, result_refs):
            result_ref[:, start : start + step] = value[filled : filled + size]
            filled += size


def run_expert(experts, row_arrays, weights, sizes):
    total = sum(array.shape[0] for array in row_arrays)
    half, model_width = weights[-1].shape
    return run_kernel(
        functools.partial(expert_kernel, experts, len(row_arrays), sizes),
        [like(size, model_width) for size in sizes],
        list(row_arrays) + list(weights),
        [
            pltpu.VMEM((total, model_width), jnp.bfloat16),
            pltpu.VMEM((total, SPLIT * half), jnp.bfloat16),
        ],
        limit=24,
    )


def plane_kernel(count, *refs):
    part_refs, out_refs = refs[:count], refs[count:]
    rows = out_refs[0].shape[0]
    for place, out_ref in enumerate(out_refs):
        out_ref[...] = sum(
            ref[place * rows : (place + 1) * rows, :].astype(jnp.float32) for ref in part_refs
        ).astype(out_ref.dtype)


def final_kernel(parts, factor, *refs):
    part_refs, refs = refs[:parts], refs[parts:]
    ids_ref, gates_ref, orig_ref, pruned_ref, terms_ref, *value_refs = refs
    tok_rows = orig_ref.shape[0]
    total = sum(ref[...].astype(jnp.float32) for ref in part_refs)
    for value_ref in value_refs:
        value_ref[...] = total
    value_orig, value_pruned = total[:tok_rows], total[tok_rows:]
    orig_ref[...] = value_orig.astype(jnp.bfloat16)
    pruned_ref[...] = value_pruned.astype(jnp.bfloat16)
    differ = value_orig - value_pruned
    errors = jnp.mean(differ * differ, axis=1, keepdims=True)
    experts = terms_ref.shape[1]
    dense = dense_weights(ids_ref[...], gates_ref[...], experts)
    terms = factor * jnp.sum(dense * errors, axis=0, keepdims=True)
    terms_ref[...] = jnp.broadcast_to(terms, terms_ref.shape)


def add_kernel(parts_ref, out_ref):
    out_ref[...] = jnp.sum(parts_ref[...], axis=0, keepdims=True)


def on_device(
    states_orig,
    states_pruned,
    ids_orig,
    ids_pruned,
    gates_orig,
    gates_pruned,
    keep_mask,
    w_in,
    w_out,
):
    devices = lax.axis_size("expert")
    section_count = lax.axis_size("section")
    section_index = lax.axis_index("section")
    micro_count, tok_rows, model_width = states_orig.shape
    experts = keep_mask.shape[1]
    top_count = ids_orig.shape[-1]
    loss_factor = experts / (top_count * micro_count * tok_rows * devices)
    extra = -(-2 * experts // LANES) * LANES
    rows = 2 * tok_rows
    chips = devices // SPLIT
    inner = min(4, chips)
    outer = chips // inner
    inner_masks = [SPLIT * i for i in range(1, inner)]
    layer_mask = lambda j: SPLIT * inner * j
    streams = [list(range(outer // 2)), list(range(outer // 2, outer))]
    own_in, own_out = w_in[0, 0], w_out[0, 0]
    other_out, other_in = exclusive(own_out, 1), exclusive(own_in, 1)
    weights = None

    step_count = micro_count + section_count - 1
    carry = jnp.zeros((2, tok_rows, model_width), jnp.bfloat16)
    moe_orig = jnp.zeros((micro_count, tok_rows, model_width), jnp.bfloat16)
    moe_pruned = moe_orig
    terms = jnp.zeros((devices, experts), jnp.float32)
    for tick in range(step_count):
        if section_count == 1:
            position = tick
            item = lambda buffer: buffer[position]
        else:
            position = jnp.clip(tick - section_index, 0, micro_count - 1)
            active = jnp.logical_and(
                tick - section_index >= 0, tick - section_index < micro_count
            )
            item = lambda buffer: lax.dynamic_index_in_dim(buffer, position, 0, keepdims=False)
        fresh = min(tick, micro_count - 1)
        state_orig, state_pruned = states_orig[fresh], states_pruned[fresh]
        if section_count > 1:
            state_orig = jnp.where(section_index == 0, state_orig, carry[0])
            state_pruned = jnp.where(section_index == 0, state_pruned, carry[1])
        picked_orig, weight_orig = item(ids_orig[0]), item(gates_orig[0])
        operands = [
            state_orig,
            state_pruned,
            picked_orig,
            item(ids_pruned[0]),
            weight_orig,
            item(gates_pruned[0]),
            keep_mask,
        ]
        packed = run_kernel(
            functools.partial(pack_kernel, len(operands)),
            like(rows, model_width + extra),
            [in_hbm(value) for value in operands],
            [pltpu.VMEM(value.shape, value.dtype) for value in operands]
            + [pltpu.SemaphoreType.DMA((len(operands),))],
            space=pl.ANY,
        )
        column = {0: packed}
        for j in streams[0][1:] + streams[1][::-1]:
            column[j] = exclusive(packed, layer_mask(j))
        blocks = []
        for stream, layers in enumerate(streams):
            joined = join_rows([column[j] for j in layers])
            if stream == 1:
                joined = after(joined, blocks[0][1])
            block = [joined]
            for mask in inner_masks:
                block.append(exclusive(joined, mask))
            blocks.append(block)
        if weights is None:
            weights = stage_weights(own_in, own_out, other_in, other_out)
        summed = []
        for stream, layers in enumerate(streams):
            partial = run_expert(
                experts, blocks[stream], weights, [len(layers) * rows] * inner
            )
            returned = [partial[0]] + [
                exclusive(part, mask) for part, mask in zip(partial[1:], inner_masks)
            ]
            outs = [like(rows, model_width)] * len(layers)
            if stream == 0:
                outs[0] = like(rows, model_width, jnp.float32)
            sums = run_kernel(functools.partial(plane_kernel, inner), outs, returned)
            for j, value in list(zip(layers, sums))[::-1]:
                summed.append(exclusive(value, layer_mask(j)) if j else value)
        round_orig, round_pruned, tick_terms, *moe = run_kernel(
            functools.partial(final_kernel, outer, loss_factor),
            [like(tok_rows, model_width)] * 2
            + [like(devices, experts, jnp.float32)]
            + [like(rows, model_width, jnp.float32)] * (section_count > 1),
            summed + [picked_orig, weight_orig],
        )
        if section_count > 1:
            tick_terms = jnp.where(active, tick_terms, 0.0)
            round_orig = jnp.where(active, round_orig, item(moe_orig))
            round_pruned = jnp.where(active, round_pruned, item(moe_pruned))
        terms = tick_terms if tick == 0 else terms + tick_terms
        moe_orig = lax.dynamic_update_index_in_dim(moe_orig, round_orig, position, 0)
        moe_pruned = lax.dynamic_update_index_in_dim(moe_pruned, round_pruned, position, 0)
        if tick + 1 < step_count and section_count > 1:
            state = jnp.stack([state_orig, state_pruned]).astype(jnp.float32)
            following = (state + moe[0].reshape(state.shape)).astype(jnp.bfloat16)
            onward = [(i, i + 1) for i in range(section_count - 1)]
            carry = lax.ppermute(following, "section", onward)
    shared = lax.all_to_all(terms, "expert", split_axis=0, concat_axis=0, tiled=True)
    loss = run_kernel(add_kernel, like(1, experts, jnp.float32), [shared])
    return (moe_orig[None], moe_pruned[None], loss)


def solution(mesh):
    return jax.shard_map(
        on_device,
        mesh=mesh,
        in_specs=(
            P(None, "expert", None),
            P(None, "expert", None),
            P("section", None, "expert", None),
            P("section", None, "expert", None),
            P("section", None, "expert", None),
            P("section", None, "expert", None),
            P("section", None),
            P("section", "expert", None, None),
            P("section", "expert", None, None),
        ),
        out_specs=(
            P("section", None, "expert", None),
            P("section", None, "expert", None),
            P("section", None),
        ),
        check_vma=False,
    )
```

```python
import functools

import jax
import jax.numpy as jnp
from jax import lax
from jax.experimental import pallas as pl
from jax.experimental.pallas import tpu as pltpu
from jax.sharding import PartitionSpec as P

SPLIT = 2
LANES = 128
MIB = 2**20


def run_kernel(body, outs, operands, scratch=(), limit=16, space=pltpu.VMEM):
    return pl.pallas_call(
        body,
        out_shape=outs,
        in_specs=[pl.BlockSpec(memory_space=space)] * len(operands),
        out_specs=jax.tree.map(lambda _: pl.BlockSpec(memory_space=pltpu.VMEM), outs),
        scratch_shapes=list(scratch),
        compiler_params=pltpu.CompilerParams(vmem_limit_bytes=limit * MIB),
    )(*operands)


def in_hbm(value):
    return pltpu.with_memory_space_constraint(value, pltpu.HBM)


def like(rows, columns, dtype=jnp.bfloat16):
    return jax.ShapeDtypeStruct((rows, columns), dtype)


def exclusive(value, mask):
    pairs = [(source, source ^ mask) for source in range(lax.axis_size("expert"))]
    return lax.ppermute(value, "expert", pairs)


def normalize_rows(values):
    factor = lax.rsqrt(jnp.mean(values * values, axis=-1, keepdims=True) + 1e-06)
    return values * factor


def dense_weights(picked, gates, experts):
    rows = picked.shape[0]
    label = lax.broadcasted_iota(jnp.int32, (rows, experts), 1)
    total = jnp.zeros((rows, experts), jnp.float32)
    for k in range(picked.shape[1]):
        total = total + jnp.where(picked[:, k : k + 1] == label, gates[:, k : k + 1], 0.0)
    return total


def pack_kernel(count, *refs):
    sources, out_ref, scratch = refs[:count], refs[count], refs[count + 1 :]
    held, sems = scratch[:count], scratch[count]
    copies = [
        pltpu.make_async_copy(source, target, sems.at[place])
        for place, (source, target) in enumerate(zip(sources, held))
    ]
    for copy in copies:
        copy.start()
    for copy in copies:
        copy.wait()
    so_ref, sp_ref, io_ref, ip_ref, go_ref, gp_ref, keep_ref = held
    model_width = so_ref.shape[1]
    extra = out_ref.shape[1] - model_width
    experts = keep_ref.shape[1]
    states = jnp.concatenate(
        [so_ref[...].astype(jnp.float32), sp_ref[...].astype(jnp.float32)], axis=0
    )
    out_ref[:, :model_width] = normalize_rows(states).astype(jnp.bfloat16)
    dense_orig = dense_weights(io_ref[...], go_ref[...], experts)
    dense_pruned = dense_weights(ip_ref[...], gp_ref[...], experts)
    dense_pruned = dense_pruned * keep_ref[...].astype(jnp.float32)
    dense = jnp.concatenate([dense_orig, dense_pruned], axis=0)
    high = dense.astype(jnp.bfloat16)
    low = (dense - high.astype(jnp.float32)).astype(jnp.bfloat16)
    source = lax.broadcasted_iota(jnp.int32, (experts, extra), 0)
    lane = lax.broadcasted_iota(jnp.int32, (experts, extra), 1)
    out_ref[:, model_width:] = (
        jnp.dot(
            high,
            (lane == source).astype(jnp.float32).astype(jnp.bfloat16),
            preferred_element_type=jnp.float32,
        )
        + jnp.dot(
            low,
            (lane == source + experts).astype(jnp.float32).astype(jnp.bfloat16),
            preferred_element_type=jnp.float32,
        )
    ).astype(jnp.bfloat16)


def stage_kernel(count, *refs):
    sources, targets, sems = refs[:count], refs[count : 2 * count], refs[2 * count]
    copies = [
        pltpu.make_async_copy(source, target, sems.at[place])
        for place, (source, target) in enumerate(zip(sources, targets))
    ]
    for copy in copies:
        copy.start()
    for copy in copies:
        copy.wait()


def stage(arrays):
    return run_kernel(
        functools.partial(stage_kernel, len(arrays)),
        [pltpu.VMEM(value.shape, value.dtype) for value in arrays],
        arrays,
        [pltpu.SemaphoreType.DMA((len(arrays),))],
        space=pl.ANY,
    )


def after(value, *awaited):
    return lax.optimization_barrier((value, awaited))[0]


def join_kernel(*refs):
    part_refs, out_ref = refs[:-1], refs[-1]
    rows = part_refs[0].shape[0]
    for place, part_ref in enumerate(part_refs):
        out_ref[place * rows : (place + 1) * rows, :] = part_ref[...]


def join_rows(parts):
    rows, columns = parts[0].shape
    return run_kernel(join_kernel, like(len(parts) * rows, columns), parts)


def expert_kernel(experts, row_count, sizes, *refs):
    row_refs, refs = refs[:row_count], refs[row_count:]
    in_refs, out_refs, refs = refs[:SPLIT], refs[SPLIT : 2 * SPLIT], refs[2 * SPLIT :]
    result_refs, (rows, hidden) = refs[: len(sizes)], refs[len(sizes) :]
    half, model_width = out_refs[0].shape
    expert = lax.axis_index("expert") // SPLIT
    weights = []
    filled = 0
    for row_ref in row_refs:
        size = row_ref.shape[0]
        rows[filled : filled + size, :] = row_ref[:, :model_width]
        filled += size
        extra = row_ref[:, model_width:].astype(jnp.float32)
        lane = lax.broadcasted_iota(jnp.int32, extra.shape, 1)
        mine = jnp.logical_or(lane == expert, lane == expert + experts)
        weights.append(jnp.sum(jnp.where(mine, extra, 0.0), axis=1, keepdims=True))
    weight = jnp.concatenate(weights, axis=0)
    for place, in_ref in enumerate(in_refs):
        both = jnp.dot(rows[...], in_ref[...], preferred_element_type=jnp.float32)
        gate, up = both[:, :half], both[:, half:]
        hidden[:, place * half : (place + 1) * half] = (
            gate / (1.0 + jnp.exp(-gate)) * up
        ).astype(jnp.bfloat16)
    step = min(512, model_width)
    for start in range(0, model_width, step):
        value = sum(
            jnp.dot(
                hidden[:, place * half : (place + 1) * half],
                out_ref[:, start : start + step],
                preferred_element_type=jnp.float32,
            )
            for place, out_ref in enumerate(out_refs)
        )
        value = (value * weight).astype(jnp.bfloat16)
        filled = 0
        for size, result_ref in zip(sizes, result_refs):
            result_ref[:, start : start + step] = value[filled : filled + size]
            filled += size


def run_expert(experts, row_arrays, weights, sizes):
    total = sum(array.shape[0] for array in row_arrays)
    half, model_width = weights[-1].shape
    return run_kernel(
        functools.partial(expert_kernel, experts, len(row_arrays), sizes),
        [like(size, model_width) for size in sizes],
        list(row_arrays) + list(weights),
        [
            pltpu.VMEM((total, model_width), jnp.bfloat16),
            pltpu.VMEM((total, SPLIT * half), jnp.bfloat16),
        ],
        limit=24,
    )


def plane_kernel(count, *refs):
    part_refs, out_refs = refs[:count], refs[count:]
    rows = out_refs[0].shape[0]
    for place, out_ref in enumerate(out_refs):
        out_ref[...] = sum(
            ref[place * rows : (place + 1) * rows, :].astype(jnp.float32) for ref in part_refs
        ).astype(out_ref.dtype)


def final_kernel(parts, factor, *refs):
    part_refs, refs = refs[:parts], refs[parts:]
    ids_ref, gates_ref, orig_ref, pruned_ref, terms_ref, *value_refs = refs
    tok_rows = orig_ref.shape[0]
    total = sum(ref[...].astype(jnp.float32) for ref in part_refs)
    for value_ref in value_refs:
        value_ref[...] = total
    value_orig, value_pruned = total[:tok_rows], total[tok_rows:]
    orig_ref[...] = value_orig.astype(jnp.bfloat16)
    pruned_ref[...] = value_pruned.astype(jnp.bfloat16)
    differ = value_orig - value_pruned
    errors = jnp.mean(differ * differ, axis=1, keepdims=True)
    experts = terms_ref.shape[1]
    dense = dense_weights(ids_ref[...], gates_ref[...], experts)
    terms = factor * jnp.sum(dense * errors, axis=0, keepdims=True)
    terms_ref[...] = jnp.broadcast_to(terms, terms_ref.shape)


def add_kernel(parts_ref, out_ref):
    out_ref[...] = jnp.sum(parts_ref[...], axis=0, keepdims=True)


def on_device(
    states_orig,
    states_pruned,
    ids_orig,
    ids_pruned,
    gates_orig,
    gates_pruned,
    keep_mask,
    w_in,
    w_out,
):
    devices = lax.axis_size("expert")
    section_count = lax.axis_size("section")
    section_index = lax.axis_index("section")
    micro_count, tok_rows, model_width = states_orig.shape
    experts = keep_mask.shape[1]
    top_count = ids_orig.shape[-1]
    loss_factor = experts / (top_count * micro_count * tok_rows * devices)
    extra = -(-2 * experts // LANES) * LANES
    rows = 2 * tok_rows
    chips = devices // SPLIT
    inner = min(4, chips)
    outer = chips // inner
    inner_masks = [SPLIT * i for i in range(1, inner)]
    layer_mask = lambda j: SPLIT * inner * j
    streams = [list(range(0, outer, 2)), list(range(1, outer, 2))]
    own_in, own_out = w_in[0, 0], w_out[0, 0]
    other_out, other_in = exclusive(own_out, 1), exclusive(own_in, 1)

    step_count = micro_count + section_count - 1
    carry = jnp.zeros((2, tok_rows, model_width), jnp.bfloat16)
    moe_orig = jnp.zeros((micro_count, tok_rows, model_width), jnp.bfloat16)
    moe_pruned = moe_orig
    terms = jnp.zeros((devices, experts), jnp.float32)
    for tick in range(step_count):
        if section_count == 1:
            position = tick
            item = lambda buffer: buffer[position]
        else:
            position = jnp.clip(tick - section_index, 0, micro_count - 1)
            active = jnp.logical_and(
                tick - section_index >= 0, tick - section_index < micro_count
            )
            item = lambda buffer: lax.dynamic_index_in_dim(buffer, position, 0, keepdims=False)
        fresh = min(tick, micro_count - 1)
        state_orig, state_pruned = states_orig[fresh], states_pruned[fresh]
        if section_count > 1:
            state_orig = jnp.where(section_index == 0, state_orig, carry[0])
            state_pruned = jnp.where(section_index == 0, state_pruned, carry[1])
        picked_orig, weight_orig = item(ids_orig[0]), item(gates_orig[0])
        operands = [
            state_orig,
            state_pruned,
            picked_orig,
            item(ids_pruned[0]),
            weight_orig,
            item(gates_pruned[0]),
            keep_mask,
        ]
        packed = run_kernel(
            functools.partial(pack_kernel, len(operands)),
            like(rows, model_width + extra),
            [in_hbm(value) for value in operands],
            [pltpu.VMEM(value.shape, value.dtype) for value in operands]
            + [pltpu.SemaphoreType.DMA((len(operands),))],
            space=pl.ANY,
        )
        column = {0: packed}
        for j in streams[0][1:] + streams[1][::-1]:
            column[j] = exclusive(packed, layer_mask(j))
        if tick == 0:
            own = stage([in_hbm(own_in), in_hbm(own_out)])
        blocks = []
        for stream, layers in enumerate(streams):
            joined = join_rows([column[j] for j in layers])
            if stream == 0:
                joined = after(joined, own)
            else:
                joined = after(joined, blocks[0][1])
            block = [joined]
            for mask in inner_masks:
                block.append(exclusive(joined, mask))
            blocks.append(block)
        if tick == 0:
            other = stage([other_in, other_out])
            weights = [own[0], other[0], own[1], other[1]]
        summed = []
        for stream, layers in enumerate(streams):
            partial = run_expert(
                experts, blocks[stream], weights, [len(layers) * rows] * inner
            )
            returned = [partial[0]] + [
                exclusive(part, mask) for part, mask in zip(partial[1:], inner_masks)
            ]
            outs = [like(rows, model_width)] * len(layers)
            if stream == 0:
                outs[0] = like(rows, model_width, jnp.float32)
            sums = run_kernel(functools.partial(plane_kernel, inner), outs, returned)
            for j, value in list(zip(layers, sums))[::-1]:
                summed.append(exclusive(value, layer_mask(j)) if j else value)
        round_orig, round_pruned, tick_terms, *moe = run_kernel(
            functools.partial(final_kernel, outer, loss_factor),
            [like(tok_rows, model_width)] * 2
            + [like(devices, experts, jnp.float32)]
            + [like(rows, model_width, jnp.float32)] * (section_count > 1),
            summed + [picked_orig, weight_orig],
        )
        if section_count > 1:
            tick_terms = jnp.where(active, tick_terms, 0.0)
            round_orig = jnp.where(active, round_orig, item(moe_orig))
            round_pruned = jnp.where(active, round_pruned, item(moe_pruned))
        terms = tick_terms if tick == 0 else terms + tick_terms
        moe_orig = lax.dynamic_update_index_in_dim(moe_orig, round_orig, position, 0)
        moe_pruned = lax.dynamic_update_index_in_dim(moe_pruned, round_pruned, position, 0)
        if tick + 1 < step_count and section_count > 1:
            state = jnp.stack([state_orig, state_pruned]).astype(jnp.float32)
            following = (state + moe[0].reshape(state.shape)).astype(jnp.bfloat16)
            onward = [(i, i + 1) for i in range(section_count - 1)]
            carry = lax.ppermute(following, "section", onward)
    shared = lax.all_to_all(terms, "expert", split_axis=0, concat_axis=0, tiled=True)
    loss = run_kernel(add_kernel, like(1, experts, jnp.float32), [shared])
    return (moe_orig[None], moe_pruned[None], loss)


def solution(mesh):
    return jax.shard_map(
        on_device,
        mesh=mesh,
        in_specs=(
            P(None, "expert", None),
            P(None, "expert", None),
            P("section", None, "expert", None),
            P("section", None, "expert", None),
            P("section", None, "expert", None),
            P("section", None, "expert", None),
            P("section", None),
            P("section", "expert", None, None),
            P("section", "expert", None, None),
        ),
        out_specs=(
            P("section", None, "expert", None),
            P("section", None, "expert", None),
            P("section", None),
        ),
        check_vma=False,
    )
```

```python
import functools

import jax
import jax.numpy as jnp
from jax import lax
from jax.experimental import pallas as pl
from jax.experimental.pallas import tpu as pltpu
from jax.sharding import PartitionSpec as P

SPLIT = 2
LANES = 128
MIB = 2**20


def run_kernel(body, outs, operands, scratch=(), limit=16, space=pltpu.VMEM, tail=0):
    spaces = [space] * (len(operands) - tail) + [pl.ANY] * tail
    return pl.pallas_call(
        body,
        out_shape=outs,
        in_specs=[pl.BlockSpec(memory_space=place) for place in spaces],
        out_specs=jax.tree.map(lambda _: pl.BlockSpec(memory_space=pltpu.VMEM), outs),
        scratch_shapes=list(scratch),
        compiler_params=pltpu.CompilerParams(vmem_limit_bytes=limit * MIB),
    )(*operands)


def in_hbm(value):
    return pltpu.with_memory_space_constraint(value, pltpu.HBM)


def like(rows, columns, dtype=jnp.bfloat16):
    return jax.ShapeDtypeStruct((rows, columns), dtype)


def exclusive(value, mask):
    masks = mask if isinstance(mask, tuple) else (mask,) * SPLIT
    pairs = [
        (source, source ^ masks[source % SPLIT]) for source in range(lax.axis_size("expert"))
    ]
    return lax.ppermute(value, "expert", pairs)


def normalize_rows(values):
    factor = lax.rsqrt(jnp.mean(values * values, axis=-1, keepdims=True) + 1e-06)
    return values * factor


def dense_weights(picked, gates, experts):
    rows = picked.shape[0]
    label = lax.broadcasted_iota(jnp.int32, (rows, experts), 1)
    total = jnp.zeros((rows, experts), jnp.float32)
    for k in range(picked.shape[1]):
        total = total + jnp.where(picked[:, k : k + 1] == label, gates[:, k : k + 1], 0.0)
    return total


def pack_kernel(count, *refs):
    sources, out_ref, scratch = refs[:count], refs[count], refs[count + 1 :]
    held, sems = scratch[:count], scratch[count]
    copies = [
        pltpu.make_async_copy(source, target, sems.at[place])
        for place, (source, target) in enumerate(zip(sources, held))
    ]
    for copy in copies:
        copy.start()
    for copy in copies:
        copy.wait()
    so_ref, sp_ref, io_ref, ip_ref, go_ref, gp_ref, keep_ref = held
    model_width = so_ref.shape[1]
    extra = out_ref.shape[1] - model_width
    experts = keep_ref.shape[1]
    states = jnp.concatenate(
        [so_ref[...].astype(jnp.float32), sp_ref[...].astype(jnp.float32)], axis=0
    )
    out_ref[:, :model_width] = normalize_rows(states).astype(jnp.bfloat16)
    dense_orig = dense_weights(io_ref[...], go_ref[...], experts)
    dense_pruned = dense_weights(ip_ref[...], gp_ref[...], experts)
    dense_pruned = dense_pruned * keep_ref[...].astype(jnp.float32)
    dense = jnp.concatenate([dense_orig, dense_pruned], axis=0)
    high = dense.astype(jnp.bfloat16)
    low = (dense - high.astype(jnp.float32)).astype(jnp.bfloat16)
    source = lax.broadcasted_iota(jnp.int32, (experts, extra), 0)
    lane = lax.broadcasted_iota(jnp.int32, (experts, extra), 1)
    out_ref[:, model_width:] = (
        jnp.dot(
            high,
            (lane == source).astype(jnp.float32).astype(jnp.bfloat16),
            preferred_element_type=jnp.float32,
        )
        + jnp.dot(
            low,
            (lane == source + experts).astype(jnp.float32).astype(jnp.bfloat16),
            preferred_element_type=jnp.float32,
        )
    ).astype(jnp.bfloat16)


def after(value, *awaited):
    return lax.optimization_barrier((value, awaited))[0]


def join_kernel(*refs):
    part_refs, out_ref = refs[:-1], refs[-1]
    rows = part_refs[0].shape[0]
    for place, part_ref in enumerate(part_refs):
        out_ref[place * rows : (place + 1) * rows, :] = part_ref[...]


def join_rows(parts):
    rows, columns = parts[0].shape
    return run_kernel(join_kernel, like(len(parts) * rows, columns), parts)


def expert_kernel(experts, row_count, sizes, loads, *refs):
    row_refs, refs = refs[:row_count], refs[row_count:]
    in_refs, out_refs, refs = refs[:SPLIT], refs[SPLIT : 2 * SPLIT], refs[2 * SPLIT :]
    copies = [None] * 2
    if loads:
        own_refs, refs = refs[:2], refs[2:]
        held_refs = refs[len(sizes) : len(sizes) + 2]
        refs, sems = refs[: len(sizes)] + refs[len(sizes) + 2 : -1], refs[-1]
        copies = [
            pltpu.make_async_copy(own_ref, held_ref, sems.at[place])
            for place, (own_ref, held_ref) in enumerate(zip(own_refs, held_refs))
        ]
        for copy in copies:
            copy.start()
    result_refs, (rows, hidden) = refs[: len(sizes)], refs[len(sizes) :]
    half, model_width = out_refs[0].shape
    expert = lax.axis_index("expert") // SPLIT
    weights = []
    filled = 0
    for row_ref in row_refs:
        size = row_ref.shape[0]
        rows[filled : filled + size, :] = row_ref[:, :model_width]
        filled += size
        extra = row_ref[:, model_width:].astype(jnp.float32)
        lane = lax.broadcasted_iota(jnp.int32, extra.shape, 1)
        mine = jnp.logical_or(lane == expert, lane == expert + experts)
        weights.append(jnp.sum(jnp.where(mine, extra, 0.0), axis=1, keepdims=True))
    weight = jnp.concatenate(weights, axis=0)
    for place, in_ref in enumerate(in_refs):
        if loads and place == SPLIT - 1:
            copies[0].wait()
        both = jnp.dot(rows[...], in_ref[...], preferred_element_type=jnp.float32)
        gate, up = both[:, :half], both[:, half:]
        hidden[:, place * half : (place + 1) * half] = (
            gate / (1.0 + jnp.exp(-gate)) * up
        ).astype(jnp.bfloat16)
    if loads:
        copies[1].wait()
    step = min(512, model_width)
    for start in range(0, model_width, step):
        value = sum(
            jnp.dot(
                hidden[:, place * half : (place + 1) * half],
                out_ref[:, start : start + step],
                preferred_element_type=jnp.float32,
            )
            for place, out_ref in enumerate(out_refs)
        )
        value = (value * weight).astype(jnp.bfloat16)
        filled = 0
        for size, result_ref in zip(sizes, result_refs):
            result_ref[:, start : start + step] = value[filled : filled + size]
            filled += size


def loading_kernel(experts, row_count, sizes, *refs):
    inputs, (other_in, other_out, own_in, own_out) = refs[:row_count], refs[row_count : row_count + 4]
    refs = refs[row_count + 4 :]
    held_in, held_out = refs[len(sizes) : len(sizes) + 2]
    expert_kernel(
        experts,
        row_count,
        sizes,
        True,
        *inputs,
        other_in,
        held_in,
        other_out,
        held_out,
        own_in,
        own_out,
        *refs,
    )


def run_expert(experts, row_arrays, weights, sizes, loads):
    total = sum(array.shape[0] for array in row_arrays)
    other_out = weights[1] if loads else weights[2]
    half, model_width = other_out.shape
    outs = [like(size, model_width) for size in sizes]
    scratch = [
        pltpu.VMEM((total, model_width), jnp.bfloat16),
        pltpu.VMEM((total, SPLIT * half), jnp.bfloat16),
    ]
    if loads:
        body = functools.partial(loading_kernel, experts, len(row_arrays), sizes)
        outs += [pltpu.VMEM(value.shape, value.dtype) for value in weights[2:]]
        scratch.append(pltpu.SemaphoreType.DMA((2,)))
    else:
        body = functools.partial(expert_kernel, experts, len(row_arrays), sizes, False)
    return run_kernel(
        body, outs, list(row_arrays) + list(weights), scratch, limit=24, tail=2 if loads else 0
    )


def relay_kernel(mine_ref, came_ref, out_ref):
    out_ref[...] = (
        mine_ref[...].astype(jnp.float32) + came_ref[...].astype(jnp.float32)
    ).astype(out_ref.dtype)


def plane_kernel(count, *refs):
    part_refs, out_refs = refs[:count], refs[count:]
    rows = out_refs[0].shape[0]
    for place, out_ref in enumerate(out_refs):
        out_ref[...] = sum(
            ref[place * rows : (place + 1) * rows, :].astype(jnp.float32) for ref in part_refs
        ).astype(out_ref.dtype)


def final_kernel(parts, factor, *refs):
    part_refs, refs = refs[:parts], refs[parts:]
    ids_ref, gates_ref, orig_ref, pruned_ref, terms_ref, *value_refs = refs
    tok_rows = orig_ref.shape[0]
    total = sum(ref[...].astype(jnp.float32) for ref in part_refs)
    for value_ref in value_refs:
        value_ref[...] = total
    value_orig, value_pruned = total[:tok_rows], total[tok_rows:]
    orig_ref[...] = value_orig.astype(jnp.bfloat16)
    pruned_ref[...] = value_pruned.astype(jnp.bfloat16)
    differ = value_orig - value_pruned
    errors = jnp.mean(differ * differ, axis=1, keepdims=True)
    experts = terms_ref.shape[1]
    dense = dense_weights(ids_ref[...], gates_ref[...], experts)
    terms = factor * jnp.sum(dense * errors, axis=0, keepdims=True)
    terms_ref[...] = jnp.broadcast_to(terms, terms_ref.shape)


def add_kernel(parts_ref, out_ref):
    out_ref[...] = jnp.sum(parts_ref[...], axis=0, keepdims=True)


def on_device(
    states_orig,
    states_pruned,
    ids_orig,
    ids_pruned,
    gates_orig,
    gates_pruned,
    keep_mask,
    w_in,
    w_out,
):
    devices = lax.axis_size("expert")
    section_count = lax.axis_size("section")
    section_index = lax.axis_index("section")
    micro_count, tok_rows, model_width = states_orig.shape
    experts = keep_mask.shape[1]
    top_count = ids_orig.shape[-1]
    loss_factor = experts / (top_count * micro_count * tok_rows * devices)
    extra = -(-2 * experts // LANES) * LANES
    rows = 2 * tok_rows
    chips = devices // SPLIT
    inner = 4
    outer = chips // inner
    first_axis, second_axis = (SPLIT, 2 * SPLIT), (2 * SPLIT, SPLIT)
    layer_mask = lambda j: SPLIT * inner * j
    streams = [list(range(outer // 2)), list(range(outer // 2, outer))]
    own_in, own_out = w_in[0, 0], w_out[0, 0]
    other_out, other_in = exclusive(own_out, 1), exclusive(own_in, 1)

    step_count = micro_count + section_count - 1
    carry = jnp.zeros((2, tok_rows, model_width), jnp.bfloat16)
    moe_orig = jnp.zeros((micro_count, tok_rows, model_width), jnp.bfloat16)
    moe_pruned = moe_orig
    terms = jnp.zeros((devices, experts), jnp.float32)
    for tick in range(step_count):
        if section_count == 1:
            position = tick
            item = lambda buffer: buffer[position]
        else:
            position = jnp.clip(tick - section_index, 0, micro_count - 1)
            active = jnp.logical_and(
                tick - section_index >= 0, tick - section_index < micro_count
            )
            item = lambda buffer: lax.dynamic_index_in_dim(buffer, position, 0, keepdims=False)
        fresh = min(tick, micro_count - 1)
        state_orig, state_pruned = states_orig[fresh], states_pruned[fresh]
        if section_count > 1:
            state_orig = jnp.where(section_index == 0, state_orig, carry[0])
            state_pruned = jnp.where(section_index == 0, state_pruned, carry[1])
        picked_orig, weight_orig = item(ids_orig[0]), item(gates_orig[0])
        operands = [
            state_orig,
            state_pruned,
            picked_orig,
            item(ids_pruned[0]),
            weight_orig,
            item(gates_pruned[0]),
            keep_mask,
        ]
        packed = run_kernel(
            functools.partial(pack_kernel, len(operands)),
            like(rows, model_width + extra),
            [in_hbm(value) for value in operands],
            [pltpu.VMEM(value.shape, value.dtype) for value in operands]
            + [pltpu.SemaphoreType.DMA((len(operands),))],
            space=pl.ANY,
        )
        column = {0: packed}
        for j in streams[0][1:] + streams[1][::-1]:
            column[j] = exclusive(packed, layer_mask(j))
        blocks = []
        for stream, layers in enumerate(streams):
            joined = join_rows([column[j] for j in layers])
            first = exclusive(joined, first_axis)
            second = exclusive(joined, second_axis)
            blocks.append([joined, first, second, exclusive(first, second_axis)])
        summed = []
        for stream, layers in enumerate(streams):
            sizes = [len(layers) * rows] * inner
            if tick == 0 and stream == 0:
                weights = [other_in, other_out, in_hbm(own_in), in_hbm(own_out)]
                *partial, held_in, held_out = run_expert(
                    experts, blocks[stream], weights, sizes, True
                )
                weights = [other_in, held_in, other_out, held_out]
            else:
                partial = run_expert(experts, blocks[stream], weights, sizes, False)
            mine, first, second, across = partial
            across = exclusive(across, first_axis)
            first = exclusive(first, first_axis)
            second = run_kernel(relay_kernel, like(*second.shape), [second, across])
            returned = [mine, first, exclusive(second, second_axis)]
            outs = [like(rows, model_width)] * len(layers)
            if stream == 0:
                outs[0] = like(rows, model_width, jnp.float32)
            sums = run_kernel(functools.partial(plane_kernel, len(returned)), outs, returned)
            for j, value in list(zip(layers, sums))[::-1]:
                summed.append(exclusive(value, layer_mask(j)) if j else value)
        round_orig, round_pruned, tick_terms, *moe = run_kernel(
            functools.partial(final_kernel, outer, loss_factor),
            [like(tok_rows, model_width)] * 2
            + [like(devices, experts, jnp.float32)]
            + [like(rows, model_width, jnp.float32)] * (section_count > 1),
            summed + [picked_orig, weight_orig],
        )
        if section_count > 1:
            tick_terms = jnp.where(active, tick_terms, 0.0)
            round_orig = jnp.where(active, round_orig, item(moe_orig))
            round_pruned = jnp.where(active, round_pruned, item(moe_pruned))
        terms = tick_terms if tick == 0 else terms + tick_terms
        moe_orig = lax.dynamic_update_index_in_dim(moe_orig, round_orig, position, 0)
        moe_pruned = lax.dynamic_update_index_in_dim(moe_pruned, round_pruned, position, 0)
        if tick + 1 < step_count and section_count > 1:
            state = jnp.stack([state_orig, state_pruned]).astype(jnp.float32)
            following = (state + moe[0].reshape(state.shape)).astype(jnp.bfloat16)
            onward = [(i, i + 1) for i in range(section_count - 1)]
            carry = lax.ppermute(following, "section", onward)
    shared = lax.all_to_all(terms, "expert", split_axis=0, concat_axis=0, tiled=True)
    loss = run_kernel(add_kernel, like(1, experts, jnp.float32), [shared])
    return (moe_orig[None], moe_pruned[None], loss)


def solution(mesh):
    return jax.shard_map(
        on_device,
        mesh=mesh,
        in_specs=(
            P(None, "expert", None),
            P(None, "expert", None),
            P("section", None, "expert", None),
            P("section", None, "expert", None),
            P("section", None, "expert", None),
            P("section", None, "expert", None),
            P("section", None),
            P("section", "expert", None, None),
            P("section", "expert", None, None),
        ),
        out_specs=(
            P("section", None, "expert", None),
            P("section", None, "expert", None),
            P("section", None),
        ),
        check_vma=False,
    )
```

```python
import functools

import jax
import jax.numpy as jnp
from jax import lax
from jax.experimental import pallas as pl
from jax.experimental.pallas import tpu as pltpu
from jax.sharding import PartitionSpec as P

SPLIT = 2
LANES = 128
MIB = 2**20


def run_kernel(body, outs, operands, scratch=(), limit=16, space=pltpu.VMEM, tail=0):
    spaces = [space] * (len(operands) - tail) + [pl.ANY] * tail
    return pl.pallas_call(
        body,
        out_shape=outs,
        in_specs=[pl.BlockSpec(memory_space=place) for place in spaces],
        out_specs=jax.tree.map(lambda _: pl.BlockSpec(memory_space=pltpu.VMEM), outs),
        scratch_shapes=list(scratch),
        compiler_params=pltpu.CompilerParams(vmem_limit_bytes=limit * MIB),
    )(*operands)


def in_hbm(value):
    return pltpu.with_memory_space_constraint(value, pltpu.HBM)


def like(rows, columns, dtype=jnp.bfloat16):
    return jax.ShapeDtypeStruct((rows, columns), dtype)


def exclusive(value, mask):
    masks = mask if isinstance(mask, tuple) else (mask,) * SPLIT
    pairs = [
        (source, source ^ masks[source % SPLIT]) for source in range(lax.axis_size("expert"))
    ]
    return lax.ppermute(value, "expert", pairs)


def normalize_rows(values):
    factor = lax.rsqrt(jnp.mean(values * values, axis=-1, keepdims=True) + 1e-06)
    return values * factor


def dense_weights(picked, gates, experts):
    rows = picked.shape[0]
    label = lax.broadcasted_iota(jnp.int32, (rows, experts), 1)
    total = jnp.zeros((rows, experts), jnp.float32)
    for k in range(picked.shape[1]):
        total = total + jnp.where(picked[:, k : k + 1] == label, gates[:, k : k + 1], 0.0)
    return total


def pack_kernel(count, *refs):
    sources, out_ref, scratch = refs[:count], refs[count], refs[count + 1 :]
    held, sems = scratch[:count], scratch[count]
    copies = [
        pltpu.make_async_copy(source, target, sems.at[place])
        for place, (source, target) in enumerate(zip(sources, held))
    ]
    for copy in copies:
        copy.start()
    for copy in copies:
        copy.wait()
    so_ref, sp_ref, io_ref, ip_ref, go_ref, gp_ref, keep_ref = held
    model_width = so_ref.shape[1]
    extra = out_ref.shape[1] - model_width
    experts = keep_ref.shape[1]
    states = jnp.concatenate(
        [so_ref[...].astype(jnp.float32), sp_ref[...].astype(jnp.float32)], axis=0
    )
    out_ref[:, :model_width] = normalize_rows(states).astype(jnp.bfloat16)
    dense_orig = dense_weights(io_ref[...], go_ref[...], experts)
    dense_pruned = dense_weights(ip_ref[...], gp_ref[...], experts)
    dense_pruned = dense_pruned * keep_ref[...].astype(jnp.float32)
    dense = jnp.concatenate([dense_orig, dense_pruned], axis=0)
    high = dense.astype(jnp.bfloat16)
    low = (dense - high.astype(jnp.float32)).astype(jnp.bfloat16)
    source = lax.broadcasted_iota(jnp.int32, (experts, extra), 0)
    lane = lax.broadcasted_iota(jnp.int32, (experts, extra), 1)
    out_ref[:, model_width:] = (
        jnp.dot(
            high,
            (lane == source).astype(jnp.float32).astype(jnp.bfloat16),
            preferred_element_type=jnp.float32,
        )
        + jnp.dot(
            low,
            (lane == source + experts).astype(jnp.float32).astype(jnp.bfloat16),
            preferred_element_type=jnp.float32,
        )
    ).astype(jnp.bfloat16)


def stage_kernel(count, *refs):
    sources, targets, sems = refs[:count], refs[count : 2 * count], refs[2 * count]
    copies = [
        pltpu.make_async_copy(source, target, sems.at[place])
        for place, (source, target) in enumerate(zip(sources, targets))
    ]
    for copy in copies:
        copy.start()
    for copy in copies:
        copy.wait()


def stage(arrays):
    return run_kernel(
        functools.partial(stage_kernel, len(arrays)),
        [pltpu.VMEM(value.shape, value.dtype) for value in arrays],
        arrays,
        [pltpu.SemaphoreType.DMA((len(arrays),))],
        space=pl.ANY,
    )


def after(value, *awaited):
    return lax.optimization_barrier((value, awaited))[0]


def join_kernel(*refs):
    part_refs, out_ref = refs[:-1], refs[-1]
    rows = part_refs[0].shape[0]
    for place, part_ref in enumerate(part_refs):
        out_ref[place * rows : (place + 1) * rows, :] = part_ref[...]


def join_rows(parts):
    rows, columns = parts[0].shape
    return run_kernel(join_kernel, like(len(parts) * rows, columns), parts)


def expert_kernel(experts, row_count, sizes, *refs):
    row_refs, refs = refs[:row_count], refs[row_count:]
    in_refs, out_refs, refs = refs[:SPLIT], refs[SPLIT : 2 * SPLIT], refs[2 * SPLIT :]
    result_refs, (rows, hidden) = refs[: len(sizes)], refs[len(sizes) :]
    half, model_width = out_refs[0].shape
    expert = lax.axis_index("expert") // SPLIT
    weights = []
    filled = 0
    for row_ref in row_refs:
        size = row_ref.shape[0]
        rows[filled : filled + size, :] = row_ref[:, :model_width]
        filled += size
        extra = row_ref[:, model_width:].astype(jnp.float32)
        lane = lax.broadcasted_iota(jnp.int32, extra.shape, 1)
        mine = jnp.logical_or(lane == expert, lane == expert + experts)
        weights.append(jnp.sum(jnp.where(mine, extra, 0.0), axis=1, keepdims=True))
    weight = jnp.concatenate(weights, axis=0)
    for place, in_ref in enumerate(in_refs):
        both = jnp.dot(rows[...], in_ref[...], preferred_element_type=jnp.float32)
        gate, up = both[:, :half], both[:, half:]
        hidden[:, place * half : (place + 1) * half] = (
            gate / (1.0 + jnp.exp(-gate)) * up
        ).astype(jnp.bfloat16)
    step = min(512, model_width)
    for start in range(0, model_width, step):
        value = sum(
            jnp.dot(
                hidden[:, place * half : (place + 1) * half],
                out_ref[:, start : start + step],
                preferred_element_type=jnp.float32,
            )
            for place, out_ref in enumerate(out_refs)
        )
        value = (value * weight).astype(jnp.bfloat16)
        filled = 0
        for size, result_ref in zip(sizes, result_refs):
            result_ref[:, start : start + step] = value[filled : filled + size]
            filled += size


def run_expert(experts, row_arrays, weights, sizes):
    total = sum(array.shape[0] for array in row_arrays)
    half, model_width = weights[-1].shape
    return run_kernel(
        functools.partial(expert_kernel, experts, len(row_arrays), sizes),
        [like(size, model_width) for size in sizes],
        list(row_arrays) + list(weights),
        [
            pltpu.VMEM((total, model_width), jnp.bfloat16),
            pltpu.VMEM((total, SPLIT * half), jnp.bfloat16),
        ],
        limit=24,
    )


def relay_kernel(mine_ref, came_ref, out_ref):
    out_ref[...] = (
        mine_ref[...].astype(jnp.float32) + came_ref[...].astype(jnp.float32)
    ).astype(out_ref.dtype)


def plane_kernel(count, *refs):
    part_refs, out_refs = refs[:count], refs[count:]
    rows = out_refs[0].shape[0]
    for place, out_ref in enumerate(out_refs):
        out_ref[...] = sum(
            ref[place * rows : (place + 1) * rows, :].astype(jnp.float32) for ref in part_refs
        ).astype(out_ref.dtype)


def final_kernel(parts, factor, *refs):
    part_refs, refs = refs[:parts], refs[parts:]
    ids_ref, gates_ref, orig_ref, pruned_ref, terms_ref, *value_refs = refs
    tok_rows = orig_ref.shape[0]
    total = sum(ref[...].astype(jnp.float32) for ref in part_refs)
    for value_ref in value_refs:
        value_ref[...] = total
    value_orig, value_pruned = total[:tok_rows], total[tok_rows:]
    orig_ref[...] = value_orig.astype(jnp.bfloat16)
    pruned_ref[...] = value_pruned.astype(jnp.bfloat16)
    differ = value_orig - value_pruned
    errors = jnp.mean(differ * differ, axis=1, keepdims=True)
    experts = terms_ref.shape[1]
    dense = dense_weights(ids_ref[...], gates_ref[...], experts)
    terms = factor * jnp.sum(dense * errors, axis=0, keepdims=True)
    terms_ref[...] = jnp.broadcast_to(terms, terms_ref.shape)


def add_kernel(parts_ref, out_ref):
    out_ref[...] = jnp.sum(parts_ref[...], axis=0, keepdims=True)


def on_device(
    states_orig,
    states_pruned,
    ids_orig,
    ids_pruned,
    gates_orig,
    gates_pruned,
    keep_mask,
    w_in,
    w_out,
):
    devices = lax.axis_size("expert")
    section_count = lax.axis_size("section")
    section_index = lax.axis_index("section")
    micro_count, tok_rows, model_width = states_orig.shape
    experts = keep_mask.shape[1]
    top_count = ids_orig.shape[-1]
    loss_factor = experts / (top_count * micro_count * tok_rows * devices)
    extra = -(-2 * experts // LANES) * LANES
    rows = 2 * tok_rows
    chips = devices // SPLIT
    inner = 4
    outer = chips // inner
    first_axis, second_axis = (SPLIT, 2 * SPLIT), (2 * SPLIT, SPLIT)
    layer_mask = lambda j: SPLIT * inner * j
    own_in, own_out = w_in[0, 0], w_out[0, 0]
    other_out, other_in = exclusive(own_out, 1), exclusive(own_in, 1)

    step_count = micro_count + section_count - 1
    carry = jnp.zeros((2, tok_rows, model_width), jnp.bfloat16)
    moe_orig = jnp.zeros((micro_count, tok_rows, model_width), jnp.bfloat16)
    moe_pruned = moe_orig
    terms = jnp.zeros((devices, experts), jnp.float32)
    for tick in range(step_count):
        if section_count == 1:
            position = tick
            item = lambda buffer: buffer[position]
        else:
            position = jnp.clip(tick - section_index, 0, micro_count - 1)
            active = jnp.logical_and(
                tick - section_index >= 0, tick - section_index < micro_count
            )
            item = lambda buffer: lax.dynamic_index_in_dim(buffer, position, 0, keepdims=False)
        fresh = min(tick, micro_count - 1)
        state_orig, state_pruned = states_orig[fresh], states_pruned[fresh]
        if section_count > 1:
            state_orig = jnp.where(section_index == 0, state_orig, carry[0])
            state_pruned = jnp.where(section_index == 0, state_pruned, carry[1])
        picked_orig, weight_orig = item(ids_orig[0]), item(gates_orig[0])
        operands = [
            state_orig,
            state_pruned,
            picked_orig,
            item(ids_pruned[0]),
            weight_orig,
            item(gates_pruned[0]),
            keep_mask,
        ]
        packed = run_kernel(
            functools.partial(pack_kernel, len(operands)),
            like(rows, model_width + extra),
            [in_hbm(value) for value in operands],
            [pltpu.VMEM(value.shape, value.dtype) for value in operands]
            + [pltpu.SemaphoreType.DMA((len(operands),))],
            space=pl.ANY,
        )
        away = [exclusive(packed, layer_mask(j)) for j in reversed(range(1, outer))]
        column = join_rows([packed] + away[::-1])
        first = exclusive(column, first_axis)
        second = exclusive(column, second_axis)
        across = exclusive(after(first, second), second_axis)
        if tick == 0:
            own = stage([in_hbm(own_in), in_hbm(own_out)])
            weights = [own[0], other_in, own[1], other_out]
        mine, first, second = run_expert(
            experts, [column, first, second], weights, [outer * rows] * 3
        )
        (across,) = run_expert(experts, [after(across, mine)], weights, [outer * rows])
        across = exclusive(across, first_axis)
        first = exclusive(first, first_axis)
        second = run_kernel(relay_kernel, like(*second.shape), [second, across])
        returned = [mine, first, exclusive(second, second_axis)]
        outs = [like(rows, model_width, jnp.float32)] + [like(rows, model_width)] * (outer - 1)
        kept, *sent = run_kernel(functools.partial(plane_kernel, len(returned)), outs, returned)
        summed = [kept] + [
            exclusive(sent[j - 1], layer_mask(j)) for j in reversed(range(1, outer))
        ]
        round_orig, round_pruned, tick_terms, *moe = run_kernel(
            functools.partial(final_kernel, outer, loss_factor),
            [like(tok_rows, model_width)] * 2
            + [like(devices, experts, jnp.float32)]
            + [like(rows, model_width, jnp.float32)] * (section_count > 1),
            summed + [picked_orig, weight_orig],
        )
        if section_count > 1:
            tick_terms = jnp.where(active, tick_terms, 0.0)
            round_orig = jnp.where(active, round_orig, item(moe_orig))
            round_pruned = jnp.where(active, round_pruned, item(moe_pruned))
        terms = tick_terms if tick == 0 else terms + tick_terms
        moe_orig = lax.dynamic_update_index_in_dim(moe_orig, round_orig, position, 0)
        moe_pruned = lax.dynamic_update_index_in_dim(moe_pruned, round_pruned, position, 0)
        if tick + 1 < step_count and section_count > 1:
            state = jnp.stack([state_orig, state_pruned]).astype(jnp.float32)
            following = (state + moe[0].reshape(state.shape)).astype(jnp.bfloat16)
            onward = [(i, i + 1) for i in range(section_count - 1)]
            carry = lax.ppermute(following, "section", onward)
    shared = lax.all_to_all(terms, "expert", split_axis=0, concat_axis=0, tiled=True)
    loss = run_kernel(add_kernel, like(1, experts, jnp.float32), [shared])
    return (moe_orig[None], moe_pruned[None], loss)


def solution(mesh):
    return jax.shard_map(
        on_device,
        mesh=mesh,
        in_specs=(
            P(None, "expert", None),
            P(None, "expert", None),
            P("section", None, "expert", None),
            P("section", None, "expert", None),
            P("section", None, "expert", None),
            P("section", None, "expert", None),
            P("section", None),
            P("section", "expert", None, None),
            P("section", "expert", None, None),
        ),
        out_specs=(
            P("section", None, "expert", None),
            P("section", None, "expert", None),
            P("section", None),
        ),
        check_vma=False,
    )
```

```python
import functools

import jax
import jax.numpy as jnp
from jax import lax
from jax.experimental import pallas as pl
from jax.experimental.pallas import tpu as pltpu
from jax.sharding import PartitionSpec as P

SPLIT = 2
LANES = 128
MIB = 2**20


def run_kernel(body, outs, operands, scratch=(), limit=16, space=pltpu.VMEM, tail=0):
    spaces = [space] * (len(operands) - tail) + [pl.ANY] * tail
    return pl.pallas_call(
        body,
        out_shape=outs,
        in_specs=[pl.BlockSpec(memory_space=place) for place in spaces],
        out_specs=jax.tree.map(lambda _: pl.BlockSpec(memory_space=pltpu.VMEM), outs),
        scratch_shapes=list(scratch),
        compiler_params=pltpu.CompilerParams(vmem_limit_bytes=limit * MIB),
    )(*operands)


def in_hbm(value):
    return pltpu.with_memory_space_constraint(value, pltpu.HBM)


def like(rows, columns, dtype=jnp.bfloat16):
    return jax.ShapeDtypeStruct((rows, columns), dtype)


def exclusive(value, mask):
    masks = mask if isinstance(mask, tuple) else (mask,) * SPLIT
    pairs = [
        (source, source ^ masks[source % SPLIT]) for source in range(lax.axis_size("expert"))
    ]
    return lax.ppermute(value, "expert", pairs)


def normalize_rows(values):
    factor = lax.rsqrt(jnp.mean(values * values, axis=-1, keepdims=True) + 1e-06)
    return values * factor


def dense_weights(picked, gates, experts):
    rows = picked.shape[0]
    label = lax.broadcasted_iota(jnp.int32, (rows, experts), 1)
    total = jnp.zeros((rows, experts), jnp.float32)
    for k in range(picked.shape[1]):
        total = total + jnp.where(picked[:, k : k + 1] == label, gates[:, k : k + 1], 0.0)
    return total


def pack_kernel(count, *refs):
    sources, out_ref, scratch = refs[:count], refs[count], refs[count + 1 :]
    held, sems = scratch[:count], scratch[count]
    copies = [
        pltpu.make_async_copy(source, target, sems.at[place])
        for place, (source, target) in enumerate(zip(sources, held))
    ]
    for copy in copies:
        copy.start()
    for copy in copies:
        copy.wait()
    so_ref, sp_ref, io_ref, ip_ref, go_ref, gp_ref, keep_ref = held
    model_width = so_ref.shape[1]
    extra = out_ref.shape[1] - model_width
    experts = keep_ref.shape[1]
    states = jnp.concatenate(
        [so_ref[...].astype(jnp.float32), sp_ref[...].astype(jnp.float32)], axis=0
    )
    out_ref[:, :model_width] = normalize_rows(states).astype(jnp.bfloat16)
    dense_orig = dense_weights(io_ref[...], go_ref[...], experts)
    dense_pruned = dense_weights(ip_ref[...], gp_ref[...], experts)
    dense_pruned = dense_pruned * keep_ref[...].astype(jnp.float32)
    dense = jnp.concatenate([dense_orig, dense_pruned], axis=0)
    high = dense.astype(jnp.bfloat16)
    low = (dense - high.astype(jnp.float32)).astype(jnp.bfloat16)
    source = lax.broadcasted_iota(jnp.int32, (experts, extra), 0)
    lane = lax.broadcasted_iota(jnp.int32, (experts, extra), 1)
    out_ref[:, model_width:] = (
        jnp.dot(
            high,
            (lane == source).astype(jnp.float32).astype(jnp.bfloat16),
            preferred_element_type=jnp.float32,
        )
        + jnp.dot(
            low,
            (lane == source + experts).astype(jnp.float32).astype(jnp.bfloat16),
            preferred_element_type=jnp.float32,
        )
    ).astype(jnp.bfloat16)


def after(value, *awaited):
    return lax.optimization_barrier((value, awaited))[0]


def stage_kernel(count, *refs):
    sources, targets, sems = refs[:count], refs[count : 2 * count], refs[2 * count]
    copies = [
        pltpu.make_async_copy(source, target, sems.at[place])
        for place, (source, target) in enumerate(zip(sources, targets))
    ]
    for copy in copies:
        copy.start()
    for copy in copies:
        copy.wait()


def stage(arrays):
    return run_kernel(
        functools.partial(stage_kernel, len(arrays)),
        [pltpu.VMEM(value.shape, value.dtype) for value in arrays],
        arrays,
        [pltpu.SemaphoreType.DMA((len(arrays),))],
        space=pl.ANY,
    )


def join_kernel(*refs):
    part_refs, out_ref = refs[:-1], refs[-1]
    rows = part_refs[0].shape[0]
    for place, part_ref in enumerate(part_refs):
        out_ref[place * rows : (place + 1) * rows, :] = part_ref[...]


def join_rows(parts):
    rows, columns = parts[0].shape
    return run_kernel(join_kernel, like(len(parts) * rows, columns), parts)


def expert_kernel(experts, row_count, sizes, *refs):
    row_refs, refs = refs[:row_count], refs[row_count:]
    in_refs, out_refs, refs = refs[:SPLIT], refs[SPLIT : 2 * SPLIT], refs[2 * SPLIT :]
    result_refs, (rows, hidden) = refs[: len(sizes)], refs[len(sizes) :]
    half, model_width = out_refs[0].shape
    expert = lax.axis_index("expert") // SPLIT
    weights = []
    filled = 0
    for row_ref in row_refs:
        size = row_ref.shape[0]
        rows[filled : filled + size, :] = row_ref[:, :model_width]
        filled += size
        extra = row_ref[:, model_width:].astype(jnp.float32)
        lane = lax.broadcasted_iota(jnp.int32, extra.shape, 1)
        mine = jnp.logical_or(lane == expert, lane == expert + experts)
        weights.append(jnp.sum(jnp.where(mine, extra, 0.0), axis=1, keepdims=True))
    weight = jnp.concatenate(weights, axis=0)
    for place, in_ref in enumerate(in_refs):
        both = jnp.dot(rows[...], in_ref[...], preferred_element_type=jnp.float32)
        gate, up = both[:, :half], both[:, half:]
        hidden[:, place * half : (place + 1) * half] = (
            gate / (1.0 + jnp.exp(-gate)) * up
        ).astype(jnp.bfloat16)
    step = min(512, model_width)
    for start in range(0, model_width, step):
        value = sum(
            jnp.dot(
                hidden[:, place * half : (place + 1) * half],
                out_ref[:, start : start + step],
                preferred_element_type=jnp.float32,
            )
            for place, out_ref in enumerate(out_refs)
        )
        value = (value * weight).astype(jnp.bfloat16)
        filled = 0
        for size, result_ref in zip(sizes, result_refs):
            result_ref[:, start : start + step] = value[filled : filled + size]
            filled += size


def run_expert(experts, row_arrays, weights, sizes):
    total = sum(array.shape[0] for array in row_arrays)
    half, model_width = weights[-1].shape
    return run_kernel(
        functools.partial(expert_kernel, experts, len(row_arrays), sizes),
        [like(size, model_width) for size in sizes],
        list(row_arrays) + list(weights),
        [
            pltpu.VMEM((total, model_width), jnp.bfloat16),
            pltpu.VMEM((total, SPLIT * half), jnp.bfloat16),
        ],
        limit=24,
    )


def plane_kernel(count, *refs):
    part_refs, out_refs = refs[:count], refs[count:]
    rows = out_refs[0].shape[0]
    for place, out_ref in enumerate(out_refs):
        out_ref[...] = sum(
            ref[place * rows : (place + 1) * rows, :].astype(jnp.float32) for ref in part_refs
        ).astype(out_ref.dtype)


def final_kernel(parts, factor, *refs):
    part_refs, refs = refs[:parts], refs[parts:]
    ids_ref, gates_ref, orig_ref, pruned_ref, terms_ref, *value_refs = refs
    tok_rows = orig_ref.shape[0]
    total = sum(ref[...].astype(jnp.float32) for ref in part_refs)
    for value_ref in value_refs:
        value_ref[...] = total
    value_orig, value_pruned = total[:tok_rows], total[tok_rows:]
    orig_ref[...] = value_orig.astype(jnp.bfloat16)
    pruned_ref[...] = value_pruned.astype(jnp.bfloat16)
    differ = value_orig - value_pruned
    errors = jnp.mean(differ * differ, axis=1, keepdims=True)
    experts = terms_ref.shape[1]
    dense = dense_weights(ids_ref[...], gates_ref[...], experts)
    terms = factor * jnp.sum(dense * errors, axis=0, keepdims=True)
    terms_ref[...] = jnp.broadcast_to(terms, terms_ref.shape)


def add_kernel(parts_ref, out_ref):
    out_ref[...] = jnp.sum(parts_ref[...], axis=0, keepdims=True)


def on_device(
    states_orig,
    states_pruned,
    ids_orig,
    ids_pruned,
    gates_orig,
    gates_pruned,
    keep_mask,
    w_in,
    w_out,
):
    devices = lax.axis_size("expert")
    section_count = lax.axis_size("section")
    section_index = lax.axis_index("section")
    micro_count, tok_rows, model_width = states_orig.shape
    experts = keep_mask.shape[1]
    top_count = ids_orig.shape[-1]
    loss_factor = experts / (top_count * micro_count * tok_rows * devices)
    extra = -(-2 * experts // LANES) * LANES
    rows = 2 * tok_rows
    chips = devices // SPLIT
    inner = 4
    outer = chips // inner
    first_axis, second_axis, both_axes = (SPLIT, 2 * SPLIT), (2 * SPLIT, SPLIT), 3 * SPLIT
    layer_mask = lambda j: SPLIT * inner * j
    nearer = list(range(1, outer // 2 + 1))
    streams = [[j for j in range(outer) if j not in nearer], nearer]
    own_in, own_out = w_in[0, 0], w_out[0, 0]
    other_out, other_in = exclusive(own_out, 1), exclusive(own_in, 1)

    step_count = micro_count + section_count - 1
    carry = jnp.zeros((2, tok_rows, model_width), jnp.bfloat16)
    moe_orig = jnp.zeros((micro_count, tok_rows, model_width), jnp.bfloat16)
    moe_pruned = moe_orig
    terms = jnp.zeros((devices, experts), jnp.float32)
    for tick in range(step_count):
        if section_count == 1:
            position = tick
            item = lambda buffer: buffer[position]
        else:
            position = jnp.clip(tick - section_index, 0, micro_count - 1)
            active = jnp.logical_and(
                tick - section_index >= 0, tick - section_index < micro_count
            )
            item = lambda buffer: lax.dynamic_index_in_dim(buffer, position, 0, keepdims=False)
        fresh = min(tick, micro_count - 1)
        state_orig, state_pruned = states_orig[fresh], states_pruned[fresh]
        if section_count > 1:
            state_orig = jnp.where(section_index == 0, state_orig, carry[0])
            state_pruned = jnp.where(section_index == 0, state_pruned, carry[1])
        picked_orig, weight_orig = item(ids_orig[0]), item(gates_orig[0])
        operands = [
            state_orig,
            state_pruned,
            picked_orig,
            item(ids_pruned[0]),
            weight_orig,
            item(gates_pruned[0]),
            keep_mask,
        ]
        packed = run_kernel(
            functools.partial(pack_kernel, len(operands)),
            like(rows, model_width + extra),
            [in_hbm(value) for value in operands],
            [pltpu.VMEM(value.shape, value.dtype) for value in operands]
            + [pltpu.SemaphoreType.DMA((len(operands),))],
            space=pl.ANY,
        )
        column = {0: packed}
        for j in streams[0][1:] + streams[1][::-1]:
            column[j] = exclusive(packed, layer_mask(j))
        if tick == 0:
            own = stage([in_hbm(own_in), in_hbm(own_out)])
            weights = [own[0], other_in, own[1], other_out]
        blocks = []
        for stream, layers in enumerate(streams):
            joined = join_rows([column[j] for j in layers])
            first = exclusive(joined, first_axis)
            second = exclusive(joined, second_axis)
            blocks.append([joined, first, second, exclusive(first, second_axis)])
        summed = []
        for stream, layers in enumerate(streams):
            partial = run_expert(
                experts, blocks[stream], weights, [len(layers) * rows] * inner
            )
            returned = [partial[0]] + [
                exclusive(part, axes)
                for part, axes in zip(partial[1:], (first_axis, second_axis, both_axes))
            ]
            outs = [like(rows, model_width)] * len(layers)
            if stream == 0:
                outs[0] = like(rows, model_width, jnp.float32)
            sums = run_kernel(functools.partial(plane_kernel, len(returned)), outs, returned)
            for j, value in list(zip(layers, sums))[::-1]:
                summed.append(exclusive(value, layer_mask(j)) if j else value)
        round_orig, round_pruned, tick_terms, *moe = run_kernel(
            functools.partial(final_kernel, outer, loss_factor),
            [like(tok_rows, model_width)] * 2
            + [like(devices, experts, jnp.float32)]
            + [like(rows, model_width, jnp.float32)] * (section_count > 1),
            summed + [picked_orig, weight_orig],
        )
        if section_count > 1:
            tick_terms = jnp.where(active, tick_terms, 0.0)
            round_orig = jnp.where(active, round_orig, item(moe_orig))
            round_pruned = jnp.where(active, round_pruned, item(moe_pruned))
        terms = tick_terms if tick == 0 else terms + tick_terms
        moe_orig = lax.dynamic_update_index_in_dim(moe_orig, round_orig, position, 0)
        moe_pruned = lax.dynamic_update_index_in_dim(moe_pruned, round_pruned, position, 0)
        if tick + 1 < step_count and section_count > 1:
            state = jnp.stack([state_orig, state_pruned]).astype(jnp.float32)
            following = (state + moe[0].reshape(state.shape)).astype(jnp.bfloat16)
            onward = [(i, i + 1) for i in range(section_count - 1)]
            carry = lax.ppermute(following, "section", onward)
    shared = lax.all_to_all(terms, "expert", split_axis=0, concat_axis=0, tiled=True)
    loss = run_kernel(add_kernel, like(1, experts, jnp.float32), [shared])
    return (moe_orig[None], moe_pruned[None], loss)


def solution(mesh):
    return jax.shard_map(
        on_device,
        mesh=mesh,
        in_specs=(
            P(None, "expert", None),
            P(None, "expert", None),
            P("section", None, "expert", None),
            P("section", None, "expert", None),
            P("section", None, "expert", None),
            P("section", None, "expert", None),
            P("section", None),
            P("section", "expert", None, None),
            P("section", "expert", None, None),
        ),
        out_specs=(
            P("section", None, "expert", None),
            P("section", None, "expert", None),
            P("section", None),
        ),
        check_vma=False,
    )
```

```python
import functools

import jax
import jax.numpy as jnp
from jax import lax
from jax.experimental import pallas as pl
from jax.experimental.pallas import tpu as pltpu
from jax.sharding import PartitionSpec as P

SPLIT = 2
LANES = 128
MIB = 2**20


def run_kernel(body, outs, operands, scratch=(), limit=16, space=pltpu.VMEM):
    return pl.pallas_call(
        body,
        out_shape=outs,
        in_specs=[pl.BlockSpec(memory_space=space)] * len(operands),
        out_specs=jax.tree.map(lambda _: pl.BlockSpec(memory_space=pltpu.VMEM), outs),
        scratch_shapes=list(scratch),
        compiler_params=pltpu.CompilerParams(vmem_limit_bytes=limit * MIB),
    )(*operands)


def in_hbm(value):
    return pltpu.with_memory_space_constraint(value, pltpu.HBM)


def like(rows, columns, dtype=jnp.bfloat16):
    return jax.ShapeDtypeStruct((rows, columns), dtype)


def exclusive(value, mask):
    pairs = [(source, source ^ mask) for source in range(lax.axis_size("expert"))]
    return lax.ppermute(value, "expert", pairs)


def normalize_rows(values):
    factor = lax.rsqrt(jnp.mean(values * values, axis=-1, keepdims=True) + 1e-06)
    return values * factor


def dense_weights(picked, gates, experts):
    rows = picked.shape[0]
    label = lax.broadcasted_iota(jnp.int32, (rows, experts), 1)
    total = jnp.zeros((rows, experts), jnp.float32)
    for k in range(picked.shape[1]):
        total = total + jnp.where(picked[:, k : k + 1] == label, gates[:, k : k + 1], 0.0)
    return total


def pack_kernel(count, *refs):
    sources, out_ref, scratch = refs[:count], refs[count], refs[count + 1 :]
    held, sems = scratch[:count], scratch[count]
    copies = [
        pltpu.make_async_copy(source, target, sems.at[place])
        for place, (source, target) in enumerate(zip(sources, held))
    ]
    for copy in copies:
        copy.start()
    for copy in copies:
        copy.wait()
    so_ref, sp_ref, io_ref, ip_ref, go_ref, gp_ref, keep_ref = held
    model_width = so_ref.shape[1]
    extra = out_ref.shape[1] - model_width
    experts = keep_ref.shape[1]
    states = jnp.concatenate(
        [so_ref[...].astype(jnp.float32), sp_ref[...].astype(jnp.float32)], axis=0
    )
    out_ref[:, :model_width] = normalize_rows(states).astype(jnp.bfloat16)
    dense_orig = dense_weights(io_ref[...], go_ref[...], experts)
    dense_pruned = dense_weights(ip_ref[...], gp_ref[...], experts)
    dense_pruned = dense_pruned * keep_ref[...].astype(jnp.float32)
    dense = jnp.concatenate([dense_orig, dense_pruned], axis=0)
    high = dense.astype(jnp.bfloat16)
    low = (dense - high.astype(jnp.float32)).astype(jnp.bfloat16)
    source = lax.broadcasted_iota(jnp.int32, (experts, extra), 0)
    lane = lax.broadcasted_iota(jnp.int32, (experts, extra), 1)
    out_ref[:, model_width:] = (
        jnp.dot(
            high,
            (lane == source).astype(jnp.float32).astype(jnp.bfloat16),
            preferred_element_type=jnp.float32,
        )
        + jnp.dot(
            low,
            (lane == source + experts).astype(jnp.float32).astype(jnp.bfloat16),
            preferred_element_type=jnp.float32,
        )
    ).astype(jnp.bfloat16)


def stage_kernel(count, *refs):
    sources, targets, sems = refs[:count], refs[count : 2 * count], refs[2 * count]
    copies = [
        pltpu.make_async_copy(source, target, sems.at[place])
        for place, (source, target) in enumerate(zip(sources, targets))
    ]
    for copy in copies:
        copy.start()
    for copy in copies:
        copy.wait()


def stage(arrays):
    return run_kernel(
        functools.partial(stage_kernel, len(arrays)),
        [pltpu.VMEM(value.shape, value.dtype) for value in arrays],
        arrays,
        [pltpu.SemaphoreType.DMA((len(arrays),))],
        space=pl.ANY,
    )


def after(value, *awaited):
    return lax.optimization_barrier((value, awaited))[0]


def join_kernel(*refs):
    part_refs, out_ref = refs[:-1], refs[-1]
    rows = part_refs[0].shape[0]
    for place, part_ref in enumerate(part_refs):
        out_ref[place * rows : (place + 1) * rows, :] = part_ref[...]


def join_rows(parts):
    rows, columns = parts[0].shape
    return run_kernel(join_kernel, like(len(parts) * rows, columns), parts)


def expert_kernel(experts, row_count, sizes, *refs):
    row_refs, refs = refs[:row_count], refs[row_count:]
    in_refs, out_refs, refs = refs[:SPLIT], refs[SPLIT : 2 * SPLIT], refs[2 * SPLIT :]
    result_refs, (rows, hidden) = refs[: len(sizes)], refs[len(sizes) :]
    half, model_width = out_refs[0].shape
    expert = lax.axis_index("expert") // SPLIT
    weights = []
    filled = 0
    for row_ref in row_refs:
        size = row_ref.shape[0]
        rows[filled : filled + size, :] = row_ref[:, :model_width]
        filled += size
        extra = row_ref[:, model_width:].astype(jnp.float32)
        lane = lax.broadcasted_iota(jnp.int32, extra.shape, 1)
        mine = jnp.logical_or(lane == expert, lane == expert + experts)
        weights.append(jnp.sum(jnp.where(mine, extra, 0.0), axis=1, keepdims=True))
    weight = jnp.concatenate(weights, axis=0)
    for place, in_ref in enumerate(in_refs):
        both = jnp.dot(rows[...], in_ref[...], preferred_element_type=jnp.float32)
        gate, up = both[:, :half], both[:, half:]
        hidden[:, place * half : (place + 1) * half] = (
            gate / (1.0 + jnp.exp(-gate)) * up
        ).astype(jnp.bfloat16)
    step = min(512, model_width)
    for start in range(0, model_width, step):
        value = sum(
            jnp.dot(
                hidden[:, place * half : (place + 1) * half],
                out_ref[:, start : start + step],
                preferred_element_type=jnp.float32,
            )
            for place, out_ref in enumerate(out_refs)
        )
        value = (value * weight).astype(jnp.bfloat16)
        filled = 0
        for size, result_ref in zip(sizes, result_refs):
            result_ref[:, start : start + step] = value[filled : filled + size]
            filled += size


def run_expert(experts, row_arrays, weights, sizes):
    total = sum(array.shape[0] for array in row_arrays)
    half, model_width = weights[-1].shape
    return run_kernel(
        functools.partial(expert_kernel, experts, len(row_arrays), sizes),
        [like(size, model_width) for size in sizes],
        list(row_arrays) + list(weights),
        [
            pltpu.VMEM((total, model_width), jnp.bfloat16),
            pltpu.VMEM((total, SPLIT * half), jnp.bfloat16),
        ],
        limit=24,
    )


def plane_kernel(count, *refs):
    part_refs, out_refs = refs[:count], refs[count:]
    rows = out_refs[0].shape[0]
    for place, out_ref in enumerate(out_refs):
        out_ref[...] = sum(
            ref[place * rows : (place + 1) * rows, :].astype(jnp.float32) for ref in part_refs
        ).astype(out_ref.dtype)


def final_kernel(parts, factor, *refs):
    part_refs, refs = refs[:parts], refs[parts:]
    ids_ref, gates_ref, orig_ref, pruned_ref, terms_ref, *value_refs = refs
    tok_rows = orig_ref.shape[0]
    total = sum(ref[...].astype(jnp.float32) for ref in part_refs)
    for value_ref in value_refs:
        value_ref[...] = total
    value_orig, value_pruned = total[:tok_rows], total[tok_rows:]
    orig_ref[...] = value_orig.astype(jnp.bfloat16)
    pruned_ref[...] = value_pruned.astype(jnp.bfloat16)
    differ = value_orig - value_pruned
    errors = jnp.mean(differ * differ, axis=1, keepdims=True)
    experts = terms_ref.shape[1]
    dense = dense_weights(ids_ref[...], gates_ref[...], experts)
    terms = factor * jnp.sum(dense * errors, axis=0, keepdims=True)
    terms_ref[...] = jnp.broadcast_to(terms, terms_ref.shape)


def add_kernel(parts_ref, out_ref):
    out_ref[...] = jnp.sum(parts_ref[...], axis=0, keepdims=True)


def on_device(
    states_orig,
    states_pruned,
    ids_orig,
    ids_pruned,
    gates_orig,
    gates_pruned,
    keep_mask,
    w_in,
    w_out,
):
    devices = lax.axis_size("expert")
    section_count = lax.axis_size("section")
    section_index = lax.axis_index("section")
    micro_count, tok_rows, model_width = states_orig.shape
    experts = keep_mask.shape[1]
    top_count = ids_orig.shape[-1]
    loss_factor = experts / (top_count * micro_count * tok_rows * devices)
    extra = -(-2 * experts // LANES) * LANES
    rows = 2 * tok_rows
    chips = devices // SPLIT
    inner = min(4, chips)
    outer = chips // inner
    inner_masks = [SPLIT * i for i in range(1, inner)]
    layer_mask = lambda j: SPLIT * inner * j
    nearer = list(range(1, outer // 2 + 1))
    streams = [[j for j in range(outer) if j not in nearer], nearer]
    own_in, own_out = w_in[0, 0], w_out[0, 0]
    other_out, other_in = exclusive(own_out, 1), exclusive(own_in, 1)

    step_count = micro_count + section_count - 1
    carry = jnp.zeros((2, tok_rows, model_width), jnp.bfloat16)
    moe_orig = jnp.zeros((micro_count, tok_rows, model_width), jnp.bfloat16)
    moe_pruned = moe_orig
    terms = jnp.zeros((devices, experts), jnp.float32)
    for tick in range(step_count):
        if section_count == 1:
            position = tick
            item = lambda buffer: buffer[position]
        else:
            position = jnp.clip(tick - section_index, 0, micro_count - 1)
            active = jnp.logical_and(
                tick - section_index >= 0, tick - section_index < micro_count
            )
            item = lambda buffer: lax.dynamic_index_in_dim(buffer, position, 0, keepdims=False)
        fresh = min(tick, micro_count - 1)
        state_orig, state_pruned = states_orig[fresh], states_pruned[fresh]
        if section_count > 1:
            state_orig = jnp.where(section_index == 0, state_orig, carry[0])
            state_pruned = jnp.where(section_index == 0, state_pruned, carry[1])
        picked_orig, weight_orig = item(ids_orig[0]), item(gates_orig[0])
        operands = [
            state_orig,
            state_pruned,
            picked_orig,
            item(ids_pruned[0]),
            weight_orig,
            item(gates_pruned[0]),
            keep_mask,
        ]
        packed = run_kernel(
            functools.partial(pack_kernel, len(operands)),
            like(rows, model_width + extra),
            [in_hbm(value) for value in operands],
            [pltpu.VMEM(value.shape, value.dtype) for value in operands]
            + [pltpu.SemaphoreType.DMA((len(operands),))],
            space=pl.ANY,
        )
        column = {0: packed}
        for j in streams[1][::-1] + streams[0][1:]:
            column[j] = exclusive(packed, layer_mask(j))
        if tick == 0:
            own = stage([in_hbm(own_in), in_hbm(own_out)])
            weights = [own[0], other_in, own[1], other_out]
        blocks = []
        for stream, layers in enumerate(streams):
            joined = join_rows([column[j] for j in layers])
            if stream == 1:
                joined = after(joined, own)
            block = [joined]
            for mask in inner_masks:
                block.append(exclusive(joined, mask))
            blocks.append(block)
        summed = []
        for stream, layers in enumerate(streams):
            partial = run_expert(
                experts, blocks[stream], weights, [len(layers) * rows] * inner
            )
            returned = [partial[0]] + [
                exclusive(part, mask) for part, mask in zip(partial[1:], inner_masks)
            ]
            outs = [like(rows, model_width)] * len(layers)
            if stream == 0:
                outs[0] = like(rows, model_width, jnp.float32)
            sums = run_kernel(functools.partial(plane_kernel, inner), outs, returned)
            for j, value in list(zip(layers, sums))[::-1]:
                summed.append(exclusive(value, layer_mask(j)) if j else value)
        round_orig, round_pruned, tick_terms, *moe = run_kernel(
            functools.partial(final_kernel, outer, loss_factor),
            [like(tok_rows, model_width)] * 2
            + [like(devices, experts, jnp.float32)]
            + [like(rows, model_width, jnp.float32)] * (section_count > 1),
            summed + [picked_orig, weight_orig],
        )
        if section_count > 1:
            tick_terms = jnp.where(active, tick_terms, 0.0)
            round_orig = jnp.where(active, round_orig, item(moe_orig))
            round_pruned = jnp.where(active, round_pruned, item(moe_pruned))
        terms = tick_terms if tick == 0 else terms + tick_terms
        moe_orig = lax.dynamic_update_index_in_dim(moe_orig, round_orig, position, 0)
        moe_pruned = lax.dynamic_update_index_in_dim(moe_pruned, round_pruned, position, 0)
        if tick + 1 < step_count and section_count > 1:
            state = jnp.stack([state_orig, state_pruned]).astype(jnp.float32)
            following = (state + moe[0].reshape(state.shape)).astype(jnp.bfloat16)
            onward = [(i, i + 1) for i in range(section_count - 1)]
            carry = lax.ppermute(following, "section", onward)
    shared = lax.all_to_all(terms, "expert", split_axis=0, concat_axis=0, tiled=True)
    loss = run_kernel(add_kernel, like(1, experts, jnp.float32), [shared])
    return (moe_orig[None], moe_pruned[None], loss)


def solution(mesh):
    return jax.shard_map(
        on_device,
        mesh=mesh,
        in_specs=(
            P(None, "expert", None),
            P(None, "expert", None),
            P("section", None, "expert", None),
            P("section", None, "expert", None),
            P("section", None, "expert", None),
            P("section", None, "expert", None),
            P("section", None),
            P("section", "expert", None, None),
            P("section", "expert", None, None),
        ),
        out_specs=(
            P("section", None, "expert", None),
            P("section", None, "expert", None),
            P("section", None),
        ),
        check_vma=False,
    )
```

```python
import functools

import jax
import jax.numpy as jnp
from jax import lax
from jax.experimental import pallas as pl
from jax.experimental.pallas import tpu as pltpu
from jax.sharding import PartitionSpec as P

SPLIT = 2
LANES = 128
MIB = 2**20


def run_kernel(body, outs, operands, scratch=(), limit=16, space=pltpu.VMEM):
    return pl.pallas_call(
        body,
        out_shape=outs,
        in_specs=[pl.BlockSpec(memory_space=space)] * len(operands),
        out_specs=jax.tree.map(lambda _: pl.BlockSpec(memory_space=pltpu.VMEM), outs),
        scratch_shapes=list(scratch),
        compiler_params=pltpu.CompilerParams(vmem_limit_bytes=limit * MIB),
    )(*operands)


def in_hbm(value):
    return pltpu.with_memory_space_constraint(value, pltpu.HBM)


def like(rows, columns, dtype=jnp.bfloat16):
    return jax.ShapeDtypeStruct((rows, columns), dtype)


def exclusive(value, mask):
    pairs = [(source, source ^ mask) for source in range(lax.axis_size("expert"))]
    return lax.ppermute(value, "expert", pairs)


def normalize_rows(values):
    factor = lax.rsqrt(jnp.mean(values * values, axis=-1, keepdims=True) + 1e-06)
    return values * factor


def dense_weights(picked, gates, experts):
    rows = picked.shape[0]
    label = lax.broadcasted_iota(jnp.int32, (rows, experts), 1)
    total = jnp.zeros((rows, experts), jnp.float32)
    for k in range(picked.shape[1]):
        total = total + jnp.where(picked[:, k : k + 1] == label, gates[:, k : k + 1], 0.0)
    return total


def pack_kernel(count, *refs):
    sources, out_ref, scratch = refs[:count], refs[count], refs[count + 1 :]
    held, sems = scratch[:count], scratch[count]
    copies = [
        pltpu.make_async_copy(source, target, sems.at[place])
        for place, (source, target) in enumerate(zip(sources, held))
    ]
    for copy in copies:
        copy.start()
    for copy in copies:
        copy.wait()
    so_ref, sp_ref, io_ref, ip_ref, go_ref, gp_ref, keep_ref = held
    model_width = so_ref.shape[1]
    extra = out_ref.shape[1] - model_width
    experts = keep_ref.shape[1]
    states = jnp.concatenate(
        [so_ref[...].astype(jnp.float32), sp_ref[...].astype(jnp.float32)], axis=0
    )
    out_ref[:, :model_width] = normalize_rows(states).astype(jnp.bfloat16)
    dense_orig = dense_weights(io_ref[...], go_ref[...], experts)
    dense_pruned = dense_weights(ip_ref[...], gp_ref[...], experts)
    dense_pruned = dense_pruned * keep_ref[...].astype(jnp.float32)
    dense = jnp.concatenate([dense_orig, dense_pruned], axis=0)
    high = dense.astype(jnp.bfloat16)
    low = (dense - high.astype(jnp.float32)).astype(jnp.bfloat16)
    source = lax.broadcasted_iota(jnp.int32, (experts, extra), 0)
    lane = lax.broadcasted_iota(jnp.int32, (experts, extra), 1)
    out_ref[:, model_width:] = (
        jnp.dot(
            high,
            (lane == source).astype(jnp.float32).astype(jnp.bfloat16),
            preferred_element_type=jnp.float32,
        )
        + jnp.dot(
            low,
            (lane == source + experts).astype(jnp.float32).astype(jnp.bfloat16),
            preferred_element_type=jnp.float32,
        )
    ).astype(jnp.bfloat16)


def stage_kernel(count, *refs):
    sources, targets, sems = refs[:count], refs[count : 2 * count], refs[2 * count]
    copies = [
        pltpu.make_async_copy(source, target, sems.at[place])
        for place, (source, target) in enumerate(zip(sources, targets))
    ]
    for copy in copies:
        copy.start()
    for copy in copies:
        copy.wait()


def stage(arrays):
    return run_kernel(
        functools.partial(stage_kernel, len(arrays)),
        [pltpu.VMEM(value.shape, value.dtype) for value in arrays],
        arrays,
        [pltpu.SemaphoreType.DMA((len(arrays),))],
        space=pl.ANY,
    )


def after(value, *awaited):
    return lax.optimization_barrier((value, awaited))[0]


def join_kernel(*refs):
    part_refs, out_ref = refs[:-1], refs[-1]
    rows = part_refs[0].shape[0]
    for place, part_ref in enumerate(part_refs):
        out_ref[place * rows : (place + 1) * rows, :] = part_ref[...]


def join_rows(parts):
    rows, columns = parts[0].shape
    return run_kernel(join_kernel, like(len(parts) * rows, columns), parts)


def expert_kernel(experts, row_count, sizes, *refs):
    row_refs, refs = refs[:row_count], refs[row_count:]
    in_refs, out_refs, refs = refs[:SPLIT], refs[SPLIT : 2 * SPLIT], refs[2 * SPLIT :]
    result_refs, (rows, hidden) = refs[: len(sizes)], refs[len(sizes) :]
    half, model_width = out_refs[0].shape
    expert = lax.axis_index("expert") // SPLIT
    weights = []
    filled = 0
    for row_ref in row_refs:
        size = row_ref.shape[0]
        rows[filled : filled + size, :] = row_ref[:, :model_width]
        filled += size
        extra = row_ref[:, model_width:].astype(jnp.float32)
        lane = lax.broadcasted_iota(jnp.int32, extra.shape, 1)
        mine = jnp.logical_or(lane == expert, lane == expert + experts)
        weights.append(jnp.sum(jnp.where(mine, extra, 0.0), axis=1, keepdims=True))
    weight = jnp.concatenate(weights, axis=0)
    for place, in_ref in enumerate(in_refs):
        both = jnp.dot(rows[...], in_ref[...], preferred_element_type=jnp.float32)
        gate, up = both[:, :half], both[:, half:]
        hidden[:, place * half : (place + 1) * half] = (
            gate / (1.0 + jnp.exp(-gate)) * up
        ).astype(jnp.bfloat16)
    step = min(512, model_width)
    for start in range(0, model_width, step):
        value = sum(
            jnp.dot(
                hidden[:, place * half : (place + 1) * half],
                out_ref[:, start : start + step],
                preferred_element_type=jnp.float32,
            )
            for place, out_ref in enumerate(out_refs)
        )
        value = (value * weight).astype(jnp.bfloat16)
        filled = 0
        for size, result_ref in zip(sizes, result_refs):
            result_ref[:, start : start + step] = value[filled : filled + size]
            filled += size


def run_expert(experts, row_arrays, weights, sizes):
    total = sum(array.shape[0] for array in row_arrays)
    half, model_width = weights[-1].shape
    return run_kernel(
        functools.partial(expert_kernel, experts, len(row_arrays), sizes),
        [like(size, model_width) for size in sizes],
        list(row_arrays) + list(weights),
        [
            pltpu.VMEM((total, model_width), jnp.bfloat16),
            pltpu.VMEM((total, SPLIT * half), jnp.bfloat16),
        ],
        limit=24,
    )


def plane_kernel(count, *refs):
    part_refs, out_refs = refs[:count], refs[count:]
    rows = out_refs[0].shape[0]
    for place, out_ref in enumerate(out_refs):
        out_ref[...] = sum(
            ref[place * rows : (place + 1) * rows, :].astype(jnp.float32) for ref in part_refs
        ).astype(out_ref.dtype)


def final_kernel(parts, factor, *refs):
    part_refs, refs = refs[:parts], refs[parts:]
    ids_ref, gates_ref, orig_ref, pruned_ref, terms_ref, *value_refs = refs
    tok_rows = orig_ref.shape[0]
    total = sum(ref[...].astype(jnp.float32) for ref in part_refs)
    for value_ref in value_refs:
        value_ref[...] = total
    value_orig, value_pruned = total[:tok_rows], total[tok_rows:]
    orig_ref[...] = value_orig.astype(jnp.bfloat16)
    pruned_ref[...] = value_pruned.astype(jnp.bfloat16)
    differ = value_orig - value_pruned
    errors = jnp.mean(differ * differ, axis=1, keepdims=True)
    experts = terms_ref.shape[1]
    dense = dense_weights(ids_ref[...], gates_ref[...], experts)
    terms = factor * jnp.sum(dense * errors, axis=0, keepdims=True)
    terms_ref[...] = jnp.broadcast_to(terms, terms_ref.shape)


def add_kernel(parts_ref, out_ref):
    out_ref[...] = jnp.sum(parts_ref[...], axis=0, keepdims=True)


def on_device(
    states_orig,
    states_pruned,
    ids_orig,
    ids_pruned,
    gates_orig,
    gates_pruned,
    keep_mask,
    w_in,
    w_out,
):
    devices = lax.axis_size("expert")
    section_count = lax.axis_size("section")
    section_index = lax.axis_index("section")
    micro_count, tok_rows, model_width = states_orig.shape
    experts = keep_mask.shape[1]
    top_count = ids_orig.shape[-1]
    loss_factor = experts / (top_count * micro_count * tok_rows * devices)
    extra = -(-2 * experts // LANES) * LANES
    rows = 2 * tok_rows
    chips = devices // SPLIT
    inner = min(4, chips)
    outer = chips // inner
    inner_masks = [SPLIT * i for i in range(1, inner)]
    layer_mask = lambda j: SPLIT * inner * j
    nearer = list(range(1, outer // 2 + 1))
    streams = [[j for j in range(outer) if j not in nearer], nearer]
    own_in, own_out = w_in[0, 0], w_out[0, 0]
    other_out, other_in = exclusive(own_out, 1), exclusive(own_in, 1)

    step_count = micro_count + section_count - 1
    carry = jnp.zeros((2, tok_rows, model_width), jnp.bfloat16)
    moe_orig = jnp.zeros((micro_count, tok_rows, model_width), jnp.bfloat16)
    moe_pruned = moe_orig
    terms = jnp.zeros((devices, experts), jnp.float32)
    for tick in range(step_count):
        if section_count == 1:
            position = tick
            item = lambda buffer: buffer[position]
        else:
            position = jnp.clip(tick - section_index, 0, micro_count - 1)
            active = jnp.logical_and(
                tick - section_index >= 0, tick - section_index < micro_count
            )
            item = lambda buffer: lax.dynamic_index_in_dim(buffer, position, 0, keepdims=False)
        fresh = min(tick, micro_count - 1)
        state_orig, state_pruned = states_orig[fresh], states_pruned[fresh]
        if section_count > 1:
            state_orig = jnp.where(section_index == 0, state_orig, carry[0])
            state_pruned = jnp.where(section_index == 0, state_pruned, carry[1])
        picked_orig, weight_orig = item(ids_orig[0]), item(gates_orig[0])
        operands = [
            state_orig,
            state_pruned,
            picked_orig,
            item(ids_pruned[0]),
            weight_orig,
            item(gates_pruned[0]),
            keep_mask,
        ]
        packed = run_kernel(
            functools.partial(pack_kernel, len(operands)),
            like(rows, model_width + extra),
            [in_hbm(value) for value in operands],
            [pltpu.VMEM(value.shape, value.dtype) for value in operands]
            + [pltpu.SemaphoreType.DMA((len(operands),))],
            space=pl.ANY,
        )
        column = {0: packed}
        for j in streams[1][::-1] + streams[0][1:]:
            column[j] = exclusive(packed, layer_mask(j))
        if tick == 0:
            own = stage([in_hbm(own_in), in_hbm(own_out)])
            weights = [own[0], other_in, own[1], other_out]
        blocks = []
        for stream, layers in enumerate(streams):
            joined = join_rows([column[j] for j in layers])
            joined = after(joined, own if stream else (other_in, other_out))
            block = [joined]
            for mask in inner_masks:
                block.append(exclusive(joined, mask))
            blocks.append(block)
        summed = []
        for stream, layers in enumerate(streams):
            partial = run_expert(
                experts, blocks[stream], weights, [len(layers) * rows] * inner
            )
            returned = [partial[0]] + [
                exclusive(part, mask) for part, mask in zip(partial[1:], inner_masks)
            ]
            outs = [like(rows, model_width)] * len(layers)
            if stream == 0:
                outs[0] = like(rows, model_width, jnp.float32)
            sums = run_kernel(functools.partial(plane_kernel, inner), outs, returned)
            for j, value in list(zip(layers, sums))[::-1]:
                summed.append(exclusive(value, layer_mask(j)) if j else value)
        round_orig, round_pruned, tick_terms, *moe = run_kernel(
            functools.partial(final_kernel, outer, loss_factor),
            [like(tok_rows, model_width)] * 2
            + [like(devices, experts, jnp.float32)]
            + [like(rows, model_width, jnp.float32)] * (section_count > 1),
            summed + [picked_orig, weight_orig],
        )
        if section_count > 1:
            tick_terms = jnp.where(active, tick_terms, 0.0)
            round_orig = jnp.where(active, round_orig, item(moe_orig))
            round_pruned = jnp.where(active, round_pruned, item(moe_pruned))
        terms = tick_terms if tick == 0 else terms + tick_terms
        moe_orig = lax.dynamic_update_index_in_dim(moe_orig, round_orig, position, 0)
        moe_pruned = lax.dynamic_update_index_in_dim(moe_pruned, round_pruned, position, 0)
        if tick + 1 < step_count and section_count > 1:
            state = jnp.stack([state_orig, state_pruned]).astype(jnp.float32)
            following = (state + moe[0].reshape(state.shape)).astype(jnp.bfloat16)
            onward = [(i, i + 1) for i in range(section_count - 1)]
            carry = lax.ppermute(following, "section", onward)
    shared = lax.all_to_all(terms, "expert", split_axis=0, concat_axis=0, tiled=True)
    loss = run_kernel(add_kernel, like(1, experts, jnp.float32), [shared])
    return (moe_orig[None], moe_pruned[None], loss)


def solution(mesh):
    return jax.shard_map(
        on_device,
        mesh=mesh,
        in_specs=(
            P(None, "expert", None),
            P(None, "expert", None),
            P("section", None, "expert", None),
            P("section", None, "expert", None),
            P("section", None, "expert", None),
            P("section", None, "expert", None),
            P("section", None),
            P("section", "expert", None, None),
            P("section", "expert", None, None),
        ),
        out_specs=(
            P("section", None, "expert", None),
            P("section", None, "expert", None),
            P("section", None),
        ),
        check_vma=False,
    )
```

```python
import functools

import jax
import jax.numpy as jnp
from jax import lax
from jax.experimental import pallas as pl
from jax.experimental.pallas import tpu as pltpu
from jax.sharding import PartitionSpec as P

SPLIT = 2
LANES = 128
MIB = 2**20


def run_kernel(body, outs, operands, scratch=(), limit=16, space=pltpu.VMEM):
    return pl.pallas_call(
        body,
        out_shape=outs,
        in_specs=[pl.BlockSpec(memory_space=space)] * len(operands),
        out_specs=jax.tree.map(lambda _: pl.BlockSpec(memory_space=pltpu.VMEM), outs),
        scratch_shapes=list(scratch),
        compiler_params=pltpu.CompilerParams(vmem_limit_bytes=limit * MIB),
    )(*operands)


def in_hbm(value):
    return pltpu.with_memory_space_constraint(value, pltpu.HBM)


def like(rows, columns, dtype=jnp.bfloat16):
    return jax.ShapeDtypeStruct((rows, columns), dtype)


def exclusive(value, mask):
    pairs = [(source, source ^ mask) for source in range(lax.axis_size("expert"))]
    return lax.ppermute(value, "expert", pairs)


def normalize_rows(values):
    factor = lax.rsqrt(jnp.mean(values * values, axis=-1, keepdims=True) + 1e-06)
    return values * factor


def dense_weights(picked, gates, experts):
    rows = picked.shape[0]
    label = lax.broadcasted_iota(jnp.int32, (rows, experts), 1)
    total = jnp.zeros((rows, experts), jnp.float32)
    for k in range(picked.shape[1]):
        total = total + jnp.where(picked[:, k : k + 1] == label, gates[:, k : k + 1], 0.0)
    return total


def pack_kernel(count, *refs):
    sources, out_ref, scratch = refs[:count], refs[count], refs[count + 1 :]
    held, sems = scratch[:count], scratch[count]
    copies = [
        pltpu.make_async_copy(source, target, sems.at[place])
        for place, (source, target) in enumerate(zip(sources, held))
    ]
    for copy in copies:
        copy.start()
    for copy in copies:
        copy.wait()
    so_ref, sp_ref, io_ref, ip_ref, go_ref, gp_ref, keep_ref = held
    model_width = so_ref.shape[1]
    extra = out_ref.shape[1] - model_width
    experts = keep_ref.shape[1]
    states = jnp.concatenate(
        [so_ref[...].astype(jnp.float32), sp_ref[...].astype(jnp.float32)], axis=0
    )
    out_ref[:, :model_width] = normalize_rows(states).astype(jnp.bfloat16)
    dense_orig = dense_weights(io_ref[...], go_ref[...], experts)
    dense_pruned = dense_weights(ip_ref[...], gp_ref[...], experts)
    dense_pruned = dense_pruned * keep_ref[...].astype(jnp.float32)
    dense = jnp.concatenate([dense_orig, dense_pruned], axis=0)
    high = dense.astype(jnp.bfloat16)
    low = (dense - high.astype(jnp.float32)).astype(jnp.bfloat16)
    source = lax.broadcasted_iota(jnp.int32, (experts, extra), 0)
    lane = lax.broadcasted_iota(jnp.int32, (experts, extra), 1)
    out_ref[:, model_width:] = (
        jnp.dot(
            high,
            (lane == source).astype(jnp.float32).astype(jnp.bfloat16),
            preferred_element_type=jnp.float32,
        )
        + jnp.dot(
            low,
            (lane == source + experts).astype(jnp.float32).astype(jnp.bfloat16),
            preferred_element_type=jnp.float32,
        )
    ).astype(jnp.bfloat16)


def stage_kernel(count, *refs):
    sources, targets, sems = refs[:count], refs[count : 2 * count], refs[2 * count]
    copies = [
        pltpu.make_async_copy(source, target, sems.at[place])
        for place, (source, target) in enumerate(zip(sources, targets))
    ]
    for copy in copies:
        copy.start()
    for copy in copies:
        copy.wait()


def stage(arrays):
    return run_kernel(
        functools.partial(stage_kernel, len(arrays)),
        [pltpu.VMEM(value.shape, value.dtype) for value in arrays],
        arrays,
        [pltpu.SemaphoreType.DMA((len(arrays),))],
        space=pl.ANY,
    )


def after(value, *awaited):
    return lax.optimization_barrier((value, awaited))[0]


def join_kernel(*refs):
    part_refs, out_ref = refs[:-1], refs[-1]
    rows = part_refs[0].shape[0]
    for place, part_ref in enumerate(part_refs):
        out_ref[place * rows : (place + 1) * rows, :] = part_ref[...]


def join_rows(parts):
    rows, columns = parts[0].shape
    return run_kernel(join_kernel, like(len(parts) * rows, columns), parts)


def expert_kernel(experts, row_count, sizes, *refs):
    row_refs, refs = refs[:row_count], refs[row_count:]
    in_refs, out_refs, refs = refs[:SPLIT], refs[SPLIT : 2 * SPLIT], refs[2 * SPLIT :]
    result_refs, (rows, hidden) = refs[: len(sizes)], refs[len(sizes) :]
    half, model_width = out_refs[0].shape
    expert = lax.axis_index("expert") // SPLIT
    weights = []
    filled = 0
    for row_ref in row_refs:
        size = row_ref.shape[0]
        rows[filled : filled + size, :] = row_ref[:, :model_width]
        filled += size
        extra = row_ref[:, model_width:].astype(jnp.float32)
        lane = lax.broadcasted_iota(jnp.int32, extra.shape, 1)
        mine = jnp.logical_or(lane == expert, lane == expert + experts)
        weights.append(jnp.sum(jnp.where(mine, extra, 0.0), axis=1, keepdims=True))
    weight = jnp.concatenate(weights, axis=0)
    for place, in_ref in enumerate(in_refs):
        both = jnp.dot(rows[...], in_ref[...], preferred_element_type=jnp.float32)
        gate, up = both[:, :half], both[:, half:]
        hidden[:, place * half : (place + 1) * half] = (
            gate / (1.0 + jnp.exp(-gate)) * up
        ).astype(jnp.bfloat16)
    step = min(512, model_width)
    for start in range(0, model_width, step):
        value = sum(
            jnp.dot(
                hidden[:, place * half : (place + 1) * half],
                out_ref[:, start : start + step],
                preferred_element_type=jnp.float32,
            )
            for place, out_ref in enumerate(out_refs)
        )
        value = (value * weight).astype(jnp.bfloat16)
        filled = 0
        for size, result_ref in zip(sizes, result_refs):
            result_ref[:, start : start + step] = value[filled : filled + size]
            filled += size


def run_expert(experts, row_arrays, weights, sizes):
    total = sum(array.shape[0] for array in row_arrays)
    half, model_width = weights[-1].shape
    return run_kernel(
        functools.partial(expert_kernel, experts, len(row_arrays), sizes),
        [like(size, model_width) for size in sizes],
        list(row_arrays) + list(weights),
        [
            pltpu.VMEM((total, model_width), jnp.bfloat16),
            pltpu.VMEM((total, SPLIT * half), jnp.bfloat16),
        ],
        limit=24,
    )


def plane_kernel(count, *refs):
    part_refs, out_refs = refs[:count], refs[count:]
    rows = out_refs[0].shape[0]
    for place, out_ref in enumerate(out_refs):
        out_ref[...] = sum(
            ref[place * rows : (place + 1) * rows, :].astype(jnp.float32) for ref in part_refs
        ).astype(out_ref.dtype)


def final_kernel(parts, factor, *refs):
    part_refs, refs = refs[:parts], refs[parts:]
    ids_ref, gates_ref, orig_ref, pruned_ref, terms_ref, *value_refs = refs
    tok_rows = orig_ref.shape[0]
    total = sum(ref[...].astype(jnp.float32) for ref in part_refs)
    for value_ref in value_refs:
        value_ref[...] = total
    value_orig, value_pruned = total[:tok_rows], total[tok_rows:]
    orig_ref[...] = value_orig.astype(jnp.bfloat16)
    pruned_ref[...] = value_pruned.astype(jnp.bfloat16)
    differ = value_orig - value_pruned
    errors = jnp.mean(differ * differ, axis=1, keepdims=True)
    experts = terms_ref.shape[1]
    dense = dense_weights(ids_ref[...], gates_ref[...], experts)
    terms = factor * jnp.sum(dense * errors, axis=0, keepdims=True)
    terms_ref[...] = jnp.broadcast_to(terms, terms_ref.shape)


def add_kernel(parts_ref, out_ref):
    out_ref[...] = jnp.sum(parts_ref[...], axis=0, keepdims=True)


def on_device(
    states_orig,
    states_pruned,
    ids_orig,
    ids_pruned,
    gates_orig,
    gates_pruned,
    keep_mask,
    w_in,
    w_out,
):
    devices = lax.axis_size("expert")
    section_count = lax.axis_size("section")
    section_index = lax.axis_index("section")
    micro_count, tok_rows, model_width = states_orig.shape
    experts = keep_mask.shape[1]
    top_count = ids_orig.shape[-1]
    loss_factor = experts / (top_count * micro_count * tok_rows * devices)
    extra = -(-2 * experts // LANES) * LANES
    rows = 2 * tok_rows
    chips = devices // SPLIT
    inner = min(4, chips)
    outer = chips // inner
    inner_masks = [SPLIT * i for i in range(1, inner)]
    layer_mask = lambda j: SPLIT * inner * j
    nearer = list(range(1, outer // 2 + 1))
    streams = [[j for j in range(outer) if j not in nearer], nearer]
    own_in, own_out = w_in[0, 0], w_out[0, 0]
    other_out, other_in = exclusive(own_out, 1), exclusive(own_in, 1)

    step_count = micro_count + section_count - 1
    carry = jnp.zeros((2, tok_rows, model_width), jnp.bfloat16)
    moe_orig = jnp.zeros((micro_count, tok_rows, model_width), jnp.bfloat16)
    moe_pruned = moe_orig
    terms = jnp.zeros((devices, experts), jnp.float32)
    for tick in range(step_count):
        if section_count == 1:
            position = tick
            item = lambda buffer: buffer[position]
        else:
            position = jnp.clip(tick - section_index, 0, micro_count - 1)
            active = jnp.logical_and(
                tick - section_index >= 0, tick - section_index < micro_count
            )
            item = lambda buffer: lax.dynamic_index_in_dim(buffer, position, 0, keepdims=False)
        fresh = min(tick, micro_count - 1)
        state_orig, state_pruned = states_orig[fresh], states_pruned[fresh]
        if section_count > 1:
            state_orig = jnp.where(section_index == 0, state_orig, carry[0])
            state_pruned = jnp.where(section_index == 0, state_pruned, carry[1])
        picked_orig, weight_orig = item(ids_orig[0]), item(gates_orig[0])
        operands = [
            state_orig,
            state_pruned,
            picked_orig,
            item(ids_pruned[0]),
            weight_orig,
            item(gates_pruned[0]),
            keep_mask,
        ]
        packed = run_kernel(
            functools.partial(pack_kernel, len(operands)),
            like(rows, model_width + extra),
            [in_hbm(value) for value in operands],
            [pltpu.VMEM(value.shape, value.dtype) for value in operands]
            + [pltpu.SemaphoreType.DMA((len(operands),))],
            space=pl.ANY,
        )
        column = {0: packed}
        for j in streams[1][::-1] + streams[0][1:]:
            column[j] = exclusive(packed, layer_mask(j))
        if tick == 0:
            own = stage([in_hbm(own_in), in_hbm(own_out)])
            weights = [own[0], other_in, own[1], other_out]
        blocks = []
        for stream, layers in enumerate(streams):
            joined = join_rows([column[j] for j in layers])
            if stream == 1:
                joined = after(joined, own, other_in, other_out)
            block = [joined]
            for mask in inner_masks:
                block.append(exclusive(joined, mask))
            blocks.append(block)
        summed = []
        for stream, layers in enumerate(streams):
            partial = run_expert(
                experts, blocks[stream], weights, [len(layers) * rows] * inner
            )
            returned = [partial[0]] + [
                exclusive(part, mask) for part, mask in zip(partial[1:], inner_masks)
            ]
            outs = [like(rows, model_width)] * len(layers)
            if stream == 0:
                outs[0] = like(rows, model_width, jnp.float32)
            sums = run_kernel(functools.partial(plane_kernel, inner), outs, returned)
            for j, value in list(zip(layers, sums))[::-1]:
                summed.append(exclusive(value, layer_mask(j)) if j else value)
        round_orig, round_pruned, tick_terms, *moe = run_kernel(
            functools.partial(final_kernel, outer, loss_factor),
            [like(tok_rows, model_width)] * 2
            + [like(devices, experts, jnp.float32)]
            + [like(rows, model_width, jnp.float32)] * (section_count > 1),
            summed + [picked_orig, weight_orig],
        )
        if section_count > 1:
            tick_terms = jnp.where(active, tick_terms, 0.0)
            round_orig = jnp.where(active, round_orig, item(moe_orig))
            round_pruned = jnp.where(active, round_pruned, item(moe_pruned))
        terms = tick_terms if tick == 0 else terms + tick_terms
        moe_orig = lax.dynamic_update_index_in_dim(moe_orig, round_orig, position, 0)
        moe_pruned = lax.dynamic_update_index_in_dim(moe_pruned, round_pruned, position, 0)
        if tick + 1 < step_count and section_count > 1:
            state = jnp.stack([state_orig, state_pruned]).astype(jnp.float32)
            following = (state + moe[0].reshape(state.shape)).astype(jnp.bfloat16)
            onward = [(i, i + 1) for i in range(section_count - 1)]
            carry = lax.ppermute(following, "section", onward)
    shared = lax.all_to_all(terms, "expert", split_axis=0, concat_axis=0, tiled=True)
    loss = run_kernel(add_kernel, like(1, experts, jnp.float32), [shared])
    return (moe_orig[None], moe_pruned[None], loss)


def solution(mesh):
    return jax.shard_map(
        on_device,
        mesh=mesh,
        in_specs=(
            P(None, "expert", None),
            P(None, "expert", None),
            P("section", None, "expert", None),
            P("section", None, "expert", None),
            P("section", None, "expert", None),
            P("section", None, "expert", None),
            P("section", None),
            P("section", "expert", None, None),
            P("section", "expert", None, None),
        ),
        out_specs=(
            P("section", None, "expert", None),
            P("section", None, "expert", None),
            P("section", None),
        ),
        check_vma=False,
    )
```

```python
import functools

import jax
import jax.numpy as jnp
from jax import lax
from jax.experimental import pallas as pl
from jax.experimental.pallas import tpu as pltpu
from jax.sharding import PartitionSpec as P

SPLIT = 2
LANES = 128
MIB = 2**20


def run_kernel(body, outs, operands, scratch=(), limit=16, space=pltpu.VMEM):
    return pl.pallas_call(
        body,
        out_shape=outs,
        in_specs=[pl.BlockSpec(memory_space=space)] * len(operands),
        out_specs=jax.tree.map(lambda _: pl.BlockSpec(memory_space=pltpu.VMEM), outs),
        scratch_shapes=list(scratch),
        compiler_params=pltpu.CompilerParams(vmem_limit_bytes=limit * MIB),
    )(*operands)


def in_hbm(value):
    return pltpu.with_memory_space_constraint(value, pltpu.HBM)


def like(rows, columns, dtype=jnp.bfloat16):
    return jax.ShapeDtypeStruct((rows, columns), dtype)


def exclusive(value, mask):
    pairs = [(source, source ^ mask) for source in range(lax.axis_size("expert"))]
    return lax.ppermute(value, "expert", pairs)


def normalize_rows(values):
    factor = lax.rsqrt(jnp.mean(values * values, axis=-1, keepdims=True) + 1e-06)
    return values * factor


def dense_weights(picked, gates, experts):
    rows = picked.shape[0]
    label = lax.broadcasted_iota(jnp.int32, (rows, experts), 1)
    total = jnp.zeros((rows, experts), jnp.float32)
    for k in range(picked.shape[1]):
        total = total + jnp.where(picked[:, k : k + 1] == label, gates[:, k : k + 1], 0.0)
    return total


def pack_kernel(count, *refs):
    sources, out_ref, scratch = refs[:count], refs[count], refs[count + 1 :]
    held, sems = scratch[:count], scratch[count]
    copies = [
        pltpu.make_async_copy(source, target, sems.at[place])
        for place, (source, target) in enumerate(zip(sources, held))
    ]
    for copy in copies:
        copy.start()
    for copy in copies:
        copy.wait()
    so_ref, sp_ref, io_ref, ip_ref, go_ref, gp_ref, keep_ref = held
    model_width = so_ref.shape[1]
    extra = out_ref.shape[1] - model_width
    experts = keep_ref.shape[1]
    states = jnp.concatenate(
        [so_ref[...].astype(jnp.float32), sp_ref[...].astype(jnp.float32)], axis=0
    )
    out_ref[:, :model_width] = normalize_rows(states).astype(jnp.bfloat16)
    dense_orig = dense_weights(io_ref[...], go_ref[...], experts)
    dense_pruned = dense_weights(ip_ref[...], gp_ref[...], experts)
    dense_pruned = dense_pruned * keep_ref[...].astype(jnp.float32)
    dense = jnp.concatenate([dense_orig, dense_pruned], axis=0)
    high = dense.astype(jnp.bfloat16)
    low = (dense - high.astype(jnp.float32)).astype(jnp.bfloat16)
    source = lax.broadcasted_iota(jnp.int32, (experts, extra), 0)
    lane = lax.broadcasted_iota(jnp.int32, (experts, extra), 1)
    out_ref[:, model_width:] = (
        jnp.dot(
            high,
            (lane == source).astype(jnp.float32).astype(jnp.bfloat16),
            preferred_element_type=jnp.float32,
        )
        + jnp.dot(
            low,
            (lane == source + experts).astype(jnp.float32).astype(jnp.bfloat16),
            preferred_element_type=jnp.float32,
        )
    ).astype(jnp.bfloat16)


def stage_kernel(count, *refs):
    sources, targets, sems = refs[:count], refs[count : 2 * count], refs[2 * count]
    copies = [
        pltpu.make_async_copy(source, target, sems.at[place])
        for place, (source, target) in enumerate(zip(sources, targets))
    ]
    for copy in copies:
        copy.start()
    for copy in copies:
        copy.wait()


def stage(arrays):
    return run_kernel(
        functools.partial(stage_kernel, len(arrays)),
        [pltpu.VMEM(value.shape, value.dtype) for value in arrays],
        arrays,
        [pltpu.SemaphoreType.DMA((len(arrays),))],
        space=pl.ANY,
    )


def after(value, *awaited):
    return lax.optimization_barrier((value, awaited))[0]


def join_kernel(*refs):
    part_refs, out_ref = refs[:-1], refs[-1]
    rows = part_refs[0].shape[0]
    for place, part_ref in enumerate(part_refs):
        out_ref[place * rows : (place + 1) * rows, :] = part_ref[...]


def join_rows(parts):
    rows, columns = parts[0].shape
    return run_kernel(join_kernel, like(len(parts) * rows, columns), parts)


def expert_kernel(experts, row_count, sizes, *refs):
    row_refs, refs = refs[:row_count], refs[row_count:]
    in_refs, out_refs, refs = refs[:SPLIT], refs[SPLIT : 2 * SPLIT], refs[2 * SPLIT :]
    result_refs, (rows, hidden) = refs[: len(sizes)], refs[len(sizes) :]
    half, model_width = out_refs[0].shape
    expert = lax.axis_index("expert") // SPLIT
    weights = []
    filled = 0
    for row_ref in row_refs:
        size = row_ref.shape[0]
        rows[filled : filled + size, :] = row_ref[:, :model_width]
        filled += size
        extra = row_ref[:, model_width:].astype(jnp.float32)
        lane = lax.broadcasted_iota(jnp.int32, extra.shape, 1)
        mine = jnp.logical_or(lane == expert, lane == expert + experts)
        weights.append(jnp.sum(jnp.where(mine, extra, 0.0), axis=1, keepdims=True))
    weight = jnp.concatenate(weights, axis=0)
    for place, in_ref in enumerate(in_refs):
        both = jnp.dot(rows[...], in_ref[...], preferred_element_type=jnp.float32)
        gate, up = both[:, :half], both[:, half:]
        hidden[:, place * half : (place + 1) * half] = (
            gate / (1.0 + jnp.exp(-gate)) * up
        ).astype(jnp.bfloat16)
    step = min(512, model_width)
    for start in range(0, model_width, step):
        value = sum(
            jnp.dot(
                hidden[:, place * half : (place + 1) * half],
                out_ref[:, start : start + step],
                preferred_element_type=jnp.float32,
            )
            for place, out_ref in enumerate(out_refs)
        )
        value = (value * weight).astype(jnp.bfloat16)
        filled = 0
        for size, result_ref in zip(sizes, result_refs):
            result_ref[:, start : start + step] = value[filled : filled + size]
            filled += size


def run_expert(experts, row_arrays, weights, sizes):
    total = sum(array.shape[0] for array in row_arrays)
    half, model_width = weights[-1].shape
    return run_kernel(
        functools.partial(expert_kernel, experts, len(row_arrays), sizes),
        [like(size, model_width) for size in sizes],
        list(row_arrays) + list(weights),
        [
            pltpu.VMEM((total, model_width), jnp.bfloat16),
            pltpu.VMEM((total, SPLIT * half), jnp.bfloat16),
        ],
        limit=24,
    )


def plane_kernel(count, *refs):
    part_refs, out_refs = refs[:count], refs[count:]
    rows = out_refs[0].shape[0]
    for place, out_ref in enumerate(out_refs):
        out_ref[...] = sum(
            ref[place * rows : (place + 1) * rows, :].astype(jnp.float32) for ref in part_refs
        ).astype(out_ref.dtype)


def final_kernel(parts, factor, *refs):
    part_refs, refs = refs[:parts], refs[parts:]
    ids_ref, gates_ref, orig_ref, pruned_ref, terms_ref, *value_refs = refs
    tok_rows = orig_ref.shape[0]
    total = sum(ref[...].astype(jnp.float32) for ref in part_refs)
    for value_ref in value_refs:
        value_ref[...] = total
    value_orig, value_pruned = total[:tok_rows], total[tok_rows:]
    orig_ref[...] = value_orig.astype(jnp.bfloat16)
    pruned_ref[...] = value_pruned.astype(jnp.bfloat16)
    differ = value_orig - value_pruned
    errors = jnp.mean(differ * differ, axis=1, keepdims=True)
    experts = terms_ref.shape[1]
    dense = dense_weights(ids_ref[...], gates_ref[...], experts)
    terms = factor * jnp.sum(dense * errors, axis=0, keepdims=True)
    terms_ref[...] = jnp.broadcast_to(terms, terms_ref.shape)


def add_kernel(parts_ref, out_ref):
    out_ref[...] = jnp.sum(parts_ref[...], axis=0, keepdims=True)


def on_device(
    states_orig,
    states_pruned,
    ids_orig,
    ids_pruned,
    gates_orig,
    gates_pruned,
    keep_mask,
    w_in,
    w_out,
):
    devices = lax.axis_size("expert")
    section_count = lax.axis_size("section")
    section_index = lax.axis_index("section")
    micro_count, tok_rows, model_width = states_orig.shape
    experts = keep_mask.shape[1]
    top_count = ids_orig.shape[-1]
    loss_factor = experts / (top_count * micro_count * tok_rows * devices)
    extra = -(-2 * experts // LANES) * LANES
    rows = 2 * tok_rows
    chips = devices // SPLIT
    inner = min(4, chips)
    outer = chips // inner
    inner_masks = [SPLIT * i for i in range(1, inner)]
    layer_mask = lambda j: SPLIT * inner * j
    nearer = list(range(1, outer // 2 + 1))
    streams = [[j for j in range(outer) if j not in nearer], nearer]
    own_in, own_out = w_in[0, 0], w_out[0, 0]
    other_out, other_in = exclusive(own_out, 1), exclusive(own_in, 1)

    step_count = micro_count + section_count - 1
    carry = jnp.zeros((2, tok_rows, model_width), jnp.bfloat16)
    moe_orig = jnp.zeros((micro_count, tok_rows, model_width), jnp.bfloat16)
    moe_pruned = moe_orig
    terms = jnp.zeros((devices, experts), jnp.float32)
    for tick in range(step_count):
        if section_count == 1:
            position = tick
            item = lambda buffer: buffer[position]
        else:
            position = jnp.clip(tick - section_index, 0, micro_count - 1)
            active = jnp.logical_and(
                tick - section_index >= 0, tick - section_index < micro_count
            )
            item = lambda buffer: lax.dynamic_index_in_dim(buffer, position, 0, keepdims=False)
        fresh = min(tick, micro_count - 1)
        state_orig, state_pruned = states_orig[fresh], states_pruned[fresh]
        if section_count > 1:
            state_orig = jnp.where(section_index == 0, state_orig, carry[0])
            state_pruned = jnp.where(section_index == 0, state_pruned, carry[1])
        picked_orig, weight_orig = item(ids_orig[0]), item(gates_orig[0])
        operands = [
            state_orig,
            state_pruned,
            picked_orig,
            item(ids_pruned[0]),
            weight_orig,
            item(gates_pruned[0]),
            keep_mask,
        ]
        packed = run_kernel(
            functools.partial(pack_kernel, len(operands)),
            like(rows, model_width + extra),
            [in_hbm(value) for value in operands],
            [pltpu.VMEM(value.shape, value.dtype) for value in operands]
            + [pltpu.SemaphoreType.DMA((len(operands),))],
            space=pl.ANY,
        )
        column = {0: packed}
        for j in streams[1][::-1] + streams[0][1:]:
            column[j] = exclusive(packed, layer_mask(j))
        if tick == 0:
            own = stage([in_hbm(own_in), in_hbm(own_out)])
            weights = [own[0], other_in, own[1], other_out]
        blocks = []
        for stream, layers in enumerate(streams):
            joined = join_rows([column[j] for j in layers])
            joined = after(joined, (other_in, other_out) if stream else own)
            block = [joined]
            for mask in inner_masks:
                block.append(exclusive(joined, mask))
            blocks.append(block)
        summed = []
        for stream, layers in enumerate(streams):
            partial = run_expert(
                experts, blocks[stream], weights, [len(layers) * rows] * inner
            )
            returned = [partial[0]] + [
                exclusive(part, mask) for part, mask in zip(partial[1:], inner_masks)
            ]
            outs = [like(rows, model_width)] * len(layers)
            if stream == 0:
                outs[0] = like(rows, model_width, jnp.float32)
            sums = run_kernel(functools.partial(plane_kernel, inner), outs, returned)
            for j, value in list(zip(layers, sums))[::-1]:
                summed.append(exclusive(value, layer_mask(j)) if j else value)
        round_orig, round_pruned, tick_terms, *moe = run_kernel(
            functools.partial(final_kernel, outer, loss_factor),
            [like(tok_rows, model_width)] * 2
            + [like(devices, experts, jnp.float32)]
            + [like(rows, model_width, jnp.float32)] * (section_count > 1),
            summed + [picked_orig, weight_orig],
        )
        if section_count > 1:
            tick_terms = jnp.where(active, tick_terms, 0.0)
            round_orig = jnp.where(active, round_orig, item(moe_orig))
            round_pruned = jnp.where(active, round_pruned, item(moe_pruned))
        terms = tick_terms if tick == 0 else terms + tick_terms
        moe_orig = lax.dynamic_update_index_in_dim(moe_orig, round_orig, position, 0)
        moe_pruned = lax.dynamic_update_index_in_dim(moe_pruned, round_pruned, position, 0)
        if tick + 1 < step_count and section_count > 1:
            state = jnp.stack([state_orig, state_pruned]).astype(jnp.float32)
            following = (state + moe[0].reshape(state.shape)).astype(jnp.bfloat16)
            onward = [(i, i + 1) for i in range(section_count - 1)]
            carry = lax.ppermute(following, "section", onward)
    shared = lax.all_to_all(terms, "expert", split_axis=0, concat_axis=0, tiled=True)
    loss = run_kernel(add_kernel, like(1, experts, jnp.float32), [shared])
    return (moe_orig[None], moe_pruned[None], loss)


def solution(mesh):
    return jax.shard_map(
        on_device,
        mesh=mesh,
        in_specs=(
            P(None, "expert", None),
            P(None, "expert", None),
            P("section", None, "expert", None),
            P("section", None, "expert", None),
            P("section", None, "expert", None),
            P("section", None, "expert", None),
            P("section", None),
            P("section", "expert", None, None),
            P("section", "expert", None, None),
        ),
        out_specs=(
            P("section", None, "expert", None),
            P("section", None, "expert", None),
            P("section", None),
        ),
        check_vma=False,
    )
```

```python
import functools

import jax
import jax.numpy as jnp
from jax import lax
from jax.experimental import pallas as pl
from jax.experimental.pallas import tpu as pltpu
from jax.sharding import PartitionSpec as P

SPLIT = 2
LANES = 128
MIB = 2**20


def run_kernel(body, outs, operands, scratch=(), limit=16, space=pltpu.VMEM):
    return pl.pallas_call(
        body,
        out_shape=outs,
        in_specs=[pl.BlockSpec(memory_space=space)] * len(operands),
        out_specs=jax.tree.map(lambda _: pl.BlockSpec(memory_space=pltpu.VMEM), outs),
        scratch_shapes=list(scratch),
        compiler_params=pltpu.CompilerParams(vmem_limit_bytes=limit * MIB),
    )(*operands)


def in_hbm(value):
    return pltpu.with_memory_space_constraint(value, pltpu.HBM)


def like(rows, columns, dtype=jnp.bfloat16):
    return jax.ShapeDtypeStruct((rows, columns), dtype)


def exclusive(value, mask):
    pairs = [(source, source ^ mask) for source in range(lax.axis_size("expert"))]
    return lax.ppermute(value, "expert", pairs)


def normalize_rows(values):
    factor = lax.rsqrt(jnp.mean(values * values, axis=-1, keepdims=True) + 1e-06)
    return values * factor


def dense_weights(picked, gates, experts):
    rows = picked.shape[0]
    label = lax.broadcasted_iota(jnp.int32, (rows, experts), 1)
    total = jnp.zeros((rows, experts), jnp.float32)
    for k in range(picked.shape[1]):
        total = total + jnp.where(picked[:, k : k + 1] == label, gates[:, k : k + 1], 0.0)
    return total


def pack_kernel(count, *refs):
    sources, out_ref, scratch = refs[:count], refs[count], refs[count + 1 :]
    held, sems = scratch[:count], scratch[count]
    copies = [
        pltpu.make_async_copy(source, target, sems.at[place])
        for place, (source, target) in enumerate(zip(sources, held))
    ]
    for copy in copies:
        copy.start()
    for copy in copies:
        copy.wait()
    so_ref, sp_ref, io_ref, ip_ref, go_ref, gp_ref, keep_ref = held
    model_width = so_ref.shape[1]
    extra = out_ref.shape[1] - model_width
    experts = keep_ref.shape[1]
    states = jnp.concatenate(
        [so_ref[...].astype(jnp.float32), sp_ref[...].astype(jnp.float32)], axis=0
    )
    out_ref[:, :model_width] = normalize_rows(states).astype(jnp.bfloat16)
    dense_orig = dense_weights(io_ref[...], go_ref[...], experts)
    dense_pruned = dense_weights(ip_ref[...], gp_ref[...], experts)
    dense_pruned = dense_pruned * keep_ref[...].astype(jnp.float32)
    dense = jnp.concatenate([dense_orig, dense_pruned], axis=0)
    high = dense.astype(jnp.bfloat16)
    low = (dense - high.astype(jnp.float32)).astype(jnp.bfloat16)
    source = lax.broadcasted_iota(jnp.int32, (experts, extra), 0)
    lane = lax.broadcasted_iota(jnp.int32, (experts, extra), 1)
    out_ref[:, model_width:] = (
        jnp.dot(
            high,
            (lane == source).astype(jnp.float32).astype(jnp.bfloat16),
            preferred_element_type=jnp.float32,
        )
        + jnp.dot(
            low,
            (lane == source + experts).astype(jnp.float32).astype(jnp.bfloat16),
            preferred_element_type=jnp.float32,
        )
    ).astype(jnp.bfloat16)


def stage_kernel(count, *refs):
    sources, targets, sems = refs[:count], refs[count : 2 * count], refs[2 * count]
    copies = [
        pltpu.make_async_copy(source, target, sems.at[place])
        for place, (source, target) in enumerate(zip(sources, targets))
    ]
    for copy in copies:
        copy.start()
    for copy in copies:
        copy.wait()


def stage(arrays):
    return run_kernel(
        functools.partial(stage_kernel, len(arrays)),
        [pltpu.VMEM(value.shape, value.dtype) for value in arrays],
        arrays,
        [pltpu.SemaphoreType.DMA((len(arrays),))],
        space=pl.ANY,
    )


def after(value, *awaited):
    return lax.optimization_barrier((value, awaited))[0]


def join_kernel(*refs):
    part_refs, out_ref = refs[:-1], refs[-1]
    rows = part_refs[0].shape[0]
    for place, part_ref in enumerate(part_refs):
        out_ref[place * rows : (place + 1) * rows, :] = part_ref[...]


def join_rows(parts):
    rows, columns = parts[0].shape
    return run_kernel(join_kernel, like(len(parts) * rows, columns), parts)


def expert_kernel(experts, row_count, sizes, *refs):
    row_refs, refs = refs[:row_count], refs[row_count:]
    in_refs, out_refs, refs = refs[:SPLIT], refs[SPLIT : 2 * SPLIT], refs[2 * SPLIT :]
    result_refs, (rows, hidden) = refs[: len(sizes)], refs[len(sizes) :]
    half, model_width = out_refs[0].shape
    expert = lax.axis_index("expert") // SPLIT
    weights = []
    filled = 0
    for row_ref in row_refs:
        size = row_ref.shape[0]
        rows[filled : filled + size, :] = row_ref[:, :model_width]
        filled += size
        extra = row_ref[:, model_width:].astype(jnp.float32)
        lane = lax.broadcasted_iota(jnp.int32, extra.shape, 1)
        mine = jnp.logical_or(lane == expert, lane == expert + experts)
        weights.append(jnp.sum(jnp.where(mine, extra, 0.0), axis=1, keepdims=True))
    weight = jnp.concatenate(weights, axis=0)
    for place, in_ref in enumerate(in_refs):
        both = jnp.dot(rows[...], in_ref[...], preferred_element_type=jnp.float32)
        gate, up = both[:, :half], both[:, half:]
        hidden[:, place * half : (place + 1) * half] = (
            gate / (1.0 + jnp.exp(-gate)) * up
        ).astype(jnp.bfloat16)
    step = min(512, model_width)
    for start in range(0, model_width, step):
        value = sum(
            jnp.dot(
                hidden[:, place * half : (place + 1) * half],
                out_ref[:, start : start + step],
                preferred_element_type=jnp.float32,
            )
            for place, out_ref in enumerate(out_refs)
        )
        value = (value * weight).astype(jnp.bfloat16)
        filled = 0
        for size, result_ref in zip(sizes, result_refs):
            result_ref[:, start : start + step] = value[filled : filled + size]
            filled += size


def run_expert(experts, row_arrays, weights, sizes):
    total = sum(array.shape[0] for array in row_arrays)
    half, model_width = weights[-1].shape
    return run_kernel(
        functools.partial(expert_kernel, experts, len(row_arrays), sizes),
        [like(size, model_width) for size in sizes],
        list(row_arrays) + list(weights),
        [
            pltpu.VMEM((total, model_width), jnp.bfloat16),
            pltpu.VMEM((total, SPLIT * half), jnp.bfloat16),
        ],
        limit=24,
    )


def plane_kernel(count, *refs):
    part_refs, out_refs = refs[:count], refs[count:]
    rows = out_refs[0].shape[0]
    for place, out_ref in enumerate(out_refs):
        out_ref[...] = sum(
            ref[place * rows : (place + 1) * rows, :].astype(jnp.float32) for ref in part_refs
        ).astype(out_ref.dtype)


def final_kernel(parts, factor, *refs):
    part_refs, refs = refs[:parts], refs[parts:]
    ids_ref, gates_ref, orig_ref, pruned_ref, terms_ref, *value_refs = refs
    tok_rows = orig_ref.shape[0]
    total = sum(ref[...].astype(jnp.float32) for ref in part_refs)
    for value_ref in value_refs:
        value_ref[...] = total
    value_orig, value_pruned = total[:tok_rows], total[tok_rows:]
    orig_ref[...] = value_orig.astype(jnp.bfloat16)
    pruned_ref[...] = value_pruned.astype(jnp.bfloat16)
    differ = value_orig - value_pruned
    errors = jnp.mean(differ * differ, axis=1, keepdims=True)
    experts = terms_ref.shape[1]
    dense = dense_weights(ids_ref[...], gates_ref[...], experts)
    terms = factor * jnp.sum(dense * errors, axis=0, keepdims=True)
    terms_ref[...] = jnp.broadcast_to(terms, terms_ref.shape)


def add_kernel(parts_ref, out_ref):
    out_ref[...] = jnp.sum(parts_ref[...], axis=0, keepdims=True)


def on_device(
    states_orig,
    states_pruned,
    ids_orig,
    ids_pruned,
    gates_orig,
    gates_pruned,
    keep_mask,
    w_in,
    w_out,
):
    devices = lax.axis_size("expert")
    section_count = lax.axis_size("section")
    section_index = lax.axis_index("section")
    micro_count, tok_rows, model_width = states_orig.shape
    experts = keep_mask.shape[1]
    top_count = ids_orig.shape[-1]
    loss_factor = experts / (top_count * micro_count * tok_rows * devices)
    extra = -(-2 * experts // LANES) * LANES
    rows = 2 * tok_rows
    chips = devices // SPLIT
    inner = min(4, chips)
    outer = chips // inner
    inner_masks = [SPLIT * i for i in range(1, inner)]
    layer_mask = lambda j: SPLIT * inner * j
    nearer = list(range(1, outer // 2 + 1))
    streams = [[j for j in range(outer) if j not in nearer], nearer]
    own_in, own_out = w_in[0, 0], w_out[0, 0]
    other_out, other_in = exclusive(own_out, 1), exclusive(own_in, 1)

    step_count = micro_count + section_count - 1
    carry = jnp.zeros((2, tok_rows, model_width), jnp.bfloat16)
    moe_orig = jnp.zeros((micro_count, tok_rows, model_width), jnp.bfloat16)
    moe_pruned = moe_orig
    terms = jnp.zeros((devices, experts), jnp.float32)
    for tick in range(step_count):
        if section_count == 1:
            position = tick
            item = lambda buffer: buffer[position]
        else:
            position = jnp.clip(tick - section_index, 0, micro_count - 1)
            active = jnp.logical_and(
                tick - section_index >= 0, tick - section_index < micro_count
            )
            item = lambda buffer: lax.dynamic_index_in_dim(buffer, position, 0, keepdims=False)
        fresh = min(tick, micro_count - 1)
        state_orig, state_pruned = states_orig[fresh], states_pruned[fresh]
        if section_count > 1:
            state_orig = jnp.where(section_index == 0, state_orig, carry[0])
            state_pruned = jnp.where(section_index == 0, state_pruned, carry[1])
        picked_orig, weight_orig = item(ids_orig[0]), item(gates_orig[0])
        operands = [
            state_orig,
            state_pruned,
            picked_orig,
            item(ids_pruned[0]),
            weight_orig,
            item(gates_pruned[0]),
            keep_mask,
        ]
        packed = run_kernel(
            functools.partial(pack_kernel, len(operands)),
            like(rows, model_width + extra),
            [in_hbm(value) for value in operands],
            [pltpu.VMEM(value.shape, value.dtype) for value in operands]
            + [pltpu.SemaphoreType.DMA((len(operands),))],
            space=pl.ANY,
        )
        column = {0: packed}
        for j in streams[1][::-1] + streams[0][1:]:
            column[j] = exclusive(packed, layer_mask(j))
        if tick == 0:
            own = stage([in_hbm(own_in), in_hbm(own_out)])
            weights = [own[0], other_in, own[1], other_out]
        blocks = []
        for stream, layers in enumerate(streams):
            joined = join_rows([column[j] for j in layers])
            if stream == 1:
                joined = after(joined, other_in, other_out)
            block = [joined]
            for mask in inner_masks:
                block.append(exclusive(joined, mask))
            blocks.append(block)
        summed = []
        for stream, layers in enumerate(streams):
            partial = run_expert(
                experts, blocks[stream], weights, [len(layers) * rows] * inner
            )
            returned = [partial[0]] + [
                exclusive(part, mask) for part, mask in zip(partial[1:], inner_masks)
            ]
            outs = [like(rows, model_width)] * len(layers)
            if stream == 0:
                outs[0] = like(rows, model_width, jnp.float32)
            sums = run_kernel(functools.partial(plane_kernel, inner), outs, returned)
            for j, value in list(zip(layers, sums))[::-1]:
                summed.append(exclusive(value, layer_mask(j)) if j else value)
        round_orig, round_pruned, tick_terms, *moe = run_kernel(
            functools.partial(final_kernel, outer, loss_factor),
            [like(tok_rows, model_width)] * 2
            + [like(devices, experts, jnp.float32)]
            + [like(rows, model_width, jnp.float32)] * (section_count > 1),
            summed + [picked_orig, weight_orig],
        )
        if section_count > 1:
            tick_terms = jnp.where(active, tick_terms, 0.0)
            round_orig = jnp.where(active, round_orig, item(moe_orig))
            round_pruned = jnp.where(active, round_pruned, item(moe_pruned))
        terms = tick_terms if tick == 0 else terms + tick_terms
        moe_orig = lax.dynamic_update_index_in_dim(moe_orig, round_orig, position, 0)
        moe_pruned = lax.dynamic_update_index_in_dim(moe_pruned, round_pruned, position, 0)
        if tick + 1 < step_count and section_count > 1:
            state = jnp.stack([state_orig, state_pruned]).astype(jnp.float32)
            following = (state + moe[0].reshape(state.shape)).astype(jnp.bfloat16)
            onward = [(i, i + 1) for i in range(section_count - 1)]
            carry = lax.ppermute(following, "section", onward)
    shared = lax.all_to_all(terms, "expert", split_axis=0, concat_axis=0, tiled=True)
    loss = run_kernel(add_kernel, like(1, experts, jnp.float32), [shared])
    return (moe_orig[None], moe_pruned[None], loss)


def solution(mesh):
    return jax.shard_map(
        on_device,
        mesh=mesh,
        in_specs=(
            P(None, "expert", None),
            P(None, "expert", None),
            P("section", None, "expert", None),
            P("section", None, "expert", None),
            P("section", None, "expert", None),
            P("section", None, "expert", None),
            P("section", None),
            P("section", "expert", None, None),
            P("section", "expert", None, None),
        ),
        out_specs=(
            P("section", None, "expert", None),
            P("section", None, "expert", None),
            P("section", None),
        ),
        check_vma=False,
    )
```

```python
import functools

import jax
import jax.numpy as jnp
from jax import lax
from jax.experimental import pallas as pl
from jax.experimental.pallas import tpu as pltpu
from jax.sharding import PartitionSpec as P

SPLIT = 2
LANES = 128
MIB = 2**20


def run_kernel(body, outs, operands, scratch=(), limit=16, space=pltpu.VMEM):
    return pl.pallas_call(
        body,
        out_shape=outs,
        in_specs=[pl.BlockSpec(memory_space=space)] * len(operands),
        out_specs=jax.tree.map(lambda _: pl.BlockSpec(memory_space=pltpu.VMEM), outs),
        scratch_shapes=list(scratch),
        compiler_params=pltpu.CompilerParams(vmem_limit_bytes=limit * MIB),
    )(*operands)


def in_hbm(value):
    return pltpu.with_memory_space_constraint(value, pltpu.HBM)


def like(rows, columns, dtype=jnp.bfloat16):
    return jax.ShapeDtypeStruct((rows, columns), dtype)


def exclusive(value, mask):
    pairs = [(source, source ^ mask) for source in range(lax.axis_size("expert"))]
    return lax.ppermute(value, "expert", pairs)


def normalize_rows(values):
    factor = lax.rsqrt(jnp.mean(values * values, axis=-1, keepdims=True) + 1e-06)
    return values * factor


def dense_weights(picked, gates, experts):
    rows = picked.shape[0]
    label = lax.broadcasted_iota(jnp.int32, (rows, experts), 1)
    total = jnp.zeros((rows, experts), jnp.float32)
    for k in range(picked.shape[1]):
        total = total + jnp.where(picked[:, k : k + 1] == label, gates[:, k : k + 1], 0.0)
    return total


def pack_kernel(count, *refs):
    sources, out_ref, scratch = refs[:count], refs[count], refs[count + 1 :]
    held, sems = scratch[:count], scratch[count]
    copies = [
        pltpu.make_async_copy(source, target, sems.at[place])
        for place, (source, target) in enumerate(zip(sources, held))
    ]
    for copy in copies:
        copy.start()
    for copy in copies:
        copy.wait()
    states_ref, io_ref, ip_ref, go_ref, gp_ref, keep_ref = held
    model_width = states_ref.shape[1]
    extra = out_ref.shape[1] - model_width
    experts = keep_ref.shape[1]
    states = states_ref[...].astype(jnp.float32)
    out_ref[:, :model_width] = normalize_rows(states).astype(jnp.bfloat16)
    dense_orig = dense_weights(io_ref[...], go_ref[...], experts)
    dense_pruned = dense_weights(ip_ref[...], gp_ref[...], experts)
    dense_pruned = dense_pruned * keep_ref[...].astype(jnp.float32)
    dense = jnp.concatenate([dense_orig, dense_pruned], axis=0)
    high = dense.astype(jnp.bfloat16)
    low = (dense - high.astype(jnp.float32)).astype(jnp.bfloat16)
    source = lax.broadcasted_iota(jnp.int32, (experts, extra), 0)
    lane = lax.broadcasted_iota(jnp.int32, (experts, extra), 1)
    out_ref[:, model_width:] = (
        jnp.dot(
            high,
            (lane == source).astype(jnp.float32).astype(jnp.bfloat16),
            preferred_element_type=jnp.float32,
        )
        + jnp.dot(
            low,
            (lane == source + experts).astype(jnp.float32).astype(jnp.bfloat16),
            preferred_element_type=jnp.float32,
        )
    ).astype(jnp.bfloat16)


def stage_kernel(count, *refs):
    sources, targets, sems = refs[:count], refs[count : 2 * count], refs[2 * count]
    copies = [
        pltpu.make_async_copy(source, target, sems.at[place])
        for place, (source, target) in enumerate(zip(sources, targets))
    ]
    for copy in copies:
        copy.start()
    for copy in copies:
        copy.wait()


def stage(arrays):
    return run_kernel(
        functools.partial(stage_kernel, len(arrays)),
        [pltpu.VMEM(value.shape, value.dtype) for value in arrays],
        arrays,
        [pltpu.SemaphoreType.DMA((len(arrays),))],
        space=pl.ANY,
    )


def after(value, *awaited):
    return lax.optimization_barrier((value, awaited))[0]


def join_kernel(*refs):
    part_refs, out_ref = refs[:-1], refs[-1]
    rows = part_refs[0].shape[0]
    for place, part_ref in enumerate(part_refs):
        out_ref[place * rows : (place + 1) * rows, :] = part_ref[...]


def join_rows(parts):
    rows, columns = parts[0].shape
    return run_kernel(join_kernel, like(len(parts) * rows, columns), parts)


def expert_kernel(experts, row_count, sizes, *refs):
    row_refs, refs = refs[:row_count], refs[row_count:]
    in_refs, out_refs, refs = refs[:SPLIT], refs[SPLIT : 2 * SPLIT], refs[2 * SPLIT :]
    result_refs, (rows, hidden) = refs[: len(sizes)], refs[len(sizes) :]
    half, model_width = out_refs[0].shape
    expert = lax.axis_index("expert") // SPLIT
    weights = []
    filled = 0
    for row_ref in row_refs:
        size = row_ref.shape[0]
        rows[filled : filled + size, :] = row_ref[:, :model_width]
        filled += size
        extra = row_ref[:, model_width:].astype(jnp.float32)
        lane = lax.broadcasted_iota(jnp.int32, extra.shape, 1)
        mine = jnp.logical_or(lane == expert, lane == expert + experts)
        weights.append(jnp.sum(jnp.where(mine, extra, 0.0), axis=1, keepdims=True))
    weight = jnp.concatenate(weights, axis=0)
    for place, in_ref in enumerate(in_refs):
        both = jnp.dot(rows[...], in_ref[...], preferred_element_type=jnp.float32)
        gate, up = both[:, :half], both[:, half:]
        hidden[:, place * half : (place + 1) * half] = (
            gate / (1.0 + jnp.exp(-gate)) * up
        ).astype(jnp.bfloat16)
    step = min(512, model_width)
    for start in range(0, model_width, step):
        value = sum(
            jnp.dot(
                hidden[:, place * half : (place + 1) * half],
                out_ref[:, start : start + step],
                preferred_element_type=jnp.float32,
            )
            for place, out_ref in enumerate(out_refs)
        )
        value = (value * weight).astype(jnp.bfloat16)
        filled = 0
        for size, result_ref in zip(sizes, result_refs):
            result_ref[:, start : start + step] = value[filled : filled + size]
            filled += size


def run_expert(experts, row_arrays, weights, sizes):
    total = sum(array.shape[0] for array in row_arrays)
    half, model_width = weights[-1].shape
    return run_kernel(
        functools.partial(expert_kernel, experts, len(row_arrays), sizes),
        [like(size, model_width) for size in sizes],
        list(row_arrays) + list(weights),
        [
            pltpu.VMEM((total, model_width), jnp.bfloat16),
            pltpu.VMEM((total, SPLIT * half), jnp.bfloat16),
        ],
        limit=24,
    )


def plane_kernel(count, *refs):
    part_refs, out_refs = refs[:count], refs[count:]
    rows = out_refs[0].shape[0]
    for place, out_ref in enumerate(out_refs):
        out_ref[...] = sum(
            ref[place * rows : (place + 1) * rows, :].astype(jnp.float32) for ref in part_refs
        ).astype(out_ref.dtype)


def final_kernel(parts, factor, *refs):
    part_refs, refs = refs[:parts], refs[parts:]
    ids_ref, gates_ref, orig_ref, pruned_ref, terms_ref, *value_refs = refs
    tok_rows = orig_ref.shape[0]
    total = sum(ref[...].astype(jnp.float32) for ref in part_refs)
    for value_ref in value_refs:
        value_ref[...] = total
    value_orig, value_pruned = total[:tok_rows], total[tok_rows:]
    orig_ref[...] = value_orig.astype(jnp.bfloat16)
    pruned_ref[...] = value_pruned.astype(jnp.bfloat16)
    differ = value_orig - value_pruned
    errors = jnp.mean(differ * differ, axis=1, keepdims=True)
    experts = terms_ref.shape[1]
    dense = dense_weights(ids_ref[...], gates_ref[...], experts)
    terms = factor * jnp.sum(dense * errors, axis=0, keepdims=True)
    terms_ref[...] = jnp.broadcast_to(terms, terms_ref.shape)


def add_kernel(parts_ref, out_ref):
    out_ref[...] = jnp.sum(parts_ref[...], axis=0, keepdims=True)


def on_device(
    states_orig,
    states_pruned,
    ids_orig,
    ids_pruned,
    gates_orig,
    gates_pruned,
    keep_mask,
    w_in,
    w_out,
):
    devices = lax.axis_size("expert")
    section_count = lax.axis_size("section")
    section_index = lax.axis_index("section")
    micro_count, tok_rows, model_width = states_orig.shape
    experts = keep_mask.shape[1]
    top_count = ids_orig.shape[-1]
    loss_factor = experts / (top_count * micro_count * tok_rows * devices)
    extra = -(-2 * experts // LANES) * LANES
    rows = 2 * tok_rows
    chips = devices // SPLIT
    inner = min(4, chips)
    outer = chips // inner
    inner_masks = [SPLIT * i for i in range(1, inner)]
    layer_mask = lambda j: SPLIT * inner * j
    nearer = list(range(1, outer // 2 + 1))
    streams = [[j for j in range(outer) if j not in nearer], nearer]
    own_in, own_out = w_in[0, 0], w_out[0, 0]
    other_out, other_in = exclusive(own_out, 1), exclusive(own_in, 1)

    step_count = micro_count + section_count - 1
    carry = jnp.zeros((2, tok_rows, model_width), jnp.bfloat16)
    moe_orig = jnp.zeros((micro_count, tok_rows, model_width), jnp.bfloat16)
    moe_pruned = moe_orig
    terms = jnp.zeros((devices, experts), jnp.float32)
    for tick in range(step_count):
        if section_count == 1:
            position = tick
            item = lambda buffer: buffer[position]
        else:
            position = jnp.clip(tick - section_index, 0, micro_count - 1)
            active = jnp.logical_and(
                tick - section_index >= 0, tick - section_index < micro_count
            )
            item = lambda buffer: lax.dynamic_index_in_dim(buffer, position, 0, keepdims=False)
        fresh = min(tick, micro_count - 1)
        state_orig, state_pruned = states_orig[fresh], states_pruned[fresh]
        if section_count > 1:
            state_orig = jnp.where(section_index == 0, state_orig, carry[0])
            state_pruned = jnp.where(section_index == 0, state_pruned, carry[1])
        picked_orig, weight_orig = item(ids_orig[0]), item(gates_orig[0])
        operands = [
            jnp.concatenate([state_orig, state_pruned], axis=0),
            picked_orig,
            item(ids_pruned[0]),
            weight_orig,
            item(gates_pruned[0]),
            keep_mask,
        ]
        packed = run_kernel(
            functools.partial(pack_kernel, len(operands)),
            like(rows, model_width + extra),
            operands[:1] + [in_hbm(value) for value in operands[1:]],
            [pltpu.VMEM(value.shape, value.dtype) for value in operands]
            + [pltpu.SemaphoreType.DMA((len(operands),))],
            space=pl.ANY,
        )
        column = {0: packed}
        for j in streams[1][::-1] + streams[0][1:]:
            column[j] = exclusive(packed, layer_mask(j))
        if tick == 0:
            own = stage([in_hbm(own_in), in_hbm(own_out)])
            weights = [own[0], other_in, own[1], other_out]
        blocks = []
        for stream, layers in enumerate(streams):
            joined = join_rows([column[j] for j in layers])
            if stream == 1:
                joined = after(joined, own, other_in, other_out)
            block = [joined]
            for mask in inner_masks:
                block.append(exclusive(joined, mask))
            blocks.append(block)
        summed = []
        for stream, layers in enumerate(streams):
            partial = run_expert(
                experts, blocks[stream], weights, [len(layers) * rows] * inner
            )
            returned = [partial[0]] + [
                exclusive(part, mask) for part, mask in zip(partial[1:], inner_masks)
            ]
            outs = [like(rows, model_width)] * len(layers)
            if stream == 0:
                outs[0] = like(rows, model_width, jnp.float32)
            sums = run_kernel(functools.partial(plane_kernel, inner), outs, returned)
            for j, value in list(zip(layers, sums))[::-1]:
                summed.append(exclusive(value, layer_mask(j)) if j else value)
        round_orig, round_pruned, tick_terms, *moe = run_kernel(
            functools.partial(final_kernel, outer, loss_factor),
            [like(tok_rows, model_width)] * 2
            + [like(devices, experts, jnp.float32)]
            + [like(rows, model_width, jnp.float32)] * (section_count > 1),
            summed + [picked_orig, weight_orig],
        )
        if section_count > 1:
            tick_terms = jnp.where(active, tick_terms, 0.0)
            round_orig = jnp.where(active, round_orig, item(moe_orig))
            round_pruned = jnp.where(active, round_pruned, item(moe_pruned))
        terms = tick_terms if tick == 0 else terms + tick_terms
        moe_orig = lax.dynamic_update_index_in_dim(moe_orig, round_orig, position, 0)
        moe_pruned = lax.dynamic_update_index_in_dim(moe_pruned, round_pruned, position, 0)
        if tick + 1 < step_count and section_count > 1:
            state = jnp.stack([state_orig, state_pruned]).astype(jnp.float32)
            following = (state + moe[0].reshape(state.shape)).astype(jnp.bfloat16)
            onward = [(i, i + 1) for i in range(section_count - 1)]
            carry = lax.ppermute(following, "section", onward)
    shared = lax.all_to_all(terms, "expert", split_axis=0, concat_axis=0, tiled=True)
    loss = run_kernel(add_kernel, like(1, experts, jnp.float32), [shared])
    return (moe_orig[None], moe_pruned[None], loss)


def solution(mesh):
    return jax.shard_map(
        on_device,
        mesh=mesh,
        in_specs=(
            P(None, "expert", None),
            P(None, "expert", None),
            P("section", None, "expert", None),
            P("section", None, "expert", None),
            P("section", None, "expert", None),
            P("section", None, "expert", None),
            P("section", None),
            P("section", "expert", None, None),
            P("section", "expert", None, None),
        ),
        out_specs=(
            P("section", None, "expert", None),
            P("section", None, "expert", None),
            P("section", None),
        ),
        check_vma=False,
    )
```
